32 devices in a mesh: dp: 8 (over z, y), tensor: 4 (over x, core).
Axes of the slice: x: 2, y: 2, z: 4, core: 2. Of those that a mesh axis runs over, the one named last changes fastest.
Arguments:
- tokens: bfloat16 [8, 1024, 512], P('dp', None, 'tensor'), may hold values from -6 to 6
- cotangent: bfloat16 [8, 1024, 512], P('dp', None, 'tensor'), may hold values from -6 to 6
- lengths: int32 [8], P('dp'), may hold values from 1 to 1024, as said below
- norm_gains: float32 [2, 512], replicated, may hold values from 0.5 to 1.5
- conv_kernel: float32 [5, 32, 512], P(None, None, 'tensor'), may hold values from -0.75 to 0.75
- mixer_weights: bfloat16 [3, 512, 512], P(None, None, 'tensor'), may hold values from -0.25 to 0.25
- mlp_weights: bfloat16 [2, 512, 2048], P(None, None, 'tensor'), may hold values from -0.25 to 0.25
- gain_moment: float32 [2, 512], replicated, may hold values from -0.0625 to 0.0625
- kernel_moment: float32 [5, 32, 512], P(None, None, 'tensor'), may hold values from -0.0625 to 0.0625
- mixer_moment: float32 [3, 512, 512], P(None, 'dp', 'tensor'), may hold values from -0.0625 to 0.0625
- mlp_moment: float32 [2, 512, 2048], P(None, 'dp', 'tensor'), may hold values from -0.0625 to 0.0625
Outputs:
- block_out: bfloat16 [8, 1024, 512], P('dp', None, 'tensor')
- input_grad: float32 [8, 1024, 512], P('dp', None, 'tensor')
- gain_moment_new: float32 [2, 512], replicated
- gains_new: float32 [2, 512], replicated
- kernel_moment_new: float32 [5, 32, 512], P(None, None, 'tensor')
- kernel_new: float32 [5, 32, 512], P(None, None, 'tensor')
- mixer_moment_new: float32 [3, 512, 512], P(None, 'dp', 'tensor')
- mixer_new: float32 [3, 512, 512], P(None, 'dp', 'tensor')
- mlp_moment_new: float32 [2, 512, 2048], P(None, 'dp', 'tensor')
- mlp_new: float32 [2, 512, 2048], P(None, 'dp', 'tensor')
The draws below stay inside these ranges and needn't reach their ends.
Inputs may be any that keep to these rules, and one draw needn't show every extreme that they name: `lengths`: valid tokens of each sequence; the last sequence is full.
All inputs are finite; a program needn't handle non-finite values.
Results may differ from the reference program's by a relative error of at most 0.011.
Values may be sent and summed in bfloat16 or wider, within the bound.
No kernel may reach another device: no remote copies, remote signals or barrier semaphores. Data moves between devices by JAX's collectives and lax.ppermute only.
A program may use at most 192 MiB of HBM per device.

```python
import jax
import jax.numpy as jnp
from jax import lax

D = 512
FF = 2048
TAPS = 32
LEVELS = 5
BUCKET = 1024
NS_STEPS = 5
SEQ_DEV = 1
SEQS = 8
TOKENS = 8192
N_DP = 8


def draw_lengths(key, part):
    key = jax.random.fold_in(key, 11)
    row_count = SEQ_DEV * N_DP
    row_index = jnp.arange(row_count, dtype=jnp.int32)
    device = row_index // SEQ_DEV
    ceiling = BUCKET // 3 + 2 * BUCKET // 3 * device // max(N_DP - 1, 1)
    floor_len = jnp.maximum(ceiling // 2, 1)
    random_draw = jax.random.randint(key, (row_count,), 0, 1 << 20, dtype=jnp.int32)
    drawn_lengths = floor_len + random_draw % (ceiling - floor_len + 1)
    return jnp.where(row_index == row_count - 1, BUCKET, drawn_lengths).astype(jnp.int32)


def block_scale(stream_key, dims, cuts, low, high):
    gain, own = 1.0, jax.random.fold_in(stream_key, 6)
    for dim, blocks in cuts:
        draws = jnp.exp(jax.random.uniform(jax.random.fold_in(own, dim), (blocks,), jnp.float32, low / len(cuts), high / len(cuts)))
        gain = gain * jnp.repeat(draws, dims[dim] // blocks).reshape([-1 if axis == dim else 1 for axis in range(len(dims))])
    return gain


def noise(rng, extent, width, reach, split=(), kind=jnp.bfloat16):
    loudness = block_scale(rng, extent, split, -0.22, 0.18) if split else 1.0
    array = jax.random.normal(rng, extent, jnp.float32) * width * loudness
    return jnp.minimum(jnp.maximum(array, -reach), reach).astype(kind)


def setup_inputs(seed: int = 0) -> dict:
    seeds = jax.random.split(jax.random.key(seed), 12)
    return {
        "tokens": noise(seeds[0], (SEQS, BUCKET, D), 1.0, 6.0, ((0, 8), (2, 4))),
        "cotangent": noise(seeds[1], (SEQS, BUCKET, D), 1.0, 6.0, ((0, 8), (2, 4))),
        "lengths": draw_lengths(jax.random.fold_in(seeds[11], 71), 0),
        "norm_gains": jnp.clip(1.0 + 0.1 * jax.random.normal(seeds[3], (2, D), jnp.float32), 0.5, 1.5),
        "conv_kernel": noise(seeds[4], (LEVELS, TAPS, D), 0.125, 0.75, ((2, 4),), jnp.float32),
        "mixer_weights": noise(seeds[5], (3, D, D), D ** -0.5, 0.25, ((2, 4),)),
        "mlp_weights": noise(seeds[6], (2, D, FF), D ** -0.5, 0.25, ((2, 4),)),
        "gain_moment": noise(seeds[7], (2, D), (1.0 / TOKENS ** 0.5), 0.0625, (), jnp.float32),
        "kernel_moment": noise(seeds[8], (LEVELS, TAPS, D), (1.0 / TOKENS ** 0.5), 0.0625, ((2, 4),), jnp.float32),
        "mixer_moment": noise(seeds[9], (3, D, D), (1.0 / TOKENS ** 0.5), 0.0625, ((1, 8), (2, 4)), jnp.float32),
        "mlp_moment": noise(seeds[10], (2, D, FF), (1.0 / TOKENS ** 0.5), 0.0625, ((1, 8), (2, 4)), jnp.float32),
    }


EPSILON = 1e-05
NS_COEF_A = 3.4445
NS_COEF_B = -4.775
NS_COEF_C = 2.0315
MOMENT_DECAY = 0.5
MATRIX_RATE = 1.0
GAIN_RATE = 0.1
KERNEL_RATE = 0.125
HIGHEST = lax.Precision.HIGHEST

@jax.custom_vjp
def low(v):
    return lax.optimization_barrier(v.astype(jnp.bfloat16)).astype(jnp.float32)

@jax.custom_vjp
def low_back(v):
    return v

def low_keep(v):
    return (low(v), None)

def low_pass(kept, grad):
    return (grad,)

def back_keep(v):
    return (v, None)

def back_low(kept, grad):
    return (low(grad),)
low.defvjp(low_keep, low_pass)
low_back.defvjp(back_keep, back_low)

def layer_norm(values, gain_row):
    average = lax.optimization_barrier(jnp.mean(values, axis=-1, keepdims=True))
    centred = values - average
    variance = lax.optimization_barrier(jnp.mean(centred * centred, axis=-1, keepdims=True))
    return centred * lax.rsqrt(variance + EPSILON) * gain_row

def full_kernel(conv_kernel):
    pieces = []
    for scale_index in range(LEVELS):
        pieces.append(jnp.repeat(conv_kernel[scale_index], 2 ** scale_index, axis=0) * 0.5 ** scale_index)
    joined = jnp.concatenate(pieces, axis=0)
    return jnp.pad(joined, ((0, BUCKET - joined.shape[0]), (0, 0)))

def convolve(values, kernel):
    length = 2 * BUCKET
    spectrum = jnp.fft.rfft(values, n=length, axis=1) * jnp.fft.rfft(kernel, n=length, axis=0)[None]
    return jnp.fft.irfft(spectrum, n=length, axis=1)[:, :BUCKET]

def forward(inputs, group_mask, norm_gains, conv_kernel, mixing, feeding):
    mask_col = group_mask[:, :, None]
    normed = low(layer_norm(inputs, norm_gains[0]))
    values = low_back(jnp.einsum('nld,dc->nlc', normed, mixing[0], precision=HIGHEST))
    gate_pre = low_back(jnp.einsum('nld,dc->nlc', normed, mixing[1], precision=HIGHEST))
    convolved = convolve(values, full_kernel(conv_kernel))
    branch = low(jax.nn.gelu(gate_pre) * convolved * mask_col)
    mixer_out = low_back(jnp.einsum('nlc,dc->nld', branch, mixing[2], precision=HIGHEST))
    middle = inputs + mixer_out
    normed_two = low(layer_norm(middle, norm_gains[1]))
    hidden = low_back(jnp.einsum('nld,df->nlf', normed_two, feeding[0], precision=HIGHEST))
    active = low(jax.nn.gelu(hidden) * mask_col)
    return middle + jnp.einsum('nlf,df->nld', active, feeding[1], precision=HIGHEST)

def orthogonalize(matrix):
    current = matrix / (jnp.sqrt(jnp.sum(matrix * matrix)) + 1e-07)
    for turn_index in range(NS_STEPS):
        square = jnp.dot(current, current.T, precision=HIGHEST)
        poly_term = NS_COEF_B * square + NS_COEF_C * jnp.dot(square, square, precision=HIGHEST)
        current = NS_COEF_A * current + jnp.dot(poly_term, current, precision=HIGHEST)
    return current

def reference(tokens, cotangent, lengths, norm_gains, conv_kernel, mixer_weights, mlp_weights, gain_moment, kernel_moment, mixer_moment, mlp_moment):
    positions = jnp.arange(BUCKET, dtype=jnp.int32)
    valid_mask = (positions[None, :] < lengths[:, None]).astype(jnp.float32)
    token_groups = tokens.reshape(N_DP, SEQ_DEV, BUCKET, D)
    cot_groups = cotangent.reshape(N_DP, SEQ_DEV, BUCKET, D)
    mask_groups = valid_mask.reshape(N_DP, SEQ_DEV, BUCKET)
    params = (norm_gains, conv_kernel, mixer_weights.astype(jnp.float32), mlp_weights.astype(jnp.float32))

    def group_step(totals, pieces):
        group_tokens, group_cot, group_mask = pieces

        def block_apply(inputs, gains_arg, kernel_arg, mixing, feeding):
            return forward(inputs, group_mask, gains_arg, kernel_arg, mixing, feeding)
        result, pullback = jax.vjp(block_apply, group_tokens.astype(jnp.float32), *params)
        gradients = pullback(group_cot.astype(jnp.float32))
        totals = jax.tree.map(jnp.add, totals, tuple(gradients[1:]))
        return (totals, (result.astype(jnp.bfloat16), gradients[0]))
    starting = tuple((jnp.zeros_like(param) for param in params))
    totals, (block_rows, grad_rows) = lax.scan(group_step, starting, (token_groups, cot_groups, mask_groups))
    block_out = block_rows.reshape(SEQS, BUCKET, D)
    input_grad = grad_rows.reshape(SEQS, BUCKET, D)
    count = jnp.sum(lengths).astype(jnp.float32)
    gain_moment_new = MOMENT_DECAY * gain_moment + totals[0] / count
    gain_scale = jnp.sqrt(lax.optimization_barrier(jnp.mean(gain_moment_new * gain_moment_new, axis=1, keepdims=True))) + 1e-08
    gains_new = norm_gains - GAIN_RATE * gain_moment_new / gain_scale
    kernel_moment_new = MOMENT_DECAY * kernel_moment + totals[1] / count
    kernel_scale = jnp.sqrt(lax.optimization_barrier(jnp.mean(kernel_moment_new * kernel_moment_new, axis=(0, 1), keepdims=True))) + 1e-08
    kernel_new = conv_kernel - KERNEL_RATE * kernel_moment_new / kernel_scale
    mixer_moment_new = MOMENT_DECAY * mixer_moment + totals[2] / count
    mlp_moment_new = MOMENT_DECAY * mlp_moment + totals[3] / count
    mixer_steps = jnp.stack([orthogonalize(mixer_moment_new[index]) for index in range(3)])
    mlp_steps = jnp.stack([orthogonalize(mlp_moment_new[index]) for index in range(2)])
    mixer_new = mixer_weights.astype(jnp.float32) - MATRIX_RATE * mixer_steps
    mlp_new = mlp_weights.astype(jnp.float32) - MATRIX_RATE * jnp.sqrt(FF / D) * mlp_steps
    return (block_out, input_grad, gain_moment_new, gains_new, kernel_moment_new, kernel_new, mixer_moment_new, mixer_new, mlp_moment_new, mlp_new)
```

```python
import functools
import math

import jax
import jax.numpy as jnp
import numpy as np
from jax import lax
from jax.experimental import pallas as pl
from jax.experimental.pallas import tpu as pltpu
from jax.sharding import PartitionSpec as P

NS_STEPS = 5
EPSILON = 1e-05
NS_COEF_A = 3.4445
NS_COEF_B = -4.775
NS_COEF_C = 2.0315
MOMENT_DECAY = 0.5
MATRIX_RATE = 1.0
GAIN_RATE = 0.1
KERNEL_RATE = 0.125
HIGHEST = lax.Precision.HIGHEST
BF16 = jnp.bfloat16
F32 = jnp.float32


def conv_tables(bucket, levels, taps, dp, slot):
    half = bucket // 4
    size = 2 * half
    t = np.arange(half)
    k = np.arange(half)
    phase = 2 * np.pi * ((k[:, None] * t[None, :]) % size) / size
    forward = np.concatenate([np.cos(phase), -np.sin(phase)], 0)
    forward[half] = (-1.0) ** t
    scale = np.full((half,), 2.0 / size)
    scale[0] = 1.0 / size
    inverse = np.concatenate(
        [np.cos(phase).T * scale[None, :], -np.sin(phase).T * scale[None, :]], 1
    )
    inverse[:, half] = ((-1.0) ** t) / size
    spread = np.zeros((bucket, levels * taps))
    at = 0
    for level in range(levels):
        for tap in range(taps):
            width = 2**level
            spread[at : at + width, level * taps + tap] = 0.5**level
            at += width
    kernel_forward = np.concatenate(
        [forward @ spread[m * half : (m + 1) * half] for m in range(4)], 0
    )
    kernel_inverse = np.concatenate(
        [spread[m * half : (m + 1) * half].T @ inverse for m in range(4)], 1
    )
    share = -(-levels * taps // dp)
    kernel_inverse = np.pad(kernel_inverse, ((0, dp * share - levels * taps), (0, 0)))
    kernel_inverse = kernel_inverse.reshape(dp, share, -1)
    kernel_inverse = np.pad(kernel_inverse, ((0, 0), (0, slot - share), (0, 0))).reshape(dp * slot, -1)
    return tuple(np.asarray(a, np.float32) for a in (forward, inverse, kernel_forward, kernel_inverse))


def cross(a, b):
    return a[0] * b[0] - a[1] * b[1], a[0] * b[1] + a[1] * b[2]


def cross_conj(a, b):
    return a[0] * b[0] + a[1] * b[1], a[1] * b[2] - a[0] * b[1]


def with_edge(spec, first):
    real, imag = spec
    return real, jnp.where(first, 0.0, imag), jnp.where(first, imag, real)


def add_pairs(pairs):
    return functools.reduce(lambda p, q: (p[0] + q[0], p[1] + q[1]), pairs)


def spectral_blocks(left, right, conj, store):
    for step in range(4):
        rows = step * 64
        index = lax.broadcasted_iota(jnp.int32, (64, 128), 0)
        first = index + rows == 0
        sign = 1.0 - 2.0 * (index % 2).astype(F32)
        a = [left(r, rows) for r in range(4)]
        b = [with_edge(right(m, rows), first) for m in range(4)]
        if conj:
            sums = [add_pairs([cross_conj(a[r], b[r - q]) for r in range(q, 4)]) for q in range(4)]
        else:
            sums = [add_pairs([cross(a[r], b[q - r]) for r in range(q + 1)]) for q in range(4)]
        for q in range(4):
            other = q + 1 if conj else q - 1
            if 0 <= other < 4:
                real = sums[q][0] + sign * sums[other][0]
                imag = sums[q][1] + sign * sums[other][1]
            else:
                real, imag = sums[q]
            store(q, rows, real, imag)


def lane_pair(ref, half):
    return lambda r, rows: (
        ref[rows : rows + 64, r * 128 : (r + 1) * 128],
        ref[half + rows : half + rows + 64, r * 128 : (r + 1) * 128],
    )


def row_pair(ref, half):
    return lambda r, rows: (
        ref[2 * half * r + rows : 2 * half * r + rows + 64, :],
        ref[2 * half * r + half + rows : 2 * half * r + half + rows + 64, :],
    )


def gelu_both(x):
    c = math.sqrt(2.0 / math.pi)
    t = jnp.tanh(c * (x + 0.044715 * x * x * x))
    value = 0.5 * x * (1.0 + t)
    slope = 0.5 * (1.0 + t) + 0.5 * x * (1.0 - t * t) * (c * (1.0 + 3 * 0.044715 * x * x))
    return value, slope


def swap(value, axis, k):
    size = lax.axis_size(axis)
    return lax.ppermute(value, axis, [(i, i ^ k) for i in range(size)])


def gather_tensor(value):
    far = swap(value, "tensor", 2)
    near = swap(value, "tensor", 1)
    far_near = swap(far, "tensor", 1)
    return [value, near, far, far_near]


def gather_dp(value, me):
    size = lax.axis_size("dp")
    low, whole = 0, value[None]
    while (1 << low) < size:
        bits = min(3, size.bit_length() - 1 - low)
        mine = (me >> low) & ((1 << bits) - 1)
        out = jnp.zeros((1 << bits,) + whole.shape, whole.dtype)
        for k in range(1 << bits):
            piece = whole if k == 0 else swap(whole, "dp", k << low)
            out = lax.dynamic_update_index_in_dim(out, piece, mine ^ k, 0)
        whole = out.reshape((-1,) + value.shape)
        low += bits
    return whole


def dot(a, b, contract):
    return lax.dot_general(a, b, ((contract[0], contract[1]), ((), ())), preferred_element_type=F32)


NN = ((1,), (0,))
NT = ((1,), (1,))
TN = ((0,), (0,))


def split(value):
    high = value.astype(BF16)
    return high, (value - high.astype(F32)).astype(BF16)


def dot3(a, b):
    a_high, a_low = split(a)
    b_high, b_low = split(b)
    mm = functools.partial(jnp.dot, preferred_element_type=F32)
    return mm(a_high, b_high) + (mm(a_high, b_low) + mm(a_low, b_high))


def newton_schulz(matrix, a_ref, q_ref, p_ref, start, out_rows):
    size = a_ref.shape[0]
    row = lax.broadcasted_iota(jnp.int32, (size, size), 0)
    col = lax.broadcasted_iota(jnp.int32, (size, size), 1)
    unit = (row == col).astype(F32)
    gram = dot(matrix, matrix, NT)
    scale = 1.0 / (jnp.sqrt(jnp.sum(gram * unit)) + 1e-07)
    a_ref[...] = gram * (scale * scale)

    def advance(first):
        a = a_ref[...]
        square = dot3(a, a)
        cube = dot3(a, square)
        poly = NS_COEF_A * unit + NS_COEF_B * a + NS_COEF_C * square
        half = NS_COEF_A * a + NS_COEF_B * square + NS_COEF_C * cube
        a_ref[...] = dot3(poly, half)
        q_ref[...] = poly if first else dot3(poly, q_ref[...])

    advance(True)
    pl.loop(0, NS_STEPS - 2)(lambda _: advance(False))
    a = a_ref[...]
    p_ref[...] = NS_COEF_A * unit + NS_COEF_B * a + NS_COEF_C * dot3(a, a)
    high, low = split(dot3(p_ref[pl.ds(start, out_rows), :], q_ref[...]))
    return scale * (dot(high, matrix, NN) + dot(low, matrix, NN))


VMEM = pl.BlockSpec(memory_space=pltpu.VMEM)
SMEM = pl.BlockSpec(memory_space=pltpu.SMEM)


def call(kernel, outs, scratch, args, flops, limit):
    shapes = tuple(jax.ShapeDtypeStruct(shape, dtype) for shape, dtype in outs)
    moved = sum(math.prod(a.shape) * a.dtype.itemsize for a in (*args, *shapes))
    return pl.pallas_call(
        kernel,
        out_shape=shapes,
        in_specs=[SMEM] + [VMEM] * (len(args) - 1),
        out_specs=(VMEM,) * len(shapes),
        scratch_shapes=[pltpu.VMEM(shape, dtype) for shape, dtype in scratch],
        compiler_params=pltpu.CompilerParams(vmem_limit_bytes=limit * 2**20),
        cost_estimate=pl.CostEstimate(flops=flops, bytes_accessed=moved, transcendentals=0),
    )(*args)


def block_at(index, size):
    return pl.ds(pl.multiple_of(index * size, size), size)


def row_mask(info, start, rows):
    return (start + lax.broadcasted_iota(jnp.int32, (rows, 1), 0) < info[1]).astype(F32)


def entry_kernel(info, p0, p1, p2, p3, weights, gains, forward, inverse, spec_k,
                 x, normed, n_own, inv, spec_v, conv, act, slope, branch, wide, spec_y):
    me = info[0]
    part = p0.shape[1]
    half = forward.shape[1]
    for k, piece in enumerate((p0, p1, p2, p3)):
        x[:, block_at(me ^ k, part)] = piece[...]
    gain = gains[0:1, :]
    for c in range(4):
        r = slice(c * half, (c + 1) * half)
        v = x[r, :].astype(F32)
        mean = jnp.mean(v, 1, keepdims=True)
        centred = v - mean
        scale = lax.rsqrt(jnp.mean(centred * centred, 1, keepdims=True) + EPSILON)
        normal = (centred * scale * gain).astype(BF16)
        normed[r, :] = normal
        inv[r, :] = scale
        n_own[r, :] = (p0[r, :].astype(F32) - mean) * scale
        wide[:, c * part : (c + 1) * part] = dot(normal, weights[0], NN)
        act[r, :], slope[r, :] = gelu_both(dot(normal, weights[1], NN))
    spec_v[...] = jnp.dot(forward[...], wide[...], precision=HIGHEST, preferred_element_type=F32)

    def store(q, rows, real, imag):
        spec_y[rows : rows + 64, q * part : (q + 1) * part] = real
        spec_y[half + rows : half + rows + 64, q * part : (q + 1) * part] = imag

    spectral_blocks(lane_pair(spec_v, half), row_pair(spec_k, half), False, store)
    wide[...] = jnp.dot(inverse[...], spec_y[...], precision=HIGHEST, preferred_element_type=F32)
    for c in range(4):
        r = slice(c * half, (c + 1) * half)
        out = wide[:, c * part : (c + 1) * part]
        conv[r, :] = out
        branch[r, :] = (act[r, :] * out * row_mask(info, c * half, half)).astype(BF16)


def cotangent_kernel(info, p0, p1, p2, p3, weights, cot, delta):
    me = info[0]
    part = p0.shape[1]
    for k, piece in enumerate((p0, p1, p2, p3)):
        cot[:, block_at(me ^ k, part)] = piece[...]
    step = cot.shape[0] // 4
    for c in range(4):
        r = slice(c * step, (c + 1) * step)
        delta[r, :] = dot(cot[r, :], weights[1], NN)


def middle_kernel(info, b0, b1, b2, b3, w0, w1, w2, w3, x, gains, weights, delta_active,
                  near, kept, normed, active, delta_hidden, n_mine, inv_mine, middle_own, branch, out_w, middle):
    me = info[0]
    part = b0.shape[1]
    step = x.shape[0] // 4
    for k, piece in enumerate((b0, b1, b2, b3)):
        branch[:, block_at(me ^ k, part)] = piece[...]
    for k, piece in enumerate((w0, w1, w2, w3)):
        out_w[:, block_at(me ^ k, part)] = piece[...]
    gain = gains[1:2, :]
    for k in (1, 3, 0, 2):
        block = me ^ k
        r = block_at(block, step)
        mid = x[r, :].astype(F32) + dot(branch[r, :], out_w[...], NT)
        middle[r, :] = mid
        centred = mid - jnp.mean(mid, 1, keepdims=True)
        scale = lax.rsqrt(jnp.mean(centred * centred, 1, keepdims=True) + EPSILON)
        normal = centred * scale
        if k == 0:
            n_mine[...] = normal
            inv_mine[...] = scale
        normal = (normal * gain).astype(BF16)
        normed[r, :] = normal
        value, slope = gelu_both(dot(normal, weights[0], NN))
        mask = row_mask(info, block * step, step)
        active[r, :] = (value * mask).astype(BF16)
        back = (delta_active[r, :] * mask * slope).astype(BF16)
        delta_hidden[r, :] = back
        share = dot(back, weights[0], NT)
        if k % 2:
            near[(k // 2) * step : (k // 2 + 1) * step, :] = share.astype(BF16)
        else:
            kept[(k // 2) * step : (k // 2 + 1) * step, :] = share
    middle_own[...] = middle[:, block_at(me, part)]


def mlp_kernel(info, normed, active, delta_hidden, cot, weights, slots, near, kept, part_out):
    me = info[0]
    dp, height, width = slots.shape
    rows = normed.shape[1] // dp
    for which, (a, b) in enumerate(((normed, delta_hidden), (cot, active))):
        grad = dot(a[...], b[...], TN)
        for i in range(dp):
            slots[i, which * rows : (which + 1) * rows, :] = grad[i * rows : (i + 1) * rows, :].astype(slots.dtype)
    length = jnp.full((height - 2 * rows, width), 1, jnp.int32) * info[1]
    first = lax.broadcasted_iota(jnp.int32, length.shape, 0) == 0
    length = jnp.where(first, length // 32, length % 32).astype(F32).astype(slots.dtype)
    for i in range(dp):
        slots[i, 2 * rows :, :] = length
    step = active.shape[0] // 4
    part = near.shape[2]
    for c in range(4):
        r = slice(c * step, (c + 1) * step)
        part_out[r, :] = dot(active[r, :], weights[1], NT)
    for k in range(4):
        share = part_out[:, block_at(me ^ k, part)]
        if k % 2:
            near[k // 2] = share.astype(BF16)
        else:
            kept[k // 2] = share


def mlp_moment_kernel(info, arrived, moment, moment_new, slots, count):
    dp, height, _ = arrived.shape
    _, rows, _ = moment.shape
    total = arrived[0].astype(F32)
    for i in range(1, dp):
        total = total + arrived[i].astype(F32)
    tokens = 32.0 * total[2 * rows : 2 * rows + 1, :] + total[2 * rows + 1 : 2 * rows + 2, :]
    count[...] = jnp.broadcast_to(tokens[:, : count.shape[1]], count.shape)
    for which in range(2):
        new = MOMENT_DECAY * moment[which] + total[which * rows : (which + 1) * rows, :] / tokens
        moment_new[which] = new
        for i in range(which, dp, 2):
            slots[i] = new.astype(slots.dtype)


def join_kernel(info, kept, came, mine, far):
    mine[...] = kept[0] + came[0].astype(F32)
    far[...] = (kept[1] + came[1].astype(F32)).astype(BF16)


def norm_back_kernel(info, mine, came, cot, n_mine, inv_mine, gains, delta, grad_gain):
    size = mine.shape[0]
    total = mine[...] + came[...].astype(F32)
    n = n_mine[...]
    q = total * gains[1:2, :]
    back = inv_mine[...] * (q - jnp.mean(q, 1, keepdims=True) - n * jnp.mean(q * n, 1, keepdims=True))
    delta[...] = (cot[block_at(info[0], size), :].astype(F32) + back).astype(BF16)
    grad_gain[...] = jnp.sum(total * n, 0, keepdims=True)


def mixer_back_kernel(info, d0, d1, d2, d3, weights, act, slope, conv, branch, normed, spec_v, spec_k, forward, inverse,
                      kernel_inverse, gains,
                      slots, near, kept, sums, delta_own,
                      delta, wide, spec_d, spec_y, spec_u, back, share):
    me = info[0]
    step, width = d0.shape
    part = weights.shape[2]
    half = forward.shape[1]
    for k, piece in enumerate((d0, d1, d2, d3)):
        block = me ^ k
        r = block_at(block, step)
        delta[r, :] = piece[...]
        down = dot(piece[...], weights[2], NN) * row_mask(info, block * step, step)
        back[r, part:] = (down * conv[r, :] * slope[r, :]).astype(BF16)
        wide[:, block_at(block, part)] = down * act[r, :]
    delta_own[...] = delta[:, block_at(me, part)]
    spec_d[...] = jnp.dot(forward[...], wide[...], precision=HIGHEST, preferred_element_type=F32)

    def store(q, rows, real, imag):
        spec_y[rows : rows + 64, q * part : (q + 1) * part] = real
        spec_y[half + rows : half + rows + 64, q * part : (q + 1) * part] = imag

    def store_rows(q, rows, real, imag):
        spec_u[2 * half * q + rows : 2 * half * q + rows + 64, :] = real
        spec_u[2 * half * q + half + rows : 2 * half * q + half + rows + 64, :] = imag

    spectral_blocks(lane_pair(spec_d, half), row_pair(spec_k, half), True, store)
    wide[...] = jnp.dot(inverse[...], spec_y[...], precision=HIGHEST, preferred_element_type=F32)
    for c in range(4):
        back[c * half : (c + 1) * half, :part] = wide[:, c * part : (c + 1) * part].astype(BF16)
    spectral_blocks(lane_pair(spec_d, half), lane_pair(spec_v, half), True, store_rows)
    grad_kernel = jnp.dot(kernel_inverse[...], spec_u[...], precision=HIGHEST, preferred_element_type=F32)
    grads = dot(normed[...], back[...], TN)
    grad_out = dot(delta[...], branch[...], TN)
    dp = slots.shape[0]
    rows = width // dp
    taps = grad_kernel.shape[0] // dp
    for i in range(dp):
        r = slice(i * rows, (i + 1) * rows)
        slots[i, :rows, :] = grads[r, :part].astype(slots.dtype)
        slots[i, rows : 2 * rows, :] = grads[r, part:].astype(slots.dtype)
        slots[i, 2 * rows : 3 * rows, :] = grad_out[r, :].astype(slots.dtype)
        slots[i, 3 * rows :, :] = grad_kernel[i * taps : (i + 1) * taps, :].astype(slots.dtype)
    ones = jnp.ones((8, width), BF16)
    gain = jnp.broadcast_to(gains[0:1, :], (8, width)).astype(BF16)
    for c in range(4):
        r = slice(c * step, (c + 1) * step)
        out = dot(back[r, :part], weights[0], NT) + dot(back[r, part:], weights[1], NT)
        share[r, :] = out
        first = dot(gain, out.astype(BF16), NT)
        second = dot(ones, (out * normed[r, :].astype(F32)).astype(BF16), NT)
        for h in range(step // part):
            at = c * (step // part) + h
            sums[at : at + 1, :] = first[0:1, h * part : (h + 1) * part]
            sums[8 + at : 9 + at, :] = second[0:1, h * part : (h + 1) * part]
    for k in range(4):
        block = share[:, block_at(me ^ k, part)]
        if k % 2:
            near[k // 2] = block.astype(BF16)
        else:
            kept[k // 2] = block


def moment_kernel(info, arrived, moment, count, sums, moment_new, kernel_total, o0, o1, o2, o3, new):
    me = info[0]
    dp = arrived.shape[0]
    _, rows, _ = moment.shape
    total = arrived[0].astype(F32)
    for i in range(1, dp):
        total = total + arrived[i].astype(F32)
    for which in range(3):
        value = MOMENT_DECAY * moment[which] + total[which * rows : (which + 1) * rows, :] / count[0:1, :]
        moment_new[which] = value
        new[which] = value.astype(new.dtype)
    kernel_total[...] = total[3 * rows :, :]
    for k, out in enumerate((o0, o1, o2, o3)):
        out[:rows, :] = new[jnp.minimum(me ^ k, 2)]
        out[rows:, :] = sums[...].astype(out.dtype)


def first_back_kernel(info, mine, came, delta_own, n_own, inv, gains, g0, g1, g2, g3, kernel_total, gain_two,
                      input_grad, payload, extra):
    me = info[0]
    part = mine.shape[1]
    width = 4 * part
    rows = g0.shape[0] - 16
    gain = gains[0:1, block_at(me, part)]
    total = mine[...] + came[...].astype(F32)
    n = n_own[...]
    sums = 0.0
    for k, piece in enumerate((g0, g1, g2, g3)):
        payload[:rows, block_at(me ^ k, part)] = piece[:rows, :]
        sums = sums + piece[rows:, :].astype(F32)
    sums = sums / width
    for h in range(total.shape[0] // part):
        r = slice(h * part, (h + 1) * part)
        column = lambda at: jnp.broadcast_to(sums[at : at + 1, :], (part, part)).T
        back = total[r, :] * gain - column(h) - n[r, :] * column(8 + h)
        input_grad[r, :] = delta_own[r, :].astype(F32) + inv[r, :] * back
    extra[...] = jnp.zeros_like(extra)
    for g in range(min(3, kernel_total.shape[0] // 8)):
        extra[:, g * part : (g + 1) * part] = kernel_total[8 * g : 8 * g + 8, :]
    extra[0:1, 3 * part :] = jnp.sum(total * n, 0, keepdims=True)
    for q in range(4):
        extra[1 + q : 2 + q, 3 * part :] = gain_two[:, q * part : (q + 1) * part]
    high, low = split(extra[...])
    payload[rows:, :] = jnp.concatenate([high.astype(F32), low.astype(F32)], 0).astype(payload.dtype)


def large_kernel(info, m0, m1, m2, m3, mine, other, matrix, a, q, p):
    me, row = info[0], info[2]
    part = m0.shape[1]
    rows = mine.shape[0]
    last = me == 3

    @pl.when(last)
    def _():
        for k, piece in enumerate((m0, m1, m2, m3)):
            matrix[:, block_at(3 ^ k, part)] = piece[...]
        start = pl.multiple_of((row // 2) * (2 * rows), 2 * rows)
        result = newton_schulz(matrix[...], a, q, p, start, 2 * rows)
        even = row % 2 == 0
        first, second = result[:rows, :], result[rows:, :]
        mine[...] = jnp.where(even, first, second).astype(mine.dtype)
        other[...] = jnp.where(even, second, first).astype(other.dtype)

    @pl.when(jnp.logical_not(last))
    def _():
        mine[...] = jnp.zeros_like(mine)
        other[...] = jnp.zeros_like(other)


def small_kernel(info, *refs):
    *pieces, large_mine, large_came, o0, o1, o2, o3, kernel_all, matrix, a, q, p, result, gains = refs
    me, row = info[0], info[2]
    outs = (o0, o1, o2, o3)
    dp = gains.shape[0]
    rows = o0.shape[0] - 16
    part = kernel_all.shape[1]
    count = len(pieces)
    size = matrix.shape[0]
    for k, piece in enumerate(pieces):
        for h in range(dp // count):
            index = (row ^ k) if count == dp else h
            at = h * (rows + 16)
            matrix[block_at(index, rows), :] = piece[at : at + rows, :]
            both = piece[at + rows : at + rows + 16, :].astype(F32)
            both = both[:8, :] + both[8:, :]
            for g in range(3):
                kernel_all[pl.ds(pl.multiple_of(index * 24 + 8 * g, 8), 8), :] = both[:, g * part : (g + 1) * part]
            gains[index] = both[:, 3 * part :]
    gain = gains[0]
    for i in range(1, dp):
        gain = gain + gains[i]
    high, low = split(gain)
    gain = jnp.concatenate([high.astype(F32), low.astype(F32)], 0).astype(o0.dtype)
    for out in outs:
        out[rows:, :part] = gain
        out[rows:, part:] = jnp.zeros((16, out.shape[1] - part), out.dtype)

    @pl.when(me < 3)
    def _():
        start = pl.multiple_of(row * rows, rows)
        result[...] = newton_schulz(matrix[...], a, q, p, start, rows)
        for k, out in enumerate(outs):
            out[:rows, :part] = result[:, block_at(me ^ k, part)].astype(out.dtype)
            out[:rows, part:] = jnp.zeros((rows, out.shape[1] - part), out.dtype)

    @pl.when(me == 3)
    def _():
        hidden = outs[0].shape[1] // 2
        even = row % 2 == 0
        for k, out in enumerate(outs):
            mine = large_mine[:, block_at(3 ^ k, hidden)]
            came = large_came[:, block_at(3 ^ k, hidden)]
            out[:rows, :hidden] = jnp.where(even, mine, came).astype(out.dtype)
            out[:rows, hidden:] = jnp.where(even, came, mine).astype(out.dtype)


def final_kernel(info, r0, r1, r2, r3, mixer_weights, mlp_weights, norm_gains, gain_moment, count,
                 mixer_new, mlp_new, gain_moment_new, gains_new, gains):
    me, row = info[0], info[2]
    _, rows, part = mixer_new.shape
    hidden = mlp_new.shape[2]
    width = 4 * part
    for k, piece in enumerate((r0, r1, r2, r3)):
        owner = me ^ k
        both = piece[rows:, :part].astype(F32)
        gains[owner] = both[:8, :] + both[8:, :]

        @pl.when(owner < 3)
        def _(piece=piece, owner=owner):
            old = mixer_weights[owner, block_at(row, rows), :].astype(F32)
            mixer_new[owner] = old - MATRIX_RATE * piece[:rows, :part].astype(F32)

        @pl.when(owner == 3)
        def _(piece=piece):
            rate = MATRIX_RATE * math.sqrt(4 * hidden / width)
            for which in range(2):
                old = mlp_weights[which, block_at(row, rows), :].astype(F32)
                step = piece[:rows, which * hidden : (which + 1) * hidden].astype(F32)
                mlp_new[which] = old - rate * step

    two = gains[0] + gains[1] + gains[2] + gains[3]
    for t in range(4):
        lanes = slice(t * part, (t + 1) * part)
        totals = (gains[t][0:1, :], two[1 + t : 2 + t, :])
        for which in range(2):
            gain_moment_new[which : which + 1, lanes] = (
                MOMENT_DECAY * gain_moment[which : which + 1, lanes] + totals[which] / count[0:1, :]
            )
    new = gain_moment_new[...]
    scale = jnp.sqrt(jnp.mean(new * new, 1, keepdims=True)) + 1e-08
    gains_new[...] = norm_gains[...] - GAIN_RATE * new / scale


def per_device(
    tokens,
    cotangent,
    lengths,
    norm_gains,
    conv_kernel,
    mixer_weights,
    mlp_weights,
    gain_moment,
    kernel_moment,
    mixer_moment,
    mlp_moment,
):
    _, bucket, part = tokens.shape
    levels, taps, _ = conv_kernel.shape
    hidden = mlp_weights.shape[2]
    me = lax.axis_index("tensor")
    row = lax.axis_index("dp")
    dp = lax.axis_size("dp")
    width = 4 * part
    rows = width // dp
    half = bucket // 4
    piece_type = BF16 if rows % 16 == 0 else F32
    share = -(-levels * taps // dp)
    slot = -(-share // 8) * 8
    slot += (3 * rows + slot) % 16
    forward, inverse, kernel_forward, kernel_inverse = conv_tables(bucket, levels, taps, dp, slot)
    info = jnp.stack([me, lengths[0], row]).astype(jnp.int32)
    mflop = 10**6

    x_pieces = gather_tensor(tokens[0])
    spec_k = jnp.dot(kernel_forward, conv_kernel.reshape(levels * taps, part), precision=HIGHEST)
    late = gather_tensor(jnp.concatenate([cotangent[0], mixer_weights[2]], 0))
    cot_pieces = [v[:bucket] for v in late]
    out_pieces = [v[bucket:] for v in late]

    act_like = ((bucket, part), F32)
    wide_like = ((half, width), F32)
    spec_like = ((2 * half, width), F32)
    x, normed, n_own, inv_one, spec_v, conv, gate_act, gate_slope, branch = call(
        entry_kernel,
        [((bucket, width), BF16), ((bucket, width), BF16), act_like, ((bucket, 1), F32), spec_like, act_like, act_like, act_like,
         ((bucket, part), BF16)],
        [wide_like, spec_like],
        (info, *x_pieces, mixer_weights, norm_gains, forward, inverse, spec_k),
        2000 * mflop, 32,
    )
    branch_pieces = gather_tensor(branch)
    cot, delta_active = call(
        cotangent_kernel,
        [((bucket, width), BF16), ((bucket, hidden), F32)],
        [],
        (info, *cot_pieces, mlp_weights),
        540 * mflop, 24,
    )
    near, kept, normed_two, active, delta_hidden, n_mine, inv_mine, middle_own = call(
        middle_kernel,
        [((width, width), BF16), ((width, width), F32), ((bucket, width), BF16), ((bucket, hidden), BF16),
         ((bucket, hidden), BF16), ((half, width), F32), ((half, 1), F32), act_like],
        [((bucket, width), BF16), ((width, width), BF16), ((bucket, width), F32)],
        (info, *branch_pieces, *out_pieces, x, norm_gains, mlp_weights, delta_active),
        1800 * mflop, 40,
    )
    split_blocks = lambda v: v.reshape(2, -1, v.shape[-1])
    came = swap(split_blocks(near), "tensor", 1)
    mlp_slots, out_near, out_kept = call(
        mlp_kernel,
        [((dp, 2 * rows + 16, hidden), piece_type), ((2, bucket, part), BF16), ((2, bucket, part), F32)],
        [((bucket, width), F32)],
        (info, normed_two, active, delta_hidden, cot, mlp_weights),
        1600 * mflop, 40,
    )
    mine, far = call(
        join_kernel, [((half, width), F32), ((half, width), BF16)], [], (info, split_blocks(kept), came), mflop, 16
    )
    came = swap(far, "tensor", 2)
    delta_mid, grad_gain_two = call(
        norm_back_kernel,
        [((half, width), BF16), ((1, width), F32)],
        [],
        (info, mine, came, cot, n_mine, inv_mine, norm_gains),
        mflop, 16,
    )
    delta_pieces = gather_tensor(delta_mid)

    came = swap(out_near, "tensor", 1)
    out_mine, far = call(
        join_kernel, [act_like, ((bucket, part), BF16)], [], (info, out_kept, came), mflop, 16
    )
    came = swap(far, "tensor", 2)
    block_out = (middle_own + (out_mine + came.astype(F32))).astype(BF16)
    mlp_arrived = lax.all_to_all(mlp_slots.astype(BF16), "dp", 0, 0, tiled=True)
    mlp_moment_new, mlp_slots, count = call(
        mlp_moment_kernel,
        [((2, rows, hidden), F32), ((dp, rows, hidden), piece_type), ((8, part), F32)],
        [],
        (info, mlp_arrived, mlp_moment),
        mflop, 16,
    )
    mlp_columns = lax.all_to_all(mlp_slots.astype(BF16), "dp", 0, 0, tiled=True).reshape(width, hidden)
    mlp_pieces = [mlp_columns] + [lax.ppermute(mlp_columns, "tensor", [(3 ^ k, 3)]) for k in (1, 2, 3)]

    slots, one_near, one_kept, sums, delta_own = call(
        mixer_back_kernel,
        [((dp, 3 * rows + slot, part), piece_type), ((2, bucket, part), BF16), ((2, bucket, part), F32), ((16, part), F32),
         ((bucket, part), BF16)],
        [((bucket, width), BF16), wide_like, spec_like, spec_like, ((8 * half, part), F32), ((bucket, 2 * part), BF16),
         ((bucket, width), F32)],
        (info, *delta_pieces, mixer_weights, gate_act, gate_slope, conv, branch, normed, spec_v, spec_k, forward, inverse,
         kernel_inverse, norm_gains),
        4000 * mflop, 48,
    )
    arrived = lax.all_to_all(slots.astype(BF16), "dp", 0, 0, tiled=True)
    came = swap(one_near, "tensor", 1)
    one_mine, far = call(
        join_kernel, [act_like, ((bucket, part), BF16)], [], (info, one_kept, came), mflop, 16
    )
    came = swap(far, "tensor", 2)
    mixer_moment_new, kernel_total, *sends = call(
        moment_kernel,
        [((3, rows, part), F32), ((slot, part), F32)] + [((rows + 16, part), piece_type)] * 4,
        [((3, rows, part), piece_type)],
        (info, arrived, mixer_moment, count, sums),
        mflop, 16,
    )
    got = [sends[0]] + [swap(sends[k].astype(BF16), "tensor", k) for k in (1, 2, 3)]
    input_grad, payload = call(
        first_back_kernel,
        [act_like, ((rows + 16, width), piece_type)],
        [((8, width), F32)],
        (info, one_mine, came, delta_own, n_own, inv_one, norm_gains, *(g.astype(piece_type) for g in got), kernel_total,
         grad_gain_two),
        mflop, 24,
    )

    square = ((width, width), F32)
    large_mine, large_other = call(
        large_kernel,
        [((rows, 4 * hidden), piece_type)] * 2,
        [((width, 4 * hidden), BF16), square, square, square],
        (info, *mlp_pieces),
        15000 * mflop, 40,
    )
    large_came = swap(large_other.astype(BF16), "dp", 1).astype(piece_type)
    payload = payload.astype(BF16)
    if dp == 8:
        pieces = [payload] + [swap(payload, "dp", k) for k in range(1, dp)]
    else:
        pieces = [gather_dp(payload, row).reshape(dp * (rows + 16), width)]
    *sends, kernel_all = call(
        small_kernel,
        [((rows + 16, 2 * hidden), piece_type)] * 4 + [((dp * 24, part), F32)],
        [((width, width), piece_type), square, square, square, ((rows, width), F32), ((dp, 8, part), F32)],
        (info, *(v.astype(piece_type) for v in pieces), large_mine, large_came),
        15000 * mflop, 40,
    )
    got = [sends[0]] + [swap(sends[k].astype(BF16), "tensor", k).astype(piece_type) for k in (1, 2, 3)]
    mixer_new, mlp_new, gain_moment_new, gains_new = call(
        final_kernel,
        [((3, rows, part), F32), ((2, rows, hidden), F32), ((2, width), F32), ((2, width), F32)],
        [((4, 8, part), F32)],
        (info, *got, mixer_weights, mlp_weights, norm_gains, gain_moment, count),
        mflop, 16,
    )
    grad_kernel = kernel_all.reshape(dp, 24, part)[:, :share].reshape(-1, part)[: levels * taps]
    kernel_moment_new = MOMENT_DECAY * kernel_moment + grad_kernel.reshape(levels, taps, part) / count[0]
    kernel_scale = (
        jnp.sqrt(jnp.mean(kernel_moment_new * kernel_moment_new, axis=(0, 1), keepdims=True)) + 1e-08
    )
    kernel_new = conv_kernel - KERNEL_RATE * kernel_moment_new / kernel_scale
    return (
        block_out[None],
        input_grad[None],
        gain_moment_new,
        gains_new,
        kernel_moment_new,
        kernel_new,
        mixer_moment_new,
        mixer_new,
        mlp_moment_new,
        mlp_new,
    )


def solution(mesh):
    tokens = P("dp", None, "tensor")
    columns = P(None, None, "tensor")
    blocks = P(None, "dp", "tensor")
    return jax.shard_map(
        per_device,
        mesh=mesh,
        in_specs=(tokens, tokens, P("dp"), P(), columns, columns, columns, P(), columns, blocks, blocks),
        out_specs=(tokens, tokens, P(), P(), columns, columns, blocks, blocks, blocks, blocks),
        check_vma=False,
    )
```

```python
import functools
import math

import jax
import jax.numpy as jnp
import ml_dtypes
import numpy as np
from jax import lax
from jax.experimental import pallas as pl
from jax.experimental.pallas import tpu as pltpu
from jax.sharding import PartitionSpec as P

NS_STEPS = 5
EPSILON = 1e-05
NS_COEF_A = 3.4445
NS_COEF_B = -4.775
NS_COEF_C = 2.0315
MOMENT_DECAY = 0.5
MATRIX_RATE = 1.0
GAIN_RATE = 0.1
KERNEL_RATE = 0.125
SCALE = 10**10
BF16 = jnp.bfloat16
F32 = jnp.float32


def conv_tables(bucket, levels, taps, dp, slot):
    half = bucket // 4
    size = 2 * half
    t = np.arange(half)
    k = np.arange(half)
    phase = 2 * np.pi * ((k[:, None] * t[None, :]) % size) / size
    forward = np.concatenate([np.cos(phase), -np.sin(phase)], 0)
    forward[half] = (-1.0) ** t
    scale = np.full((half,), 2.0 / size)
    scale[0] = 1.0 / size
    inverse = np.concatenate(
        [np.cos(phase).T * scale[None, :], -np.sin(phase).T * scale[None, :]], 1
    )
    inverse[:, half] = ((-1.0) ** t) / size
    spread = np.zeros((bucket, levels * taps))
    at = 0
    for level in range(levels):
        for tap in range(taps):
            width = 2**level
            spread[at : at + width, level * taps + tap] = 0.5**level
            at += width
    kernel_forward = np.concatenate(
        [forward @ spread[m * half : (m + 1) * half] for m in range(4)], 0
    )
    kernel_inverse = np.concatenate(
        [spread[m * half : (m + 1) * half].T @ inverse for m in range(4)], 1
    )
    share = -(-levels * taps // dp)
    kernel_inverse = np.pad(kernel_inverse, ((0, dp * share - levels * taps), (0, 0)))
    kernel_inverse = kernel_inverse.reshape(dp, share, -1)
    kernel_inverse = np.pad(kernel_inverse, ((0, 0), (0, slot - share), (0, 0))).reshape(dp * slot, -1)
    tables = []
    for table in (forward, inverse, kernel_forward, kernel_inverse):
        high = table.astype(ml_dtypes.bfloat16)
        low = (table - high.astype(np.float64)).astype(ml_dtypes.bfloat16)
        tables.append(np.stack([high, low]))
    return tables


def cross(a, b):
    return a[0] * b[0] - a[1] * b[1], a[0] * b[1] + a[1] * b[2]


def cross_conj(a, b):
    return a[0] * b[0] + a[1] * b[1], a[1] * b[2] - a[0] * b[1]


def with_edge(spec, first):
    real, imag = spec
    return real, jnp.where(first, 0.0, imag), jnp.where(first, imag, real)


def add_pairs(pairs):
    return functools.reduce(lambda p, q: (p[0] + q[0], p[1] + q[1]), pairs)


def spectral_blocks(left, right, conj, store):
    for step in range(4):
        rows = step * 64
        index = lax.broadcasted_iota(jnp.int32, (64, 128), 0)
        first = index + rows == 0
        sign = 1.0 - 2.0 * (index % 2).astype(F32)
        a = [left(r, rows) for r in range(4)]
        b = [with_edge(right(m, rows), first) for m in range(4)]
        if conj:
            sums = [add_pairs([cross_conj(a[r], b[r - q]) for r in range(q, 4)]) for q in range(4)]
        else:
            sums = [add_pairs([cross(a[r], b[q - r]) for r in range(q + 1)]) for q in range(4)]
        for q in range(4):
            other = q + 1 if conj else q - 1
            if 0 <= other < 4:
                real = sums[q][0] + sign * sums[other][0]
                imag = sums[q][1] + sign * sums[other][1]
            else:
                real, imag = sums[q]
            store(q, rows, real, imag)


def lane_pair(ref, half):
    return lambda r, rows: (
        ref[rows : rows + 64, r * 128 : (r + 1) * 128],
        ref[half + rows : half + rows + 64, r * 128 : (r + 1) * 128],
    )


def row_pair(ref, half):
    return lambda r, rows: (
        ref[2 * half * r + rows : 2 * half * r + rows + 64, :],
        ref[2 * half * r + half + rows : 2 * half * r + half + rows + 64, :],
    )


def gelu_both(x):
    c = math.sqrt(2.0 / math.pi)
    t = jnp.tanh(c * (x + 0.044715 * x * x * x))
    value = 0.5 * x * (1.0 + t)
    slope = 0.5 * (1.0 + t) + 0.5 * x * (1.0 - t * t) * (c * (1.0 + 3 * 0.044715 * x * x))
    return value, slope


def after(value, *others):
    return lax.optimization_barrier((value, *others))[0]


def swap(value, axis, k):
    size = lax.axis_size(axis)
    return lax.ppermute(value, axis, [(i, i ^ k) for i in range(size)])


def gather_tensor(value, *meanwhile):
    far = swap(value, "tensor", 2)
    near = swap(value, "tensor", 1)
    if meanwhile:
        far = after(far, *meanwhile)
    far_near = swap(far, "tensor", 1)
    return [value, near, far, far_near]


def gather_dp(value, me, low=0):
    size = lax.axis_size("dp")
    whole = value[None]
    while (1 << low) < size:
        bits = min(3, size.bit_length() - 1 - low)
        mine = (me >> low) & ((1 << bits) - 1)
        out = jnp.zeros((1 << bits,) + whole.shape, whole.dtype)
        for k in range(1 << bits):
            piece = whole if k == 0 else swap(whole, "dp", k << low)
            out = lax.dynamic_update_index_in_dim(out, piece, mine ^ k, 0)
        whole = out.reshape((-1,) + value.shape)
        low += bits
    return whole


def dot(a, b, contract):
    return lax.dot_general(a, b, ((contract[0], contract[1]), ((), ())), preferred_element_type=F32)


NN = ((1,), (0,))
NT = ((1,), (1,))
TN = ((0,), (0,))


def split(value):
    high = value.astype(BF16)
    return high, (value - high.astype(F32)).astype(BF16)


def dot3(a, b):
    a_high, a_low = split(a)
    b_high, b_low = split(b)
    mm = functools.partial(jnp.dot, preferred_element_type=F32)
    return mm(a_high, b_high) + (mm(a_high, b_low) + mm(a_low, b_high))


def table_dot(table, value):
    high, low = split(value)
    return dot(table[0], high, NN) + (dot(table[1], high, NN) + dot(table[0], low, NN))


def newton_schulz(matrix, a_ref, q_ref, p_ref, start, out_rows):
    size = a_ref.shape[0]
    row = lax.broadcasted_iota(jnp.int32, (size, size), 0)
    col = lax.broadcasted_iota(jnp.int32, (size, size), 1)
    unit = (row == col).astype(F32)
    gram = dot(matrix, matrix, NT)
    scale = 1.0 / (jnp.sqrt(jnp.sum(gram * unit)) + 1e-07)
    a_ref[...] = gram * (scale * scale)

    def advance(first):
        a = a_ref[...]
        square = dot3(a, a)
        cube = dot3(a, square)
        poly = NS_COEF_A * unit + NS_COEF_B * a + NS_COEF_C * square
        half = NS_COEF_A * a + NS_COEF_B * square + NS_COEF_C * cube
        a_ref[...] = dot3(poly, half)
        q_ref[...] = poly if first else dot3(poly, q_ref[...])

    advance(True)
    pl.loop(0, NS_STEPS - 2)(lambda _: advance(False))
    a = a_ref[...]
    p_ref[...] = NS_COEF_A * unit + NS_COEF_B * a + NS_COEF_C * dot3(a, a)
    high, low = split(dot3(p_ref[pl.ds(start, out_rows), :], q_ref[...]))
    return scale * (dot(high, matrix, NN) + dot(low, matrix, NN))


VMEM = pl.BlockSpec(memory_space=pltpu.VMEM)
SMEM = pl.BlockSpec(memory_space=pltpu.SMEM)


HBM = pl.BlockSpec(memory_space=pltpu.HBM)


class Late:
    def __init__(self, array):
        self.shape, self.dtype = array.shape, array.dtype
        self.array = pltpu.with_memory_space_constraint(array, pltpu.HBM)


class Store:
    def __init__(self, shape, dtype):
        self.shape, self.dtype = shape, dtype


class Waiting:
    def __init__(self, copy, ref):
        self.copy, self.ref, self.started = copy, ref, False

    def ready(self):
        self.copy.wait()
        return self.ref

    def send(self):
        self.copy.start()
        self.started = True


def call(kernel, outs, scratch, args, time, limit):
    outs = [o if isinstance(o, Store) else jax.ShapeDtypeStruct(*o) for o in outs]
    late = [a for a in (*args, *outs) if isinstance(a, (Late, Store))]
    n_in, n_out = len(args), len(outs)

    def body(*refs):
        given, rest = refs[: n_in + n_out], refs[n_in + n_out :]
        buffers, rest = rest[: len(late)], rest[len(late) :]
        semaphores = rest[-1] if late else None
        passed, stores, at = [], [], 0
        for what, ref in zip((*args, *outs), given):
            if isinstance(what, Late):
                copy = pltpu.make_async_copy(ref, buffers[at], semaphores.at[at])
                copy.start()
            elif isinstance(what, Store):
                copy = pltpu.make_async_copy(buffers[at], ref, semaphores.at[at])
            else:
                passed.append(ref)
                continue
            passed.append(Waiting(copy, buffers[at]))
            if isinstance(what, Store):
                stores.append(passed[-1])
            at += 1
        kernel(*passed, *(rest[:-1] if late else rest))
        for store in stores:
            if not store.started:
                store.send()
        for store in stores:
            store.copy.wait()

    moved = sum(math.prod(a.shape) * jnp.dtype(a.dtype).itemsize for a in (*args, *outs))
    return pl.pallas_call(
        body,
        out_shape=tuple(pltpu.HBM(o.shape, o.dtype) if isinstance(o, Store) else o for o in outs),
        in_specs=[SMEM] + [HBM if isinstance(a, Late) else VMEM for a in args[1:]],
        out_specs=tuple(HBM if isinstance(o, Store) else VMEM for o in outs),
        scratch_shapes=[pltpu.VMEM(a.shape, a.dtype) for a in late]
        + [pltpu.VMEM(shape, dtype) for shape, dtype in scratch]
        + ([pltpu.SemaphoreType.DMA((len(late),))] if late else []),
        compiler_params=pltpu.CompilerParams(vmem_limit_bytes=limit * 2**20),
        cost_estimate=pl.CostEstimate(flops=max(time * SCALE, 10**6), bytes_accessed=moved, transcendentals=0),
    )(*(a.array if isinstance(a, Late) else a for a in args))


def fetch(token, *arrays):
    arrays = [a if isinstance(a, tuple) else (a,) for a in arrays]
    shapes = [
        jax.ShapeDtypeStruct((sum(p.shape[0] for p in a), *a[0].shape[1:]), a[0].dtype) for a in arrays
    ]
    flat = [pltpu.with_memory_space_constraint(p, pltpu.HBM) for a in arrays for p in a]

    def body(token_ref, *refs):
        outs, semaphores, copies, at = refs[len(flat) : -1], refs[-1], [], 0
        for a, out in zip(arrays, outs):
            row = 0
            for p in a:
                target = out if len(a) == 1 else out.at[row : row + p.shape[0]]
                copies.append(pltpu.make_async_copy(refs[at], target, semaphores.at[at]))
                copies[-1].start()
                row, at = row + p.shape[0], at + 1
        for copy in copies:
            copy.wait()

    return pl.pallas_call(
        body,
        out_shape=tuple(shapes),
        in_specs=[SMEM] + [HBM] * len(flat),
        out_specs=(VMEM,) * len(shapes),
        scratch_shapes=[pltpu.SemaphoreType.DMA((len(flat),))],
        compiler_params=pltpu.CompilerParams(vmem_limit_bytes=2 * 2**20),
        cost_estimate=pl.CostEstimate(flops=10**10, bytes_accessed=2 * sum(a.size * a.dtype.itemsize for a in flat), transcendentals=0),
    )(token, *flat)


def block_at(index, size):
    return pl.ds(pl.multiple_of(index * size, size), size)


def row_mask(info, start, rows):
    return (start + lax.broadcasted_iota(jnp.int32, (rows, 1), 0) < info[1]).astype(F32)


def spectrum_kernel(info, table, taps, spec_k):
    taps = taps.ready()[...]
    spec_k[...] = table_dot(table.ready(), taps)


def entry_kernel(info, p0, p1, p2, p3, weights, gains, forward, inverse, spec_k,
                 x, normed, n_own, inv, spec_v, conv, act, slope, branch, gains_kept, wide, spec_y):
    me = info[0]
    part = p1.shape[1]
    for k, piece in enumerate((p0, p1, p2, p3)):
        x[:, block_at(me ^ k, part)] = piece[...]
    gains_kept[...] = gains[...]
    gain = gains[0:1, :]
    half = x.shape[0] // 4
    for c in range(4):
        r = slice(c * half, (c + 1) * half)
        v = x[r, :].astype(F32)
        mean = jnp.mean(v, 1, keepdims=True)
        centred = v - mean
        scale = lax.rsqrt(jnp.mean(centred * centred, 1, keepdims=True) + EPSILON)
        normed[r, :] = (centred * scale * gain).astype(BF16)
        inv.ref[r, :] = scale
        n_own.ref[r, :] = (p0[r, :].astype(F32) - mean) * scale
    n_own.send()
    inv.send()
    for c in range(4):
        r = slice(c * half, (c + 1) * half)
        normal = normed[r, :]
        wide[:, c * part : (c + 1) * part] = dot(normal, weights[0], NN)
        act[r, :], slope[r, :] = gelu_both(dot(normal, weights[1], NN))
    spec_v[...] = table_dot(forward, wide[...])

    def store(q, rows, real, imag):
        spec_y[rows : rows + 64, q * part : (q + 1) * part] = real
        spec_y[half + rows : half + rows + 64, q * part : (q + 1) * part] = imag

    spectral_blocks(lane_pair(spec_v, half), row_pair(spec_k, half), False, store)
    wide[...] = table_dot(inverse, spec_y[...])
    for c in range(4):
        r = slice(c * half, (c + 1) * half)
        out = wide[:, c * part : (c + 1) * part]
        conv[r, :] = out
        out = (act[r, :] * out * row_mask(info, c * half, half)).astype(BF16)
        branch[r, :] = out


def cotangent_kernel(info, p0, p1, p2, p3, weights, cot, out_w, delta, weights_kept):
    part = p0.shape[1]
    for k, piece in enumerate((p0, p1, p2, p3)):
        cot[:, block_at(info[0] ^ k, part)] = piece[: cot.shape[0], :]
        out_w[:, block_at(info[0] ^ k, part)] = piece[cot.shape[0] :, :]
    step = cot.shape[0] // 4
    weights = weights.ready()
    weights_kept[...] = weights[...]
    for c in range(4):
        r = slice(c * step, (c + 1) * step)
        delta[r, :] = dot(cot[r, :], weights[1], NN)


def middle_kernel(info, b0, b1, b2, b3, out_w, x, gains, weights, delta_active,
                  near, kept, normed, active, delta_hidden, n_mine, inv_mine, middle_own, branch, middle):
    me = info[0]
    part = b0.shape[1]
    step = x.shape[0] // 4
    for k, piece in enumerate((b0, b1, b2, b3)):
        branch[:, block_at(me ^ k, part)] = piece[...]
    gain = gains[1:2, :]
    for k in (1, 3, 0, 2):
        block = me ^ k
        r = block_at(block, step)
        mid = x[r, :].astype(F32) + dot(branch[r, :], out_w[...], NT)
        middle[r, :] = mid
        centred = mid - jnp.mean(mid, 1, keepdims=True)
        scale = lax.rsqrt(jnp.mean(centred * centred, 1, keepdims=True) + EPSILON)
        normal = centred * scale
        if k == 0:
            n_mine[...] = normal
            inv_mine[...] = scale
        normal = (normal * gain).astype(BF16)
        normed[r, :] = normal
        value, slope = gelu_both(dot(normal, weights[0], NN))
        mask = row_mask(info, block * step, step)
        active[r, :] = (value * mask).astype(BF16)
        back = (delta_active[r, :] * mask * slope).astype(BF16)
        delta_hidden[r, :] = back
        share = dot(back, weights[0], NT)
        if k % 2:
            near[(k // 2) * step : (k // 2 + 1) * step, :] = share.astype(BF16)
        else:
            kept[(k // 2) * step : (k // 2 + 1) * step, :] = share
    middle_own.ref[...] = middle[:, block_at(me, part)]


def mlp_kernel(info, normed, active, delta_hidden, cot, weights, moment, keep, send, moment_send, near, kept, part_out):
    me = info[0]
    size = normed.shape[1]
    side = info[2] % 2
    for which, (a, b) in enumerate(((normed, delta_hidden), (cot, active))):
        grad = dot(a[...], b[...], TN)

        @pl.when(side == which)
        def _(grad=grad):
            keep[:size, :] = grad

        @pl.when(side != which)
        def _(grad=grad):
            send[:size, :] = grad.astype(BF16)

    length = jnp.full((16, grad.shape[1]), 1, jnp.int32) * info[1]
    first = lax.broadcasted_iota(jnp.int32, length.shape, 0) == 0
    length = jnp.where(first, length // 32, length % 32).astype(F32)
    keep[size:, :] = length
    send[size:, :] = length.astype(BF16)
    moment_send[...] = moment.ready()[1 - side]
    step = active.shape[0] // 4
    part = near.ref.shape[2]
    for c in range(4):
        r = slice(c * step, (c + 1) * step)
        part_out[r, :] = dot(active[r, :], weights[1], NT)
    for k in range(4):
        share = part_out[:, block_at(me ^ k, part)]
        if k % 2:
            near.ref[k // 2] = share.astype(BF16)
        else:
            kept.ref[k // 2] = share


def mlp_rows_kernel(info, keep, came, *outs):
    size = came.shape[0] - 16
    pairs = outs[0].shape[0] if len(outs) == 1 else len(outs)
    rows = size // pairs
    length = keep[size:, :] + came[size:, :].astype(F32)
    for k in range(pairs):
        if len(outs) == 1:
            r, out = pl.ds(k * rows, rows), outs[0].at[k]
        else:
            r, out = block_at((info[2] // 2) ^ k, rows), outs[k]
        out[:rows, :] = (keep[r, :] + came[r, :].astype(F32)).astype(out.dtype)
        out[rows:, :] = length.astype(out.dtype)


def mlp_moment_kernel(info, moment, other_moment, *refs):
    *pieces, matrix, mine, other, count = refs
    rows = moment.shape[1]
    side = info[2] % 2
    if len(pieces) == 1:
        pieces = [pieces[0].at[k] for k in range(pieces[0].shape[0])]
    total = pieces[0][...].astype(F32)
    for piece in pieces[1:]:
        total = total + piece[...].astype(F32)
    tokens = 32.0 * total[2 * rows : 2 * rows + 1, :] + total[2 * rows + 1 : 2 * rows + 2, :]
    count[...] = jnp.broadcast_to(tokens[:, : count.shape[1]], count.shape)
    old = moment[side]
    for which in range(2):
        new = total[which * rows : (which + 1) * rows, :] / tokens

        @pl.when(side == which)
        def _(new=new, which=which):
            now = MOMENT_DECAY * old + new
            mine.ref[...] = now
            matrix[which * rows : (which + 1) * rows, :] = now.astype(matrix.dtype)

        @pl.when(side != which)
        def _(new=new, which=which):
            now = MOMENT_DECAY * other_moment[...] + new
            other.ref[...] = now
            matrix[which * rows : (which + 1) * rows, :] = now.astype(matrix.dtype)


def columns_kernel(info, *refs):
    *pieces, out = refs
    rows = pieces[0].shape[0]
    for k, piece in enumerate(pieces):
        out[block_at((info[2] // 2) ^ k, rows), :] = piece[...]


def join_kernel(info, kept, came, mine, far):
    mine[...] = kept[0] + came[0].astype(F32)
    far[...] = (kept[1] + came[1].astype(F32)).astype(BF16)


def join_late_kernel(info, kept, came, mine, far):
    join_kernel(info, kept.ready(), came, mine, far)


def norm_back_kernel(info, mine, came, cot, n_mine, inv_mine, gains, delta, grad_gain):
    size = mine.shape[0]
    total = mine[...] + came[...].astype(F32)
    n = n_mine[...]
    q = total * gains[1:2, :]
    back = inv_mine[...] * (q - jnp.mean(q, 1, keepdims=True) - n * jnp.mean(q * n, 1, keepdims=True))
    delta[...] = (cot[block_at(info[0], size), :].astype(F32) + back).astype(BF16)
    grad_gain[...] = jnp.sum(total * n, 0, keepdims=True)


def mixer_back_kernel(info, d0, d1, d2, d3, weights, act, slope, conv, branch, normed, spec_v, spec_k, forward, inverse,
                      kernel_inverse, gains,
                      slots, near, kept, sums, delta_own,
                      delta, wide, spec_d, spec_y, spec_u, back, share):
    me = info[0]
    step, width = d0.shape
    part = slots.ref.shape[2]
    half = step
    for k, piece in enumerate((d0, d1, d2, d3)):
        block = me ^ k
        r = block_at(block, step)
        delta[r, :] = piece[...]
        down = dot(piece[...], weights[2], NN) * row_mask(info, block * step, step)
        back[r, part:] = (down * conv[r, :] * slope[r, :]).astype(BF16)
        wide[:, block_at(block, part)] = down * act[r, :]
    delta_own.ref[...] = delta[:, block_at(me, part)]
    delta_own.send()
    spec_d[...] = table_dot(forward, wide[...])

    def store(q, rows, real, imag):
        spec_y[rows : rows + 64, q * part : (q + 1) * part] = real
        spec_y[half + rows : half + rows + 64, q * part : (q + 1) * part] = imag

    def store_rows(q, rows, real, imag):
        spec_u[2 * half * q + rows : 2 * half * q + rows + 64, :] = real
        spec_u[2 * half * q + half + rows : 2 * half * q + half + rows + 64, :] = imag

    spectral_blocks(lane_pair(spec_d, half), row_pair(spec_k, half), True, store)
    wide[...] = table_dot(inverse, spec_y[...])
    for c in range(4):
        back[c * half : (c + 1) * half, :part] = wide[:, c * part : (c + 1) * part].astype(BF16)
    spectral_blocks(lane_pair(spec_d, half), lane_pair(spec_v, half), True, store_rows)
    grad_kernel = table_dot(kernel_inverse, spec_u[...])
    grads = dot(normed[...], back[...], TN)
    grad_out = dot(delta[...], branch[...], TN)
    dp = slots.ref.shape[0]
    rows = width // dp
    taps = grad_kernel.shape[0] // dp
    for i in range(dp):
        r = slice(i * rows, (i + 1) * rows)
        slots.ref[i, :rows, :] = grads[r, :part].astype(slots.ref.dtype)
        slots.ref[i, rows : 2 * rows, :] = grads[r, part:].astype(slots.ref.dtype)
        slots.ref[i, 2 * rows : 3 * rows, :] = grad_out[r, :].astype(slots.ref.dtype)
        slots.ref[i, 3 * rows :, :] = grad_kernel[i * taps : (i + 1) * taps, :].astype(slots.ref.dtype)
    slots.send()
    ones = jnp.ones((8, width), BF16)
    gain = jnp.broadcast_to(gains[0:1, :], (8, width)).astype(BF16)
    for c in range(4):
        r = slice(c * step, (c + 1) * step)
        out = dot(back[r, :part], weights[0], NT) + dot(back[r, part:], weights[1], NT)
        share[r, :] = out
        first = dot(gain, out.astype(BF16), NT)
        second = dot(ones, (out * normed[r, :].astype(F32)).astype(BF16), NT)
        for h in range(step // part):
            at = c * (step // part) + h
            sums[at : at + 1, :] = first[0:1, h * part : (h + 1) * part]
            sums[8 + at : 9 + at, :] = second[0:1, h * part : (h + 1) * part]
    for k in range(4):
        block = share[:, block_at(me ^ k, part)]
        if k % 2:
            near.ref[k // 2] = block.astype(BF16)
        else:
            kept.ref[k // 2] = block


def moment_kernel(info, arrived, moment, count, sums, moment_new, kernel_total, o0, o1, o2, o3, new):
    me = info[0]
    dp = arrived.shape[0]
    _, rows, _ = moment.ref.shape
    total = arrived[0].astype(F32)
    for i in range(1, dp):
        total = total + arrived[i].astype(F32)
    moment = moment.ready()
    for which in range(3):
        value = MOMENT_DECAY * moment[which] + total[which * rows : (which + 1) * rows, :] / count[0:1, :]
        moment_new.ref[which] = value
        new[which] = value.astype(new.dtype)
    kernel_total[...] = total[3 * rows :, :]
    for k, out in enumerate((o0, o1, o2, o3)):
        out[:rows, :] = new[jnp.minimum(me ^ k, 2)]
        out[rows:, :] = sums[...].astype(out.dtype)


def payload_kernel(info, mine, came, n_own, g0, g1, g2, g3, kernel_total, gain_two, payload, extra):
    me = info[0]
    part = mine.shape[1]
    rows = g0.shape[0] - 16
    total = mine[...] + came[...].astype(F32)
    for k, piece in enumerate((g0, g1, g2, g3)):
        payload[0, :rows, block_at(me ^ k, part)] = piece[:rows, :]
    extra[...] = jnp.zeros_like(extra)
    for g in range(min(3, kernel_total.shape[0] // 8)):
        extra[:, g * part : (g + 1) * part] = kernel_total[8 * g : 8 * g + 8, :]
    extra[0:1, 3 * part :] = jnp.sum(total * n_own.ready()[...], 0, keepdims=True)
    for q in range(4):
        extra[1 + q : 2 + q, 3 * part :] = gain_two[:, q * part : (q + 1) * part]
    high, low = split(extra[...])
    payload[0, rows:, :] = jnp.concatenate([high.astype(F32), low.astype(F32)], 0).astype(payload.dtype)
    for i in range(1, payload.shape[0]):
        payload[i] = payload[0]


def output_kernel(info, mine, came, out_mine, out_came, delta_own, n_own, inv, middle_own, gains, g0, g1, g2, g3, input_grad, block_out):
    part = mine.shape[1]
    width = 4 * part
    rows = g0.shape[0] - 16
    gain = gains[0:1, block_at(info[0], part)]
    sums = 0.0
    for piece in (g0, g1, g2, g3):
        sums = sums + piece[rows:, :].astype(F32)
    sums = sums / width
    middle_own = middle_own.ready()
    n_own, inv, delta_own = n_own.ready(), inv.ready(), delta_own.ready()
    for h in range(mine.shape[0] // part):
        r = slice(h * part, (h + 1) * part)
        block_out.ref[r, :] = (middle_own[r, :] + (out_mine[r, :] + out_came[r, :].astype(F32))).astype(BF16)
        column = lambda at: jnp.broadcast_to(sums[at : at + 1, :], (part, part)).T
        total = mine[r, :] + came[r, :].astype(F32)
        back = total * gain - column(h) - n_own[r, :] * column(8 + h)
        input_grad.ref[r, :] = delta_own[r, :].astype(F32) + inv[r, :] * back


def step_kernel(info, pieces, m0, m1, m2, m3, out, kernel_all, matrix, large, a, q, p, gains, small):
    me, row = info[0], info[2]
    dp = gains.shape[0]
    rows = small.shape[0]
    part = kernel_all.shape[1]
    hidden = m0.shape[1]
    for i in range(dp):
        matrix[i * rows : (i + 1) * rows, :] = pieces[i, :rows, :]
        both = pieces[i, rows:, :].astype(F32)
        both = both[:8, :] + both[8:, :]
        for g in range(3):
            kernel_all[i * 24 + 8 * g : i * 24 + 8 * g + 8, :] = both[:, g * part : (g + 1) * part]
        gains[i] = both[:, 3 * part :]
    gain = gains[0]
    for i in range(1, dp):
        gain = gain + gains[i]
    high, low = split(gain)
    gain = jnp.concatenate([high.astype(F32), low.astype(F32)], 0).astype(out.dtype)
    for k in range(8):
        out[k, rows:, :part] = gain
        out[k, rows:, part:] = jnp.zeros((16, out.shape[2] - part), out.dtype)

    @pl.when(me < 3)
    def _():
        small[...] = newton_schulz(matrix[...], a, q, p, pl.multiple_of(row * rows, rows), rows)
        for k in range(8):

            @pl.when(row % 2 == k // 4)
            def _(k=k):
                out[k, :rows, :part] = small[:, (k % 4) * part : (k % 4 + 1) * part].astype(out.dtype)

    @pl.when(me == 3)
    def _():
        for k, piece in enumerate((m0, m1, m2, m3)):
            large[:, block_at(3 ^ k, hidden)] = piece[...]
        start = pl.multiple_of((row // 2) * (2 * rows), 2 * rows)
        result = newton_schulz(large[...], a, q, p, start, 2 * rows)
        for k in range(8):
            lanes = slice((k % 4) * hidden, (k % 4 + 1) * hidden)
            out[k, :rows, :] = result[(k // 4) * rows : (k // 4 + 1) * rows, lanes].astype(out.dtype)


def final_kernel(info, got, moment_mine, moment_back, mixer_weights, mlp_weights, norm_gains, gain_moment, count,
                 mixer_new, mlp_new, mlp_moment_new, gain_moment_new, gains_new, gains):
    row = info[2]
    _, rows, part = mixer_new.ref.shape
    hidden = mlp_new.ref.shape[2]
    width = 4 * part
    side = row % 2
    for t in range(4):
        both = got[4 * side + t, rows:, :part].astype(F32)
        gains[t] = both[:8, :] + both[8:, :]
    for t in range(3):
        old = mixer_weights[t, block_at(row, rows), :].astype(F32)
        mixer_new.ref[t] = old - MATRIX_RATE * got[4 * side + t, :rows, :part].astype(F32)
    mixer_new.send()
    mlp_moment_new.ref[side] = moment_mine.ready()[...]
    mlp_moment_new.ref[1 - side] = moment_back.ready()[...]
    mlp_moment_new.send()
    rate = MATRIX_RATE * math.sqrt(4 * hidden / width)
    for which in range(2):
        old = mlp_weights[which, block_at(row, rows), :].astype(F32)
        mlp_new.ref[which] = old - rate * got[4 * which + 3, :rows, :].astype(F32)

    mlp_new.send()
    two = gains[0] + gains[1] + gains[2] + gains[3]
    for t in range(4):
        lanes = slice(t * part, (t + 1) * part)
        totals = (gains[t][0:1, :], two[1 + t : 2 + t, :])
        for which in range(2):
            gain_moment_new[which : which + 1, lanes] = (
                MOMENT_DECAY * gain_moment[which : which + 1, lanes] + totals[which] / count[0:1, :]
            )
    new = gain_moment_new[...]
    scale = jnp.sqrt(jnp.mean(new * new, 1, keepdims=True)) + 1e-08
    gains_new[...] = norm_gains[...] - GAIN_RATE * new / scale


def per_device(
    tokens,
    cotangent,
    lengths,
    norm_gains,
    conv_kernel,
    mixer_weights,
    mlp_weights,
    gain_moment,
    kernel_moment,
    mixer_moment,
    mlp_moment,
):
    _, bucket, part = tokens.shape
    levels, taps, _ = conv_kernel.shape
    hidden = mlp_weights.shape[2]
    me = lax.axis_index("tensor")
    row = lax.axis_index("dp")
    dp = lax.axis_size("dp")
    width = 4 * part
    rows = width // dp
    half = bucket // 4
    piece_type = BF16 if rows % 16 == 0 else F32
    share = -(-levels * taps // dp)
    slot = -(-share // 8) * 8
    slot += (3 * rows + slot) % 16
    forward, inverse, kernel_forward, kernel_inverse = conv_tables(bucket, levels, taps, dp, slot)
    info = jnp.stack([me, lengths[0], row]).astype(jnp.int32)

    (spec_k,) = call(
        spectrum_kernel,
        [((8 * half, part), F32)],
        [],
        (info, Late(kernel_forward), Late(conv_kernel.reshape(levels * taps, part))),
        2, 10,
    )
    x_own, in_weights, in_gains, forward_one, inverse_one, late = fetch(
        info, tokens[0], mixer_weights, norm_gains, forward, inverse, (cotangent[0], mixer_weights[2])
    )
    x_pieces = gather_tensor(tokens[0], spec_k, x_own)

    act_like = ((bucket, part), F32)
    wide_like = ((half, width), F32)
    spec_like = ((2 * half, width), F32)
    whole_like = ((bucket, width), BF16)
    quarter_like = ((half, width), BF16)
    x, normed, n_own, inv_one, spec_v, conv, gate_act, gate_slope, branch, gains = call(
        entry_kernel,
        [whole_like, whole_like, Store(*act_like), Store((bucket, 1), F32), spec_like, act_like, act_like, act_like,
         ((bucket, part), BF16), ((2, width), F32)],
        [wide_like, spec_like],
        (info, x_own, *x_pieces[1:], in_weights, in_gains, forward_one, inverse_one, spec_k),
        0, 24,
    )
    late = gather_tensor(late, branch)
    cot, out_weights, delta_active, mlp_kept = call(
        cotangent_kernel,
        [whole_like, ((width, width), BF16), ((bucket, hidden), F32), (mlp_weights.shape, BF16)],
        [],
        (after(info, branch), *late, Late(mlp_weights)),
        3, 8,
    )
    branch_pieces = gather_tensor(branch, delta_active)
    near, kept, normed_two, active, delta_hidden, n_mine, inv_mine, middle_own = call(
        middle_kernel,
        [((width, width), BF16), ((width, width), F32), whole_like, ((bucket, hidden), BF16),
         ((bucket, hidden), BF16), wide_like, ((half, 1), F32), Store(*act_like)],
        [whole_like, ((bucket, width), F32)],
        (info, *branch_pieces, out_weights, x, gains, mlp_kept, delta_active),
        6, 24,
    )
    split_blocks = lambda v: v.reshape(2, -1, v.shape[-1])
    came = swap(split_blocks(near), "tensor", 1)
    mine, far = call(join_kernel, [wide_like, quarter_like], [], (info, split_blocks(kept), came), 1, 4)
    mlp_keep, mlp_send, moment_send, out_near, out_kept = call(
        mlp_kernel,
        [((width + 16, hidden), F32), ((width + 16, hidden), BF16), ((rows, hidden), F32), Store((2, bucket, part), BF16),
         Store((2, bucket, part), F32)],
        [((bucket, width), F32)],
        (after(info, far), normed_two, active, delta_hidden, cot, mlp_kept, Late(mlp_moment)),
        4, 20,
    )
    mlp_came = swap(mlp_send, "dp", 1)
    moment_came = swap(moment_send, "dp", 1)
    came = swap(far, "tensor", 2)
    delta_mid, grad_gain_two = call(
        norm_back_kernel,
        [quarter_like, ((1, width), F32)],
        [],
        (after(info, out_near), mine, came, cot, n_mine, inv_mine, gains),
        1000, 6,
    )
    (kernel_inverse_one,) = fetch(after(info, delta_mid), kernel_inverse)
    delta_pieces = gather_tensor(delta_mid, kernel_inverse_one)

    slots, one_near, one_kept, sums, delta_own = call(
        mixer_back_kernel,
        [Store((dp, 3 * rows + slot, part), piece_type), Store((2, bucket, part), BF16), Store((2, bucket, part), F32),
         ((16, part), F32), Store((bucket, part), BF16)],
        [whole_like, wide_like, spec_like, spec_like, ((8 * half, part), F32), ((bucket, 2 * part), BF16),
         ((bucket, width), F32)],
        (info, *delta_pieces, in_weights, gate_act, gate_slope, conv, branch, normed, spec_v, spec_k, forward_one, inverse_one,
         kernel_inverse_one, gains),
        0, 32,
    )
    arrived = lax.all_to_all(slots.astype(BF16), "dp", 0, 0, tiled=True)
    one_mine, far = call(
        join_late_kernel,
        [act_like, ((bucket, part), BF16)],
        [],
        (info, Late(one_kept), swap(one_near, "tensor", 1)),
        0, 4,
    )
    one_came = swap(far, "tensor", 2)
    out_mine, out_far = call(
        join_late_kernel,
        [act_like, ((bucket, part), BF16)],
        [],
        (info, Late(out_kept), swap(after(out_near, far), "tensor", 1)),
        1000, 4,
    )
    out_came = swap(out_far, "tensor", 2)
    pairs = dp // 2
    block = (2 * rows + 16, hidden)
    if dp == 8:
        blocks = call(mlp_rows_kernel, [(block, BF16)] * pairs, [], (info, mlp_keep, mlp_came), 1, 6)
        blocks = [blocks[0]] + [swap(blocks[k], "dp", 2 * k) for k in range(1, pairs)]
    else:
        (blocks,) = call(mlp_rows_kernel, [((pairs, *block), BF16)], [], (info, mlp_keep, mlp_came), 1, 6)
        parities = [[i for i in range(dp) if i % 2 == y] for y in range(2)]
        blocks = [lax.all_to_all(blocks, "dp", 0, 0, tiled=True, axis_index_groups=parities)]
    pair, moment_mine, moment_other, count = call(
        mlp_moment_kernel,
        [((2 * rows, hidden), BF16), Store((rows, hidden), F32), Store((rows, hidden), F32), ((8, part), F32)],
        [],
        (info, mlp_moment, moment_came, *blocks),
        1, 8,
    )
    if dp == 8:
        pair_pieces = [pair] + [swap(pair, "dp", 2 * k) for k in range(1, pairs)]
    else:
        pair_pieces = [lax.all_gather(pair, "dp", axis=0, tiled=True, axis_index_groups=parities)]
    mixer_moment_new, kernel_total, *sends = call(
        moment_kernel,
        [Store((3, rows, part), F32), ((slot, part), F32)] + [((rows + 16, part), piece_type)] * 4,
        [((3, rows, part), piece_type)],
        (after(info, out_far), arrived, Late(mixer_moment), count, sums),
        0, 6,
    )
    got = [sends[0]] + [swap(sends[k].astype(BF16), "tensor", k) for k in (1, 2, 3)]
    (payload,) = call(
        payload_kernel,
        [((dp, rows + 16, width), piece_type)],
        [((8, width), F32)],
        (info, one_mine, one_came, Late(n_own), *(g.astype(piece_type) for g in got), kernel_total, grad_gain_two),
        0, 4,
    )
    everything = lax.all_to_all(payload.astype(BF16), "dp", 0, 0, tiled=True)
    (mlp_columns,) = call(
        columns_kernel, [((width, hidden), BF16)], [], (after(info, payload), *pair_pieces), 0, 4
    )
    mlp_pieces = [mlp_columns] + [lax.ppermute(mlp_columns, "tensor", [(3 ^ k, 3)]) for k in (1, 2, 3)]
    input_grad, block_out = call(
        output_kernel,
        [Store(*act_like), Store((bucket, part), BF16)],
        [],
        (after(info, payload), one_mine, one_came, out_mine, out_came, Late(delta_own), Late(n_own), Late(inv_one), Late(middle_own), gains,
         *(g.astype(piece_type) for g in got)),
        1000, 8,
    )
    square = ((width, width), F32)
    sends, kernel_all = call(
        step_kernel,
        [((8, rows + 16, hidden), piece_type), ((dp * 24, part), F32)],
        [((width, width), piece_type), ((width, 4 * hidden), BF16), square, square, square, ((dp, 8, part), F32),
         ((rows, width), F32)],
        (after(info, block_out), everything.astype(piece_type), *mlp_pieces),
        18, 24,
    )
    groups = [[8 * z + q for q in range(8)] for z in range(dp // 2)]
    got = lax.all_to_all(sends.astype(BF16), ("dp", "tensor"), 0, 0, tiled=True, axis_index_groups=groups)
    moment_back = swap(after(moment_other, payload), "dp", 1)
    old = fetch(after(info, kernel_all), mixer_weights, mlp_weights, norm_gains, gain_moment)
    mixer_new, mlp_new, mlp_moment_new, gain_moment_new, gains_new = call(
        final_kernel,
        [Store((3, rows, part), F32), Store((2, rows, hidden), F32), Store((2, rows, hidden), F32), ((2, width), F32),
         ((2, width), F32)],
        [((4, 8, part), F32)],
        (info, got.astype(piece_type), Late(moment_mine), Late(moment_back), *old, count),
        3, 10,
    )
    grad_kernel = kernel_all.reshape(dp, 24, part)[:, :share].reshape(-1, part)[: levels * taps]
    kernel_moment_new = MOMENT_DECAY * kernel_moment + grad_kernel.reshape(levels, taps, part) / count[0]
    kernel_scale = (
        jnp.sqrt(jnp.mean(kernel_moment_new * kernel_moment_new, axis=(0, 1), keepdims=True)) + 1e-08
    )
    kernel_new = conv_kernel - KERNEL_RATE * kernel_moment_new / kernel_scale
    return (
        block_out[None],
        input_grad[None],
        gain_moment_new,
        gains_new,
        kernel_moment_new,
        kernel_new,
        mixer_moment_new,
        mixer_new,
        mlp_moment_new,
        mlp_new,
    )


def solution(mesh):
    tokens = P("dp", None, "tensor")
    columns = P(None, None, "tensor")
    blocks = P(None, "dp", "tensor")
    return jax.shard_map(
        per_device,
        mesh=mesh,
        in_specs=(tokens, tokens, P("dp"), P(), columns, columns, columns, P(), columns, blocks, blocks),
        out_specs=(tokens, tokens, P(), P(), columns, columns, blocks, blocks, blocks, blocks),
        check_vma=False,
    )
```

```python
import functools
import math

import jax
import jax.numpy as jnp
import ml_dtypes
import numpy as np
from jax import lax
from jax.experimental import pallas as pl
from jax.experimental.pallas import tpu as pltpu
from jax.sharding import PartitionSpec as P

NS_STEPS = 5
EPSILON = 1e-05
NS_COEF_A = 3.4445
NS_COEF_B = -4.775
NS_COEF_C = 2.0315
MOMENT_DECAY = 0.5
MATRIX_RATE = 1.0
GAIN_RATE = 0.1
KERNEL_RATE = 0.125
SCALE = 10**10
BF16 = jnp.bfloat16
F32 = jnp.float32


def conv_tables(bucket, levels, taps, dp, slot):
    half = bucket // 4
    size = 2 * half
    t = np.arange(half)
    k = np.arange(half)
    phase = 2 * np.pi * ((k[:, None] * t[None, :]) % size) / size
    forward = np.concatenate([np.cos(phase), -np.sin(phase)], 0)
    forward[half] = (-1.0) ** t
    scale = np.full((half,), 2.0 / size)
    scale[0] = 1.0 / size
    inverse = np.concatenate(
        [np.cos(phase).T * scale[None, :], -np.sin(phase).T * scale[None, :]], 1
    )
    inverse[:, half] = ((-1.0) ** t) / size
    spread = np.zeros((bucket, levels * taps))
    at = 0
    for level in range(levels):
        for tap in range(taps):
            width = 2**level
            spread[at : at + width, level * taps + tap] = 0.5**level
            at += width
    kernel_forward = np.concatenate(
        [forward @ spread[m * half : (m + 1) * half] for m in range(4)], 0
    )
    kernel_inverse = np.concatenate(
        [spread[m * half : (m + 1) * half].T @ inverse for m in range(4)], 1
    )
    share = -(-levels * taps // dp)
    kernel_inverse = np.pad(kernel_inverse, ((0, dp * share - levels * taps), (0, 0)))
    kernel_inverse = kernel_inverse.reshape(dp, share, -1)
    kernel_inverse = np.pad(kernel_inverse, ((0, 0), (0, slot - share), (0, 0))).reshape(dp * slot, -1)
    tables = []
    for table in (forward, inverse, kernel_forward, kernel_inverse):
        high = table.astype(ml_dtypes.bfloat16)
        low = (table - high.astype(np.float64)).astype(ml_dtypes.bfloat16)
        tables.append(np.stack([high, low]))
    return tables


def cross(a, b):
    return a[0] * b[0] - a[1] * b[1], a[0] * b[1] + a[1] * b[2]


def cross_conj(a, b):
    return a[0] * b[0] + a[1] * b[1], a[1] * b[2] - a[0] * b[1]


def with_edge(spec, first):
    real, imag = spec
    return real, jnp.where(first, 0.0, imag), jnp.where(first, imag, real)


def add_pairs(pairs):
    return functools.reduce(lambda p, q: (p[0] + q[0], p[1] + q[1]), pairs)


def spectral_blocks(left, right, conj, store):
    for step in range(4):
        rows = step * 64
        index = lax.broadcasted_iota(jnp.int32, (64, 128), 0)
        first = index + rows == 0
        sign = 1.0 - 2.0 * (index % 2).astype(F32)
        a = [left(r, rows) for r in range(4)]
        b = [with_edge(right(m, rows), first) for m in range(4)]
        if conj:
            sums = [add_pairs([cross_conj(a[r], b[r - q]) for r in range(q, 4)]) for q in range(4)]
        else:
            sums = [add_pairs([cross(a[r], b[q - r]) for r in range(q + 1)]) for q in range(4)]
        for q in range(4):
            other = q + 1 if conj else q - 1
            if 0 <= other < 4:
                real = sums[q][0] + sign * sums[other][0]
                imag = sums[q][1] + sign * sums[other][1]
            else:
                real, imag = sums[q]
            store(q, rows, real, imag)


def lane_pair(ref, half):
    return lambda r, rows: (
        ref[rows : rows + 64, r * 128 : (r + 1) * 128],
        ref[half + rows : half + rows + 64, r * 128 : (r + 1) * 128],
    )


def row_pair(ref, half):
    return lambda r, rows: (
        ref[2 * half * r + rows : 2 * half * r + rows + 64, :],
        ref[2 * half * r + half + rows : 2 * half * r + half + rows + 64, :],
    )


def gelu_both(x):
    c = math.sqrt(2.0 / math.pi)
    t = jnp.tanh(c * (x + 0.044715 * x * x * x))
    value = 0.5 * x * (1.0 + t)
    slope = 0.5 * (1.0 + t) + 0.5 * x * (1.0 - t * t) * (c * (1.0 + 3 * 0.044715 * x * x))
    return value, slope


def after(value, *others):
    return lax.optimization_barrier((value, *others))[0]


def swap(value, axis, k):
    size = lax.axis_size(axis)
    return lax.ppermute(value, axis, [(i, i ^ k) for i in range(size)])


def gather_tensor(value, *meanwhile):
    far = swap(value, "tensor", 2)
    near = swap(value, "tensor", 1)
    if meanwhile:
        far = after(far, *meanwhile)
    far_near = swap(far, "tensor", 1)
    return [value, near, far, far_near]


def gather_dp(value, me, low=0):
    size = lax.axis_size("dp")
    whole = value[None]
    while (1 << low) < size:
        bits = min(3, size.bit_length() - 1 - low)
        mine = (me >> low) & ((1 << bits) - 1)
        out = jnp.zeros((1 << bits,) + whole.shape, whole.dtype)
        for k in range(1 << bits):
            piece = whole if k == 0 else swap(whole, "dp", k << low)
            out = lax.dynamic_update_index_in_dim(out, piece, mine ^ k, 0)
        whole = out.reshape((-1,) + value.shape)
        low += bits
    return whole


def dot(a, b, contract):
    return lax.dot_general(a, b, ((contract[0], contract[1]), ((), ())), preferred_element_type=F32)


NN = ((1,), (0,))
NT = ((1,), (1,))
TN = ((0,), (0,))


def split(value):
    high = value.astype(BF16)
    return high, (value - high.astype(F32)).astype(BF16)


def table_dot(table, value):
    high, low = split(value)
    return dot(table[0], high, NN) + (dot(table[1], high, NN) + dot(table[0], low, NN))


def symmetric(left, right, product):
    half = left[0].shape[0] // 2
    top = product([v[:half] for v in left], right, None)
    low = product([v[half:] for v in left], right, half)
    return jnp.concatenate([top, jnp.concatenate([top[:, half:].T, low], 1)], 0)


def three_terms(left, right, cut=None):
    right = right if cut is None else [v[:, cut:] for v in right]
    return dot(left[0], right[0], NN) + (dot(left[0], right[1], NN) + dot(left[1], right[0], NN))


def newton_schulz(matrix, a_ref, p_ref, r_ref, start):
    size = a_ref.shape[0]
    row = lax.broadcasted_iota(jnp.int32, (size, size), 0)
    col = lax.broadcasted_iota(jnp.int32, (size, size), 1)
    unit = (row == col).astype(F32)
    gram = symmetric([matrix], [matrix], lambda a, b, cut: dot(a[0], b[0] if cut is None else b[0][cut:], NT))
    scale = 1.0 / (jnp.sqrt(jnp.sum(gram * unit)) + 1e-07)
    a_ref[...] = gram * (scale * scale)

    def advance(first):
        a = a_ref[...]
        terms = split(a)
        poly = NS_COEF_A * unit + NS_COEF_B * a + NS_COEF_C * symmetric(terms, terms, three_terms)
        poly_terms = split(poly)
        if first:
            p_ref[...] = poly
            r_ref[...] = p_ref[pl.ds(start, r_ref.shape[0]), :]
        else:
            r_ref[...] = three_terms(split(r_ref[...]), poly_terms)
        half = symmetric(terms, poly_terms, three_terms)
        a_ref[...] = symmetric(poly_terms, split(half), three_terms)

    advance(True)
    pl.loop(0, NS_STEPS - 2)(lambda _: advance(False))
    rows, terms = r_ref[...], split(a_ref[...])
    once = three_terms(split(rows), terms)
    rows = NS_COEF_A * rows + NS_COEF_B * once + NS_COEF_C * three_terms(split(once), terms)
    high, low = split(rows)
    return scale * (dot(high, matrix, NN) + dot(low, matrix, NN))


VMEM = pl.BlockSpec(memory_space=pltpu.VMEM)
SMEM = pl.BlockSpec(memory_space=pltpu.SMEM)


HBM = pl.BlockSpec(memory_space=pltpu.HBM)


class Late:
    def __init__(self, array):
        self.shape, self.dtype = array.shape, array.dtype
        self.array = pltpu.with_memory_space_constraint(array, pltpu.HBM)


class Store:
    def __init__(self, shape, dtype):
        self.shape, self.dtype = shape, dtype


class Waiting:
    def __init__(self, copy, ref):
        self.copy, self.ref, self.started = copy, ref, False

    def ready(self):
        self.copy.wait()
        return self.ref

    def send(self):
        self.copy.start()
        self.started = True


def call(kernel, outs, scratch, args, time, limit):
    outs = [o if isinstance(o, Store) else jax.ShapeDtypeStruct(*o) for o in outs]
    late = [a for a in (*args, *outs) if isinstance(a, (Late, Store))]
    n_in, n_out = len(args), len(outs)

    def body(*refs):
        given, rest = refs[: n_in + n_out], refs[n_in + n_out :]
        buffers, rest = rest[: len(late)], rest[len(late) :]
        semaphores = rest[-1] if late else None
        passed, stores, at = [], [], 0
        for what, ref in zip((*args, *outs), given):
            if isinstance(what, Late):
                copy = pltpu.make_async_copy(ref, buffers[at], semaphores.at[at])
                copy.start()
            elif isinstance(what, Store):
                copy = pltpu.make_async_copy(buffers[at], ref, semaphores.at[at])
            else:
                passed.append(ref)
                continue
            passed.append(Waiting(copy, buffers[at]))
            if isinstance(what, Store):
                stores.append(passed[-1])
            at += 1
        kernel(*passed, *(rest[:-1] if late else rest))
        for store in stores:
            if not store.started:
                store.send()
        for store in stores:
            store.copy.wait()

    return pl.pallas_call(
        body,
        out_shape=tuple(pltpu.HBM(o.shape, o.dtype) if isinstance(o, Store) else o for o in outs),
        in_specs=[SMEM] + [HBM if isinstance(a, Late) else VMEM for a in args[1:]],
        out_specs=tuple(HBM if isinstance(o, Store) else VMEM for o in outs),
        scratch_shapes=[pltpu.VMEM(a.shape, a.dtype) for a in late]
        + [pltpu.VMEM(shape, dtype) for shape, dtype in scratch]
        + ([pltpu.SemaphoreType.DMA((len(late),))] if late else []),
        compiler_params=pltpu.CompilerParams(vmem_limit_bytes=limit * 2**20),
        cost_estimate=pl.CostEstimate(flops=max(time * SCALE, 10**6), bytes_accessed=0, transcendentals=0),
    )(*(a.array if isinstance(a, Late) else a for a in args))


def fetch(token, time, *arrays):
    arrays = [a if isinstance(a, list) else [(a, None)] for a in arrays]
    shapes = []
    for a in arrays:
        cuts = [p.shape if index is None else p.shape[1:] for p, index in a]
        shapes.append(jax.ShapeDtypeStruct((sum(c[0] for c in cuts), *cuts[0][1:]), a[0][0].dtype))
    flat = [pltpu.with_memory_space_constraint(p, pltpu.HBM) for a in arrays for p, _ in a]

    def body(token_ref, *refs):
        outs, semaphores, copies, at = refs[len(flat) : -1], refs[-1], [], 0
        for a, out in zip(arrays, outs):
            row = 0
            for _, index in a:
                source = refs[at] if index is None else refs[at].at[index]
                target = out if len(a) == 1 else out.at[row : row + source.shape[0]]
                copies.append(pltpu.make_async_copy(source, target, semaphores.at[at]))
                copies[-1].start()
                row, at = row + source.shape[0], at + 1
        for copy in copies:
            copy.wait()

    return pl.pallas_call(
        body,
        out_shape=tuple(shapes),
        in_specs=[SMEM] + [HBM] * len(flat),
        out_specs=(VMEM,) * len(shapes),
        scratch_shapes=[pltpu.SemaphoreType.DMA((len(flat),))],
        compiler_params=pltpu.CompilerParams(vmem_limit_bytes=2 * 2**20),
        cost_estimate=pl.CostEstimate(flops=max(time * SCALE, 10**6), bytes_accessed=0, transcendentals=0),
    )(token, *flat)


def block_at(index, size):
    return pl.ds(pl.multiple_of(index * size, size), size)


def row_mask(info, start, rows):
    return (start + lax.broadcasted_iota(jnp.int32, (rows, 1), 0) < info[1]).astype(F32)


def spectrum_kernel(info, table, taps, spec_k):
    taps = taps.ready()[...]
    spec_k[...] = table_dot(table.ready(), taps)


def entry_kernel(info, p0, p1, p2, p3, weights, gains, forward, inverse, spec_k,
                 x, normed, n_own, inv, spec_v, conv, act, slope, branch, gains_kept, wide, spec_y):
    me = info[0]
    part = p1.shape[1]
    for k, piece in enumerate((p0, p1, p2, p3)):
        x[:, block_at(me ^ k, part)] = piece[...]
    gains_kept[...] = gains[...]
    gain = gains[0:1, :]
    half = x.shape[0] // 4
    for c in range(4):
        r = slice(c * half, (c + 1) * half)
        v = x[r, :].astype(F32)
        mean = jnp.mean(v, 1, keepdims=True)
        centred = v - mean
        scale = lax.rsqrt(jnp.mean(centred * centred, 1, keepdims=True) + EPSILON)
        normed[r, :] = (centred * scale * gain).astype(BF16)
        inv.ref[r, :] = scale
        n_own.ref[r, :] = (p0[r, :].astype(F32) - mean) * scale
    n_own.send()
    inv.send()
    for c in range(4):
        r = slice(c * half, (c + 1) * half)
        normal = normed[r, :]
        wide[:, c * part : (c + 1) * part] = dot(normal, weights[0], NN)
        act[r, :], slope[r, :] = gelu_both(dot(normal, weights[1], NN))
    spec_v[...] = table_dot(forward, wide[...])

    def store(q, rows, real, imag):
        spec_y[rows : rows + 64, q * part : (q + 1) * part] = real
        spec_y[half + rows : half + rows + 64, q * part : (q + 1) * part] = imag

    spectral_blocks(lane_pair(spec_v, half), row_pair(spec_k, half), False, store)
    wide[...] = table_dot(inverse, spec_y[...])
    for c in range(4):
        r = slice(c * half, (c + 1) * half)
        out = wide[:, c * part : (c + 1) * part]
        conv[r, :] = out
        out = (act[r, :] * out * row_mask(info, c * half, half)).astype(BF16)
        branch[r, :] = out


def cotangent_kernel(info, p0, p1, p2, p3, weights, cot, out_w, delta, weights_kept):
    part = p0.shape[1]
    for k, piece in enumerate((p0, p1, p2, p3)):
        cot[:, block_at(info[0] ^ k, part)] = piece[: cot.shape[0], :]
        out_w[:, block_at(info[0] ^ k, part)] = piece[cot.shape[0] :, :]
    step = cot.shape[0] // 4
    weights = weights.ready()
    weights_kept[...] = weights[...]
    for c in range(4):
        r = slice(c * step, (c + 1) * step)
        delta[r, :] = dot(cot[r, :], weights[1], NN)


def middle_kernel(info, b0, b1, b2, b3, out_w, x, gains, weights, delta_active,
                  near, kept, normed, active, delta_hidden, n_mine, inv_mine, middle_own, branch, middle):
    me = info[0]
    part = b0.shape[1]
    step = x.shape[0] // 4
    for k, piece in enumerate((b0, b1, b2, b3)):
        branch[:, block_at(me ^ k, part)] = piece[...]
    gain = gains[1:2, :]
    for k in (1, 3, 0, 2):
        block = me ^ k
        r = block_at(block, step)
        mid = x[r, :].astype(F32) + dot(branch[r, :], out_w[...], NT)
        middle[r, :] = mid
        centred = mid - jnp.mean(mid, 1, keepdims=True)
        scale = lax.rsqrt(jnp.mean(centred * centred, 1, keepdims=True) + EPSILON)
        normal = centred * scale
        if k == 0:
            n_mine[...] = normal
            inv_mine[...] = scale
        normal = (normal * gain).astype(BF16)
        normed[r, :] = normal
        value, slope = gelu_both(dot(normal, weights[0], NN))
        mask = row_mask(info, block * step, step)
        active[r, :] = (value * mask).astype(BF16)
        back = (delta_active[r, :] * mask * slope).astype(BF16)
        delta_hidden[r, :] = back
        share = dot(back, weights[0], NT)
        if k % 2:
            near[(k // 2) * step : (k // 2 + 1) * step, :] = share.astype(BF16)
        else:
            kept[(k // 2) * step : (k // 2 + 1) * step, :] = share
    middle_own.ref[...] = middle[:, block_at(me, part)]


def mlp_kernel(info, normed, active, delta_hidden, cot, moment, out, moment_send, away):
    size = normed.shape[1]
    wanted = (info[2] + away) % 2

    @pl.when(wanted == 0)
    def _():
        out[:size, :] = dot(normed[...], delta_hidden[...], TN).astype(out.dtype)

    @pl.when(wanted == 1)
    def _():
        out[:size, :] = dot(cot[...], active[...], TN).astype(out.dtype)

    length = jnp.full((16, out.shape[1]), 1, jnp.int32) * info[1]
    first = lax.broadcasted_iota(jnp.int32, length.shape, 0) == 0
    out[size:, :] = jnp.where(first, length // 32, length % 32).astype(F32).astype(out.dtype)
    if away:
        moment_send[...] = moment.ready()[wanted]


def mlp_away_kernel(info, normed, active, delta_hidden, cot, moment, out, moment_send):
    mlp_kernel(info, normed, active, delta_hidden, cot, moment, out, moment_send, 1)


def mlp_here_kernel(info, normed, active, delta_hidden, cot, out):
    mlp_kernel(info, normed, active, delta_hidden, cot, None, out, None, 0)


def mlp_out_kernel(info, active, weights, near, kept, part_out):
    me = info[0]
    step = active.shape[0] // 4
    part = near.ref.shape[2]
    for c in range(4):
        r = slice(c * step, (c + 1) * step)
        part_out[r, :] = dot(active[r, :], weights[1], NT)
    for k in range(4):
        share = part_out[:, block_at(me ^ k, part)]
        if k % 2:
            near.ref[k // 2] = share.astype(BF16)
        else:
            kept.ref[k // 2] = share


def mlp_rows_kernel(info, keep, came, *outs):
    size = came.shape[0] - 16
    pairs = outs[0].shape[0] if len(outs) == 1 else len(outs)
    rows = size // pairs
    length = keep[size:, :] + came[size:, :].astype(F32)
    for k in range(pairs):
        if len(outs) == 1:
            r, out = pl.ds(k * rows, rows), outs[0].at[k]
        else:
            r, out = block_at((info[2] // 2) ^ k, rows), outs[k]
        out[:rows, :] = (keep[r, :] + came[r, :].astype(F32)).astype(out.dtype)
        out[rows:, :] = length.astype(out.dtype)


def mlp_moment_kernel(info, moment, other_moment, *refs):
    *pieces, matrix, mine, other, count = refs
    rows = moment.shape[1]
    side = info[2] % 2
    if len(pieces) == 1:
        pieces = [pieces[0].at[k] for k in range(pieces[0].shape[0])]
    total = pieces[0][...].astype(F32)
    for piece in pieces[1:]:
        total = total + piece[...].astype(F32)
    tokens = 32.0 * total[2 * rows : 2 * rows + 1, :] + total[2 * rows + 1 : 2 * rows + 2, :]
    count.ref[...] = jnp.broadcast_to(tokens[:, : count.ref.shape[1]], count.ref.shape)
    old = moment[side]
    for which in range(2):
        new = total[which * rows : (which + 1) * rows, :] / tokens

        @pl.when(side == which)
        def _(new=new, which=which):
            now = MOMENT_DECAY * old + new
            mine.ref[...] = now
            matrix[which * rows : (which + 1) * rows, :] = now.astype(matrix.dtype)

        @pl.when(side != which)
        def _(new=new, which=which):
            now = MOMENT_DECAY * other_moment[...] + new
            other.ref[...] = now
            matrix[which * rows : (which + 1) * rows, :] = now.astype(matrix.dtype)


def columns_kernel(info, *refs):
    *pieces, out = refs
    rows = pieces[0].shape[0]
    for k, piece in enumerate(pieces):
        out[block_at((info[2] // 2) ^ k, rows), :] = piece[...]


def join_kernel(info, kept, came, mine, far):
    mine[...] = kept[0] + came[0].astype(F32)
    far[...] = (kept[1] + came[1].astype(F32)).astype(BF16)


def join_late_kernel(info, one_kept, one_came, out_kept, out_came, one_mine, tail, out_mine, far):
    one_kept, out_kept = one_kept.ready(), out_kept.ready()
    size = out_mine.shape[0]
    one_mine[...] = one_kept[0, :size, :] + one_came[0, :size, :].astype(F32)
    far[:size, :] = (one_kept[1, :size, :] + one_came[1, :size, :].astype(F32)).astype(BF16)
    below = one_kept[0, size:, :] + one_came[0, size:, :].astype(F32)
    high, low = split(below[16:24, :] + below[24:, :])
    below = jnp.concatenate([below[:16, :], high.astype(F32), low.astype(F32)], 0)
    tail[...] = below
    far[size : size + 32, :] = below.astype(BF16)
    out_mine[...] = out_kept[0] + out_came[0].astype(F32)
    far[size + 32 :, :] = (out_kept[1] + out_came[1].astype(F32)).astype(BF16)


def norm_back_kernel(info, mine, came, cot, n_mine, inv_mine, gains, delta, grad_gain):
    size = mine.shape[0]
    total = mine[...] + came[...].astype(F32)
    n = n_mine[...]
    q = total * gains[1:2, :]
    back = inv_mine[...] * (q - jnp.mean(q, 1, keepdims=True) - n * jnp.mean(q * n, 1, keepdims=True))
    delta[...] = (cot[block_at(info[0], size), :].astype(F32) + back).astype(BF16)
    grad_gain[...] = jnp.sum(total * n, 0, keepdims=True)


def mixer_back_kernel(info, d0, d1, d2, d3, weights, act, slope, conv, branch, normed, spec_v, spec_k, forward, inverse,
                      kernel_inverse, gains, gain_two,
                      slots, near, kept, delta_own,
                      delta, wide, spec_d, spec_y, spec_u, back, share):
    me = info[0]
    step, width = d0.shape
    part = slots.ref.shape[2]
    half = step
    for k, piece in enumerate((d0, d1, d2, d3)):
        block = me ^ k
        r = block_at(block, step)
        delta[r, :] = piece[...]
        down = dot(piece[...], weights[2], NN) * row_mask(info, block * step, step)
        back[r, part:] = (down * conv[r, :] * slope[r, :]).astype(BF16)
        wide[:, block_at(block, part)] = down * act[r, :]
    delta_own.ref[...] = delta[:, block_at(me, part)]
    delta_own.send()
    spec_d[...] = table_dot(forward, wide[...])

    def store(q, rows, real, imag):
        spec_y[rows : rows + 64, q * part : (q + 1) * part] = real
        spec_y[half + rows : half + rows + 64, q * part : (q + 1) * part] = imag

    def store_rows(q, rows, real, imag):
        spec_u[2 * half * q + rows : 2 * half * q + rows + 64, :] = real
        spec_u[2 * half * q + half + rows : 2 * half * q + half + rows + 64, :] = imag

    spectral_blocks(lane_pair(spec_d, half), row_pair(spec_k, half), True, store)
    wide[...] = table_dot(inverse, spec_y[...])
    for c in range(4):
        back[c * half : (c + 1) * half, :part] = wide[:, c * part : (c + 1) * part].astype(BF16)
    spectral_blocks(lane_pair(spec_d, half), lane_pair(spec_v, half), True, store_rows)
    grad_kernel = table_dot(kernel_inverse, spec_u[...])
    grads = dot(normed[...], back[...], TN)
    grad_out = dot(delta[...], branch[...], TN)
    dp = slots.ref.shape[0]
    rows = width // dp
    taps = grad_kernel.shape[0] // dp
    for i in range(dp):
        r = slice(i * rows, (i + 1) * rows)
        slots.ref[i, :rows, :] = grads[r, :part].astype(slots.ref.dtype)
        slots.ref[i, rows : 2 * rows, :] = grads[r, part:].astype(slots.ref.dtype)
        slots.ref[i, 2 * rows : 3 * rows, :] = grad_out[r, :].astype(slots.ref.dtype)
        slots.ref[i, 3 * rows :, :] = grad_kernel[i * taps : (i + 1) * taps, :].astype(slots.ref.dtype)
    slots.send()
    ones = jnp.ones((8, width), BF16)
    gain_one = jnp.zeros((1, width), F32)
    sums = [[], []]
    gain = jnp.broadcast_to(gains[0:1, :], (8, width)).astype(BF16)
    for c in range(4):
        r = slice(c * step, (c + 1) * step)
        out = dot(back[r, :part], weights[0], NT) + dot(back[r, part:], weights[1], NT)
        share[r, :] = out
        first = dot(gain, out.astype(BF16), NT)
        both = out * normed[r, :].astype(F32)
        gain_one = gain_one + jnp.sum(both, 0, keepdims=True)
        second = dot(ones, both.astype(BF16), NT)
        for h in range(step // part):
            sums[0].append(first[0:1, h * part : (h + 1) * part])
            sums[1].append(second[0:1, h * part : (h + 1) * part])
    gain_one = gain_one / gains[0:1, :]
    gain = [g[:, q * part : (q + 1) * part] for g in (gain_one, gain_two[...]) for q in range(4)]
    gain_high, gain_low = split(jnp.concatenate(gain, 0))
    tail = jnp.concatenate([*sums[0], *sums[1], gain_high.astype(F32), gain_low.astype(F32)], 0)
    for k in range(4):
        block = share[:, block_at(me ^ k, part)]
        if k % 2:
            near.ref[k // 2, : share.shape[0], :] = block.astype(BF16)
            near.ref[k // 2, share.shape[0] :, :] = tail.astype(BF16)
        else:
            kept.ref[k // 2, : share.shape[0], :] = block
            kept.ref[k // 2, share.shape[0] :, :] = tail


def keeper(t):
    return 4 * (1 - t // 2) + t


def moment_kernel(info, arrived, moment, count, tail, came, moment_new, slots, came_kept):
    me = info[0]
    dp = arrived.shape[0]
    _, rows, part = moment.ref.shape
    taps = arrived.shape[1] - 3 * rows
    total = arrived[0].astype(F32)
    for i in range(1, dp):
        total = total + arrived[i].astype(F32)
    size = (came.shape[0] - 32) // 2
    below = tail[16:, :] + came[size + 16 : size + 32, :].astype(F32)
    came_kept.ref[...] = came[...]
    high, low = split(below[:8, :] + below[8:, :])
    rest = jnp.concatenate([total[3 * rows :, :], high.astype(F32), low.astype(F32)], 0).astype(slots.ref.dtype)
    moment, count = moment.ready(), count.ready()
    for which in range(3):
        value = MOMENT_DECAY * moment[which] + total[which * rows : (which + 1) * rows, :] / count[0:1, :]
        moment_new.ref[which] = value
        for z in range(dp // 2):
            slots.ref[8 * z + keeper(which), :rows, :] = value.astype(slots.ref.dtype)
    for t in range(4):
        for z in range(dp // 2):
            slots.ref[8 * z + (keeper(t) ^ 4), : taps + 16, :] = rest
    slots.send()


def output_kernel(info, mine, came, out_mine, delta_own, n_own, inv, middle_own, gains, tail, input_grad, block_out):
    part = mine.shape[1]
    came = came.ready()
    gain = gains.ready()[0:1, block_at(info[0], part)]
    size = mine.shape[0]
    sums = (tail[:16, :] + came[size : size + 16, :].astype(F32)) / (4 * part)
    middle_own = middle_own.ready()
    n_own, inv, delta_own = n_own.ready(), inv.ready(), delta_own.ready()
    for h in range(mine.shape[0] // part):
        r = slice(h * part, (h + 1) * part)
        block_out.ref[r, :] = (middle_own[r, :] + (out_mine[r, :] + came[size + 32 + h * part : size + 32 + (h + 1) * part, :].astype(F32))).astype(BF16)
        column = lambda at: jnp.broadcast_to(sums[at : at + 1, :], (part, part)).T
        total = mine[r, :] + came[r, :].astype(F32)
        back = total * gain - column(h) - n_own[r, :] * column(8 + h)
        input_grad.ref[r, :] = delta_own[r, :].astype(F32) + inv[r, :] * back


def step_kernel(info, got, m0, m1, m2, m3, out, extra, matrix, large, a, p, r, result):
    me, row = info[0], info[2]
    side = row % 2
    size, width = matrix.shape
    rows = r.shape[0] // 2
    part = width // 4
    hidden = m0.ref.shape[1]
    start = pl.multiple_of((row // 2) * (2 * rows), 2 * rows)
    for i in range(extra.shape[0]):
        extra[i] = got[4 * i + me, : extra.shape[1], :].astype(BF16)

    @pl.when(jnp.logical_and(side == 1 - me // 2, me < 3))
    def _():
        for i in range(size // rows):
            for t in range(4):
                matrix[i * rows : (i + 1) * rows, t * part : (t + 1) * part] = got[4 * i + t, :rows, :].astype(BF16)
        result[...] = newton_schulz(matrix[...], a, p, r, start)
        for q in range(8):
            lanes = slice((q % 4) * part, (q % 4 + 1) * part)
            out[q, :, :part] = result[(q // 4) * rows : (q // 4 + 1) * rows, lanes].astype(out.dtype)

    @pl.when(me == side + 1)
    def _():
        for k, piece in enumerate((m0, m1, m2, m3)):
            large[:, block_at(me ^ k, hidden)] = piece.ready()[...]
        steps = newton_schulz(large[...], a, p, r, start)
        for q in range(8):
            lanes = slice((q % 4) * hidden, (q % 4 + 1) * hidden)
            out[q] = steps[(q // 4) * rows : (q // 4 + 1) * rows, lanes].astype(out.dtype)

    @pl.when(me != side + 1)
    def _():
        for piece in (m0, m1, m2, m3):
            piece.ready()


def aside_kernel(info, moment_mine, moment_back, moment_new):
    side = info[2] % 2
    moment_new.ref[side] = moment_mine.ready()[...]
    moment_new.ref[1 - side] = moment_back.ready()[...]


def final_kernel(info, got, extra_mine, extra_came, mixer_weights, mlp_weights, norm_gains, gain_moment, taps, taps_moment, count,
                 mixer_new, mlp_new, gain_moment_new, gains_new, taps_moment_new, taps_new, extra, packed):
    me, row = info[0], info[2]
    side = row % 2
    count = count.ready()
    _, rows, part = mixer_new.ref.shape
    hidden = mlp_new.ref.shape[2]
    width = 4 * part
    for t in range(3):
        old = mixer_weights[t, block_at(row, rows), :].astype(F32)
        mixer_new.ref[t] = old - MATRIX_RATE * got[keeper(t), :rows, :part].astype(F32)
    mixer_new.send()
    rate = MATRIX_RATE * math.sqrt(4 * hidden / width)
    for which in range(2):
        old = mlp_weights[which, block_at(row, rows), :].astype(F32)
        mlp_new.ref[which] = old - rate * got[4 * which + 1 + which, :rows, :].astype(F32)
    mlp_new.send()
    here = side != 1 - me // 2

    @pl.when(here)
    def _():
        extra[...] = extra_mine[...].astype(F32)

    @pl.when(jnp.logical_not(here))
    def _():
        extra[...] = extra_came[...].astype(F32)

    dp, height, _ = extra.shape
    total = taps.shape[0]
    share = -(-total // dp)
    gain = 0.0
    for i in range(dp):
        size = min(share, total - i * share)
        if size > 0:
            packed[i * share : i * share + size, :] = extra[i, :size, :]
        gain = gain + (extra[i, height - 16 : height - 8, :] + extra[i, height - 8 :, :])
    new = MOMENT_DECAY * taps_moment[...] + packed[...] / count[0:1, :]
    taps_moment_new[...] = new
    scale = jnp.sqrt(jnp.mean(new * new, 0, keepdims=True)) + 1e-08
    taps_new[...] = taps[...] - KERNEL_RATE * new / scale
    for which in range(2):
        for t in range(4):
            lanes = slice(t * part, (t + 1) * part)
            gain_moment_new[which : which + 1, lanes] = (
                MOMENT_DECAY * gain_moment[which : which + 1, lanes]
                + gain[4 * which + t : 4 * which + t + 1, :] / count[0:1, :]
            )
    new = gain_moment_new[...]
    scale = jnp.sqrt(jnp.mean(new * new, 1, keepdims=True)) + 1e-08
    gains_new[...] = norm_gains[...] - GAIN_RATE * new / scale


def per_device(
    tokens,
    cotangent,
    lengths,
    norm_gains,
    conv_kernel,
    mixer_weights,
    mlp_weights,
    gain_moment,
    kernel_moment,
    mixer_moment,
    mlp_moment,
):
    _, bucket, part = tokens.shape
    levels, taps, _ = conv_kernel.shape
    hidden = mlp_weights.shape[2]
    me = lax.axis_index("tensor")
    row = lax.axis_index("dp")
    dp = lax.axis_size("dp")
    width = 4 * part
    rows = width // dp
    half = bucket // 4
    piece_type = BF16 if rows % 16 == 0 else F32
    share = -(-levels * taps // dp)
    slot = -(-share // 8) * 8
    slot += (3 * rows + slot) % 16
    forward, inverse, kernel_forward, kernel_inverse = conv_tables(bucket, levels, taps, dp, slot)
    info = jnp.stack([me, lengths[0], row]).astype(jnp.int32)

    x_own, in_weights, in_gains, forward_one, inverse_one, late = fetch(
        info, 1, tokens[0], mixer_weights, norm_gains, forward, inverse, [(cotangent, 0), (mixer_weights, 2)]
    )
    (spec_k,) = call(
        spectrum_kernel,
        [((8 * half, part), F32)],
        [],
        (after(info, x_own), Late(kernel_forward), Late(conv_kernel.reshape(levels * taps, part))),
        2, 10,
    )
    x_pieces = gather_tensor(tokens[0], spec_k, x_own)

    act_like = ((bucket, part), F32)
    wide_like = ((half, width), F32)
    spec_like = ((2 * half, width), F32)
    whole_like = ((bucket, width), BF16)
    quarter_like = ((half, width), BF16)
    x, normed, n_own, inv_one, spec_v, conv, gate_act, gate_slope, branch, gains = call(
        entry_kernel,
        [whole_like, whole_like, Store(*act_like), Store((bucket, 1), F32), spec_like, act_like, act_like, act_like,
         ((bucket, part), BF16), ((2, width), F32)],
        [wide_like, spec_like],
        (info, x_own, *x_pieces[1:], in_weights, in_gains, forward_one, inverse_one, spec_k),
        0, 12,
    )
    late = gather_tensor(late, branch)
    cot, out_weights, delta_active, mlp_kept = call(
        cotangent_kernel,
        [whole_like, ((width, width), BF16), ((bucket, hidden), F32), (mlp_weights.shape, BF16)],
        [],
        (after(info, branch), *late, Late(mlp_weights)),
        3, 5,
    )
    branch_pieces = gather_tensor(branch, delta_active)
    near, kept, normed_two, active, delta_hidden, n_mine, inv_mine, middle_own = call(
        middle_kernel,
        [((width, width), BF16), ((width, width), F32), whole_like, ((bucket, hidden), BF16),
         ((bucket, hidden), BF16), wide_like, ((half, 1), F32), Store(*act_like)],
        [whole_like, ((bucket, width), F32)],
        (info, *branch_pieces, out_weights, x, gains, mlp_kept, delta_active),
        6, 12,
    )
    split_blocks = lambda v: v.reshape(2, -1, v.shape[-1])
    came = swap(split_blocks(near), "tensor", 1)
    mine, far = call(join_kernel, [wide_like, quarter_like], [], (info, split_blocks(kept), came), 1, 4)
    mlp_inputs = (normed_two, active, delta_hidden, cot)
    mlp_send, moment_send = call(
        mlp_away_kernel,
        [((width + 16, hidden), BF16), ((rows, hidden), F32)],
        [],
        (after(info, far), *mlp_inputs, Late(mlp_moment)),
        2, 5,
    )
    (mlp_keep,) = call(
        mlp_here_kernel, [((width + 16, hidden), F32)], [], (after(info, mlp_send), *mlp_inputs), 1000, 8
    )
    mlp_came = swap(mlp_send, "dp", 1)
    moment_came = swap(moment_send, "dp", 1)
    came = swap(far, "tensor", 2)
    delta_mid, grad_gain_two = call(
        norm_back_kernel,
        [quarter_like, ((1, width), F32)],
        [],
        (after(info, mlp_keep), mine, came, cot, n_mine, inv_mine, gains),
        1000, 4,
    )
    (kernel_inverse_one,) = fetch(after(info, delta_mid), 0, kernel_inverse)
    out_near, out_kept = call(
        mlp_out_kernel,
        [Store((2, bucket, part), BF16), Store((2, bucket, part), F32)],
        [((bucket, width), F32)],
        (after(info, kernel_inverse_one), active, mlp_kept),
        1, 8,
    )
    delta_pieces = gather_tensor(delta_mid, kernel_inverse_one, out_near)

    pairs = dp // 2
    parities = [[i for i in range(dp) if i % 2 == y] for y in range(2)]
    groups = [[8 * z + q for q in range(8)] for z in range(pairs)]
    block = (2 * rows + 16, hidden)
    if dp == 8:
        blocks = call(mlp_rows_kernel, [(block, BF16)] * pairs, [], (info, mlp_keep, mlp_came), 0, 6)
        blocks = [blocks[0]] + [swap(blocks[k], "dp", 2 * k) for k in range(1, pairs)]
    else:
        (blocks,) = call(mlp_rows_kernel, [((pairs, *block), BF16)], [], (info, mlp_keep, mlp_came), 0, 6)
        blocks = [lax.all_to_all(blocks, "dp", 0, 0, tiled=True, axis_index_groups=parities)]

    slots, one_near, one_kept, delta_own = call(
        mixer_back_kernel,
        [Store((dp, 3 * rows + slot, part), piece_type), Store((2, bucket + 32, part), BF16),
         Store((2, bucket + 32, part), F32), Store((bucket, part), BF16)],
        [whole_like, wide_like, spec_like, spec_like, ((8 * half, part), F32), ((bucket, 2 * part), BF16),
         ((bucket, width), F32)],
        (after(info, blocks[0]), *delta_pieces, in_weights, gate_act, gate_slope, conv, branch, normed, spec_v, spec_k, forward_one, inverse_one,
         kernel_inverse_one, gains, grad_gain_two),
        1000, 18,
    )
    arrived = lax.all_to_all(slots.astype(BF16), "dp", 0, 0, tiled=True)
    one_mine, one_tail, out_mine, far = call(
        join_late_kernel,
        [act_like, ((32, part), F32), act_like, ((2 * bucket + 32, part), BF16)],
        [],
        (info, Late(one_kept), swap(one_near, "tensor", 1), Late(out_kept), swap(out_near, "tensor", 1)),
        0, 6,
    )
    far_came = swap(far, "tensor", 2)
    pair, moment_mine, moment_other, count = call(
        mlp_moment_kernel,
        [((2 * rows, hidden), BF16), Store((rows, hidden), F32), Store((rows, hidden), F32), Store((8, part), F32)],
        [],
        (info, mlp_moment, moment_came, *blocks),
        1, 8,
    )
    if dp == 8:
        pair_pieces = [pair] + [swap(pair, "dp", 2 * k) for k in range(1, pairs)]
    else:
        pair_pieces = [lax.all_gather(pair, "dp", axis=0, tiled=True, axis_index_groups=parities)]
    height = -(-max(rows, slot + 16) // 16) * 16
    mixer_moment_new, slots, far_kept = call(
        moment_kernel,
        [Store((3, rows, part), F32), Store((4 * dp, height, part), piece_type), Store((2 * bucket + 32, part), BF16)],
        [],
        (info, arrived, Late(mixer_moment), Late(count), one_tail, far_came),
        1000, 8,
    )
    got = lax.all_to_all(slots.astype(BF16), ("dp", "tensor"), 0, 0, tiled=True)
    (mlp_columns,) = call(
        columns_kernel, [((width, hidden), BF16)], [], (after(info, slots), *pair_pieces), 1000, 4
    )
    mlp_pieces = [mlp_columns] + [
        lax.ppermute(
            mlp_columns,
            ("dp", "tensor"),
            [(8 * z + 4 * y + ((1 + y) ^ k), 8 * z + 4 * y + 1 + y) for z in range(pairs) for y in range(2)],
        )
        for k in (1, 2, 3)
    ]
    moment_back = swap(moment_other, "dp", 1)
    input_grad, block_out = call(
        output_kernel,
        [Store(*act_like), Store((bucket, part), BF16)],
        [],
        (after(info, slots), one_mine, Late(far_kept), out_mine, Late(delta_own), Late(n_own), Late(inv_one),
         Late(middle_own), Late(norm_gains), one_tail),
        0, 8,
    )
    (mlp_moment_new,) = call(
        aside_kernel, [Store((2, rows, hidden), F32)], [], (after(info, slots), Late(moment_mine), Late(moment_back)), 1, 4
    )
    square = ((width, width), F32)
    sends, extra = call(
        step_kernel,
        [((8, rows, hidden), piece_type), ((dp, slot + 16, part), BF16)],
        [((width, width), BF16), ((width, 4 * hidden), BF16), square, square, ((2 * rows, width), F32),
         ((2 * rows, width), F32)],
        (after(info, block_out, mlp_moment_new), got, *(Late(v) for v in mlp_pieces)),
        18, 24,
    )
    got = lax.all_to_all(sends.astype(BF16), ("dp", "tensor"), 0, 0, tiled=True, axis_index_groups=groups)
    extra_came = swap(extra, "dp", 1)
    flat = (levels * taps, part)
    old = fetch(
        after(info, extra), 0, mixer_weights, mlp_weights, norm_gains, gain_moment, conv_kernel.reshape(flat),
        kernel_moment.reshape(flat),
    )
    mixer_new, mlp_new, gain_moment_new, gains_new, kernel_moment_new, kernel_new = call(
        final_kernel,
        [Store((3, rows, part), F32), Store((2, rows, hidden), F32), ((2, width), F32), ((2, width), F32), (flat, F32),
         (flat, F32)],
        [((dp, slot + 16, part), F32), (flat, F32)],
        (info, got.astype(piece_type), extra, extra_came, *old, Late(count)),
        0, 8,
    )
    kernel_moment_new, kernel_new = (v.reshape(conv_kernel.shape) for v in (kernel_moment_new, kernel_new))
    return (
        block_out[None],
        input_grad[None],
        gain_moment_new,
        gains_new,
        kernel_moment_new,
        kernel_new,
        mixer_moment_new,
        mixer_new,
        mlp_moment_new,
        mlp_new,
    )


def solution(mesh):
    tokens = P("dp", None, "tensor")
    columns = P(None, None, "tensor")
    blocks = P(None, "dp", "tensor")
    return jax.shard_map(
        per_device,
        mesh=mesh,
        in_specs=(tokens, tokens, P("dp"), P(), columns, columns, columns, P(), columns, blocks, blocks),
        out_specs=(tokens, tokens, P(), P(), columns, columns, blocks, blocks, blocks, blocks),
        check_vma=False,
    )
```

```python
import functools
import math

import jax
import jax.numpy as jnp
import ml_dtypes
import numpy as np
from jax import lax
from jax.experimental import pallas as pl
from jax.experimental.pallas import tpu as pltpu
from jax.sharding import PartitionSpec as P

NS_STEPS = 5
EPSILON = 1e-05
NS_COEF_A = 3.4445
NS_COEF_B = -4.775
NS_COEF_C = 2.0315
MOMENT_DECAY = 0.5
MATRIX_RATE = 1.0
GAIN_RATE = 0.1
KERNEL_RATE = 0.125
SCALE = 10**10
BF16 = jnp.bfloat16
F32 = jnp.float32


def conv_tables(bucket, levels, taps, dp, slot):
    half = bucket // 4
    size = 2 * half
    t = np.arange(half)
    k = np.arange(half)
    phase = 2 * np.pi * ((k[:, None] * t[None, :]) % size) / size
    forward = np.concatenate([np.cos(phase), -np.sin(phase)], 0)
    forward[half] = (-1.0) ** t
    scale = np.full((half,), 2.0 / size)
    scale[0] = 1.0 / size
    inverse = np.concatenate(
        [np.cos(phase).T * scale[None, :], -np.sin(phase).T * scale[None, :]], 1
    )
    inverse[:, half] = ((-1.0) ** t) / size
    spread = np.zeros((bucket, levels * taps))
    at = 0
    for level in range(levels):
        for tap in range(taps):
            width = 2**level
            spread[at : at + width, level * taps + tap] = 0.5**level
            at += width
    kernel_forward = np.concatenate(
        [forward @ spread[m * half : (m + 1) * half] for m in range(4)], 0
    )
    kernel_inverse = np.concatenate(
        [spread[m * half : (m + 1) * half].T @ inverse for m in range(4)], 1
    )
    share = -(-levels * taps // dp)
    kernel_inverse = np.pad(kernel_inverse, ((0, dp * share - levels * taps), (0, 0)))
    kernel_inverse = kernel_inverse.reshape(dp, share, -1)
    kernel_inverse = np.pad(kernel_inverse, ((0, 0), (0, slot - share), (0, 0))).reshape(dp * slot, -1)
    tables = []
    for table in (forward, inverse, kernel_forward, kernel_inverse):
        high = table.astype(ml_dtypes.bfloat16)
        low = (table - high.astype(np.float64)).astype(ml_dtypes.bfloat16)
        tables.append(np.stack([high, low]))
    return tables


def cross(a, b):
    return a[0] * b[0] - a[1] * b[1], a[0] * b[1] + a[1] * b[2]


def cross_conj(a, b):
    return a[0] * b[0] + a[1] * b[1], a[1] * b[2] - a[0] * b[1]


def with_edge(spec, first):
    real, imag = spec
    return real, jnp.where(first, 0.0, imag), jnp.where(first, imag, real)


def add_pairs(pairs):
    return functools.reduce(lambda p, q: (p[0] + q[0], p[1] + q[1]), pairs)


def spectral_blocks(left, right, conj, store):
    for step in range(4):
        rows = step * 64
        index = lax.broadcasted_iota(jnp.int32, (64, 128), 0)
        first = index + rows == 0
        sign = 1.0 - 2.0 * (index % 2).astype(F32)
        a = [left(r, rows) for r in range(4)]
        b = [with_edge(right(m, rows), first) for m in range(4)]
        if conj:
            sums = [add_pairs([cross_conj(a[r], b[r - q]) for r in range(q, 4)]) for q in range(4)]
        else:
            sums = [add_pairs([cross(a[r], b[q - r]) for r in range(q + 1)]) for q in range(4)]
        for q in range(4):
            other = q + 1 if conj else q - 1
            if 0 <= other < 4:
                real = sums[q][0] + sign * sums[other][0]
                imag = sums[q][1] + sign * sums[other][1]
            else:
                real, imag = sums[q]
            store(q, rows, real, imag)


def lane_pair(ref, half):
    return lambda r, rows: (
        ref[rows : rows + 64, r * 128 : (r + 1) * 128],
        ref[half + rows : half + rows + 64, r * 128 : (r + 1) * 128],
    )


def row_pair(ref, half):
    return lambda r, rows: (
        ref[2 * half * r + rows : 2 * half * r + rows + 64, :],
        ref[2 * half * r + half + rows : 2 * half * r + half + rows + 64, :],
    )


def gelu_both(x):
    c = math.sqrt(2.0 / math.pi)
    t = jnp.tanh(c * (x + 0.044715 * x * x * x))
    value = 0.5 * x * (1.0 + t)
    slope = 0.5 * (1.0 + t) + 0.5 * x * (1.0 - t * t) * (c * (1.0 + 3 * 0.044715 * x * x))
    return value, slope


def after(value, *others):
    return lax.optimization_barrier((value, *others))[0]


def swap(value, axis, k):
    size = lax.axis_size(axis)
    return lax.ppermute(value, axis, [(i, i ^ k) for i in range(size)])


def gather_tensor(value, *meanwhile):
    far = swap(value, "tensor", 2)
    near = swap(value, "tensor", 1)
    if meanwhile:
        far = after(far, *meanwhile)
    far_near = swap(far, "tensor", 1)
    return [value, near, far, far_near]


def gather_dp(value, me, low=0):
    size = lax.axis_size("dp")
    whole = value[None]
    while (1 << low) < size:
        bits = min(3, size.bit_length() - 1 - low)
        mine = (me >> low) & ((1 << bits) - 1)
        out = jnp.zeros((1 << bits,) + whole.shape, whole.dtype)
        for k in range(1 << bits):
            piece = whole if k == 0 else swap(whole, "dp", k << low)
            out = lax.dynamic_update_index_in_dim(out, piece, mine ^ k, 0)
        whole = out.reshape((-1,) + value.shape)
        low += bits
    return whole


def dot(a, b, contract):
    return lax.dot_general(a, b, ((contract[0], contract[1]), ((), ())), preferred_element_type=F32)


NN = ((1,), (0,))
NT = ((1,), (1,))
TN = ((0,), (0,))


def split(value):
    high = value.astype(BF16)
    return high, (value - high.astype(F32)).astype(BF16)


def table_dot(table, value):
    high, low = split(value)
    return dot(table[0], high, NN) + (dot(table[1], high, NN) + dot(table[0], low, NN))


def symmetric(left, right, product):
    half = left[0].shape[0] // 2
    top = product([v[:half] for v in left], right, None)
    low = product([v[half:] for v in left], right, half)
    return jnp.concatenate([top, jnp.concatenate([top[:, half:].T, low], 1)], 0)


def three_terms(left, right, cut=None):
    right = right if cut is None else [v[:, cut:] for v in right]
    left = jnp.concatenate([left[0], left[0], left[1]], 1)
    return dot(left, jnp.concatenate([right[0], right[1], right[0]], 0), NN)


def newton_schulz(blocks, a_ref, p_ref, r_ref, start):
    size = a_ref.shape[0]
    row = lax.broadcasted_iota(jnp.int32, (size, size), 0)
    col = lax.broadcasted_iota(jnp.int32, (size, size), 1)
    unit = (row == col).astype(F32)
    blocks = [block() for block in blocks]
    gram = 0.0
    for block in blocks:
        gram = gram + symmetric([block], [block], lambda a, b, cut: dot(a[0], b[0] if cut is None else b[0][cut:], NT))
    scale = 1.0 / (jnp.sqrt(jnp.sum(gram * unit)) + 1e-07)
    a_ref[...] = gram * (scale * scale)

    def advance(first):
        a = a_ref[...]
        terms = split(a)
        poly = NS_COEF_A * unit + NS_COEF_B * a + NS_COEF_C * symmetric(terms, terms, three_terms)
        poly_terms = split(poly)
        if first:
            p_ref[...] = poly
            r_ref[...] = p_ref[pl.ds(start, r_ref.shape[0]), :]
        else:
            r_ref[...] = three_terms(split(r_ref[...]), poly_terms)
        half = symmetric(terms, poly_terms, three_terms)
        a_ref[...] = symmetric(poly_terms, split(half), three_terms)

    advance(True)
    pl.loop(0, NS_STEPS - 2)(lambda _: advance(False))
    rows, terms = r_ref[...], split(a_ref[...])
    once = three_terms(split(rows), terms)
    rows = NS_COEF_A * rows + NS_COEF_B * once + NS_COEF_C * three_terms(split(once), terms)
    high, low = split(rows)
    return [scale * (dot(high, block, NN) + dot(low, block, NN)) for block in blocks]


VMEM = pl.BlockSpec(memory_space=pltpu.VMEM)
SMEM = pl.BlockSpec(memory_space=pltpu.SMEM)


HBM = pl.BlockSpec(memory_space=pltpu.HBM)


class Late:
    def __init__(self, array):
        self.shape, self.dtype = array.shape, array.dtype
        self.array = pltpu.with_memory_space_constraint(array, pltpu.HBM)


class Store:
    def __init__(self, shape, dtype, own=False):
        self.shape, self.dtype, self.own = shape, dtype, own


class Waiting:
    def __init__(self, copy, ref):
        self.copy, self.ref, self.started = copy, ref, False

    def ready(self):
        self.copy.wait()
        return self.ref

    def send(self):
        self.copy.start()
        self.started = True


def call(kernel, outs, scratch, args, time, limit):
    outs = [o if isinstance(o, Store) else jax.ShapeDtypeStruct(*o) for o in outs]
    late = [a for a in (*args, *outs) if isinstance(a, (Late, Store))]
    n_in, n_out = len(args), len(outs)

    def body(*refs):
        given, rest = refs[: n_in + n_out], refs[n_in + n_out :]
        buffers, rest = rest[: len(late)], rest[len(late) :]
        semaphores = rest[-1] if late else None
        passed, stores, at = [], [], 0
        for what, ref in zip((*args, *outs), given):
            if isinstance(what, Late):
                copy = pltpu.make_async_copy(ref, buffers[at], semaphores.at[at])
                copy.start()
            elif isinstance(what, Store):
                copy = pltpu.make_async_copy(buffers[at], ref, semaphores.at[at])
            else:
                passed.append(ref)
                continue
            passed.append(Waiting(copy, buffers[at]))
            if isinstance(what, Store) and not what.own:
                stores.append(passed[-1])
            at += 1
        kernel(*passed, *(rest[:-1] if late else rest))
        for store in stores:
            if not store.started:
                store.send()
        for store in stores:
            store.copy.wait()

    return pl.pallas_call(
        body,
        out_shape=tuple(pltpu.HBM(o.shape, o.dtype) if isinstance(o, Store) else o for o in outs),
        in_specs=[SMEM] + [HBM if isinstance(a, Late) else VMEM for a in args[1:]],
        out_specs=tuple(HBM if isinstance(o, Store) else VMEM for o in outs),
        scratch_shapes=[pltpu.VMEM(a.shape, a.dtype) for a in late]
        + [pltpu.VMEM(shape, dtype) for shape, dtype in scratch]
        + ([pltpu.SemaphoreType.DMA((len(late),))] if late else []),
        compiler_params=pltpu.CompilerParams(vmem_limit_bytes=limit * 2**20),
        cost_estimate=pl.CostEstimate(flops=max(time * SCALE, 10**6), bytes_accessed=0, transcendentals=0),
    )(*(a.array if isinstance(a, Late) else a for a in args))


def fetch(token, time, *arrays):
    arrays = [a if isinstance(a, list) else [(a, None)] for a in arrays]
    shapes = []
    for a in arrays:
        cuts = [p.shape if index is None else p.shape[1:] for p, index in a]
        shapes.append(jax.ShapeDtypeStruct((sum(c[0] for c in cuts), *cuts[0][1:]), a[0][0].dtype))
    flat = [pltpu.with_memory_space_constraint(p, pltpu.HBM) for a in arrays for p, _ in a]

    def body(token_ref, *refs):
        outs, semaphores, copies, at = refs[len(flat) : -1], refs[-1], [], 0
        for a, out in zip(arrays, outs):
            row = 0
            for _, index in a:
                source = refs[at] if index is None else refs[at].at[index]
                target = out if len(a) == 1 else out.at[row : row + source.shape[0]]
                copies.append(pltpu.make_async_copy(source, target, semaphores.at[at]))
                copies[-1].start()
                row, at = row + source.shape[0], at + 1
        for copy in copies:
            copy.wait()

    return pl.pallas_call(
        body,
        out_shape=tuple(shapes),
        in_specs=[SMEM] + [HBM] * len(flat),
        out_specs=(VMEM,) * len(shapes),
        scratch_shapes=[pltpu.SemaphoreType.DMA((len(flat),))],
        compiler_params=pltpu.CompilerParams(vmem_limit_bytes=2 * 2**20),
        cost_estimate=pl.CostEstimate(flops=max(time * SCALE, 10**6), bytes_accessed=0, transcendentals=0),
    )(token, *flat)


def block_at(index, size):
    return pl.ds(pl.multiple_of(index * size, size), size)


def row_mask(info, start, rows):
    return (start + lax.broadcasted_iota(jnp.int32, (rows, 1), 0) < info[1]).astype(F32)


def spectrum_kernel(info, table, taps, spec_k):
    taps = taps.ready()[...]
    spec_k[...] = table_dot(table.ready(), taps)


def entry_kernel(info, p0, p1, p2, p3, weights, gains, forward, inverse, spec_k,
                 x, normed, n_own, inv, spec_v, conv, act, slope, branch, gains_kept, wide, spec_y):
    me = info[0]
    part = p1.shape[1]
    for k, piece in enumerate((p0, p1, p2, p3)):
        x[:, block_at(me ^ k, part)] = piece[...]
    gains_kept[...] = gains[...]
    gain = gains[0:1, :]
    half = x.shape[0] // 4
    for c in range(4):
        r = slice(c * half, (c + 1) * half)
        v = x[r, :].astype(F32)
        mean = jnp.mean(v, 1, keepdims=True)
        centred = v - mean
        scale = lax.rsqrt(jnp.mean(centred * centred, 1, keepdims=True) + EPSILON)
        normed[r, :] = (centred * scale * gain).astype(BF16)
        inv.ref[r, :] = scale
        n_own.ref[r, :] = (p0[r, :].astype(F32) - mean) * scale
    n_own.send()
    inv.send()
    for c in range(4):
        r = slice(c * half, (c + 1) * half)
        normal = normed[r, :]
        wide[:, c * part : (c + 1) * part] = dot(normal, weights[0], NN)
        act[r, :], slope[r, :] = gelu_both(dot(normal, weights[1], NN))
    spec_v[...] = table_dot(forward, wide[...])

    def store(q, rows, real, imag):
        spec_y[rows : rows + 64, q * part : (q + 1) * part] = real
        spec_y[half + rows : half + rows + 64, q * part : (q + 1) * part] = imag

    spectral_blocks(lane_pair(spec_v, half), row_pair(spec_k, half), False, store)
    wide[...] = table_dot(inverse, spec_y[...])
    for c in range(4):
        r = slice(c * half, (c + 1) * half)
        out = wide[:, c * part : (c + 1) * part]
        conv[r, :] = out
        out = (act[r, :] * out * row_mask(info, c * half, half)).astype(BF16)
        branch[r, :] = out


def cotangent_kernel(info, p0, p1, p2, p3, weights, cot, out_w, delta, weights_kept):
    part = p0.shape[1]
    for k, piece in enumerate((p0, p1, p2, p3)):
        cot[:, block_at(info[0] ^ k, part)] = piece[: cot.shape[0], :]
        out_w[:, block_at(info[0] ^ k, part)] = piece[cot.shape[0] :, :]
    step = cot.shape[0] // 4
    weights = weights.ready()
    weights_kept[...] = weights[...]
    for c in range(4):
        r = slice(c * step, (c + 1) * step)
        delta[r, :] = dot(cot[r, :], weights[1], NN)


def middle_kernel(info, b0, b1, b2, b3, out_w, x, gains, weights, delta_active,
                  near, kept, normed, active, delta_hidden, n_mine, inv_mine, middle_own, branch, middle):
    me = info[0]
    part = b0.shape[1]
    step = x.shape[0] // 4
    for k, piece in enumerate((b0, b1, b2, b3)):
        branch[:, block_at(me ^ k, part)] = piece[...]
    gain = gains[1:2, :]
    for k in (1, 3, 0, 2):
        block = me ^ k
        r = block_at(block, step)
        mid = x[r, :].astype(F32) + dot(branch[r, :], out_w[...], NT)
        middle[r, :] = mid
        centred = mid - jnp.mean(mid, 1, keepdims=True)
        scale = lax.rsqrt(jnp.mean(centred * centred, 1, keepdims=True) + EPSILON)
        normal = centred * scale
        if k == 0:
            n_mine[...] = normal
            inv_mine[...] = scale
        normal = (normal * gain).astype(BF16)
        normed[r, :] = normal
        value, slope = gelu_both(dot(normal, weights[0], NN))
        mask = row_mask(info, block * step, step)
        active[r, :] = (value * mask).astype(BF16)
        back = (delta_active[r, :] * mask * slope).astype(BF16)
        delta_hidden[r, :] = back
        share = dot(back, weights[0], NT)
        if k % 2:
            near[(k // 2) * step : (k // 2 + 1) * step, :] = share.astype(BF16)
        else:
            kept[(k // 2) * step : (k // 2 + 1) * step, :] = share
    middle_own.ref[...] = middle[:, block_at(me, part)]


def mlp_kernel(info, normed, active, delta_hidden, cot, moment, out, moment_send, away):
    size = normed.shape[1]
    wanted = (info[2] + away) % 2

    @pl.when(wanted == 0)
    def _():
        out[:size, :] = dot(normed[...], delta_hidden[...], TN).astype(out.dtype)

    @pl.when(wanted == 1)
    def _():
        out[:size, :] = dot(cot[...], active[...], TN).astype(out.dtype)

    length = jnp.full((16, out.shape[1]), 1, jnp.int32) * info[1]
    first = lax.broadcasted_iota(jnp.int32, length.shape, 0) == 0
    out[size:, :] = jnp.where(first, length // 32, length % 32).astype(F32).astype(out.dtype)
    if away:
        moment_send[...] = moment.ready()[wanted]


def mlp_away_kernel(info, normed, active, delta_hidden, cot, moment, out, moment_send):
    mlp_kernel(info, normed, active, delta_hidden, cot, moment, out, moment_send, 1)


def mlp_here_kernel(info, normed, active, delta_hidden, cot, out):
    mlp_kernel(info, normed, active, delta_hidden, cot, None, out, None, 0)


def mlp_out_kernel(info, active, weights, near, kept, part_out):
    me = info[0]
    step = active.shape[0] // 4
    part = near.ref.shape[2]
    for c in range(4):
        r = slice(c * step, (c + 1) * step)
        part_out[r, :] = dot(active[r, :], weights[1], NT)
    for k in range(4):
        share = part_out[:, block_at(me ^ k, part)]
        if k % 2:
            near.ref[k // 2] = share.astype(BF16)
        else:
            kept.ref[k // 2] = share


def mlp_rows_kernel(info, keep, came, *outs):
    size = came.shape[0] - 16
    pairs = outs[0].shape[0] if len(outs) == 1 else len(outs)
    rows = size // pairs
    length = keep[size:, :] + came[size:, :].astype(F32)
    for k in range(pairs):
        if len(outs) == 1:
            r, out = pl.ds(k * rows, rows), outs[0].at[k]
        else:
            r, out = block_at((info[2] // 2) ^ k, rows), outs[k]
        out[:rows, :] = (keep[r, :] + came[r, :].astype(F32)).astype(out.dtype)
        out[rows:, :] = length.astype(out.dtype)


def mlp_moment_kernel(info, moment, other_moment, *refs):
    *pieces, matrix, mine, other, count = refs
    rows = moment.shape[1]
    side = info[2] % 2
    if len(pieces) == 1:
        pieces = [pieces[0].at[k] for k in range(pieces[0].shape[0])]
    total = pieces[0][...].astype(F32)
    for piece in pieces[1:]:
        total = total + piece[...].astype(F32)
    tokens = 32.0 * total[2 * rows : 2 * rows + 1, :] + total[2 * rows + 1 : 2 * rows + 2, :]
    count.ref[...] = jnp.broadcast_to(tokens[:, : count.ref.shape[1]], count.ref.shape)
    old = moment[side]
    for which in range(2):
        new = total[which * rows : (which + 1) * rows, :] / tokens

        @pl.when(side == which)
        def _(new=new, which=which):
            now = MOMENT_DECAY * old + new
            mine.ref[...] = now
            matrix[which * rows : (which + 1) * rows, :] = now.astype(matrix.dtype)

        @pl.when(side != which)
        def _(new=new, which=which):
            now = MOMENT_DECAY * other_moment[...] + new
            other.ref[...] = now
            matrix[which * rows : (which + 1) * rows, :] = now.astype(matrix.dtype)


def columns_kernel(info, *refs):
    *pieces, out = refs
    rows = pieces[0].shape[0]
    for k, piece in enumerate(pieces):
        out[block_at((info[2] // 2) ^ k, rows), :] = piece[...]


def join_kernel(info, kept, came, mine, far):
    mine[...] = kept[0] + came[0].astype(F32)
    far[...] = (kept[1] + came[1].astype(F32)).astype(BF16)


def join_late_kernel(info, one_kept, one_came, out_kept, out_came, one_mine, tail, out_mine, far):
    one_kept, out_kept = one_kept.ready(), out_kept.ready()
    size = out_mine.shape[0]
    one_mine[...] = one_kept[0, :size, :] + one_came[0, :size, :].astype(F32)
    far[:size, :] = (one_kept[1, :size, :] + one_came[1, :size, :].astype(F32)).astype(BF16)
    below = one_kept[0, size:, :] + one_came[0, size:, :].astype(F32)
    high, low = split(below[16:24, :] + below[24:, :])
    below = jnp.concatenate([below[:16, :], high.astype(F32), low.astype(F32)], 0)
    tail[...] = below
    far[size : size + 32, :] = below.astype(BF16)
    out_mine[...] = out_kept[0] + out_came[0].astype(F32)
    far[size + 32 :, :] = (out_kept[1] + out_came[1].astype(F32)).astype(BF16)


def norm_back_kernel(info, mine, came, cot, n_mine, inv_mine, gains, delta, grad_gain):
    size = mine.shape[0]
    total = mine[...] + came[...].astype(F32)
    n = n_mine[...]
    q = total * gains[1:2, :]
    back = inv_mine[...] * (q - jnp.mean(q, 1, keepdims=True) - n * jnp.mean(q * n, 1, keepdims=True))
    delta[...] = (cot[block_at(info[0], size), :].astype(F32) + back).astype(BF16)
    grad_gain[...] = jnp.sum(total * n, 0, keepdims=True)


def mixer_back_kernel(info, d0, d1, d2, d3, weights, act, slope, conv, branch, normed, spec_v, spec_k, forward, inverse,
                      kernel_inverse, gains, gain_two,
                      slots, near, kept, delta_own,
                      delta, wide, spec_d, spec_y, spec_u, back, share):
    me = info[0]
    step, width = d0.shape
    part = slots.ref.shape[2]
    half = step
    for k, piece in enumerate((d0, d1, d2, d3)):
        block = me ^ k
        r = block_at(block, step)
        delta[r, :] = piece[...]
        down = dot(piece[...], weights[2], NN) * row_mask(info, block * step, step)
        back[r, part:] = (down * conv[r, :] * slope[r, :]).astype(BF16)
        wide[:, block_at(block, part)] = down * act[r, :]
    delta_own.ref[...] = delta[:, block_at(me, part)]
    delta_own.send()
    spec_d[...] = table_dot(forward, wide[...])

    def store(q, rows, real, imag):
        spec_y[rows : rows + 64, q * part : (q + 1) * part] = real
        spec_y[half + rows : half + rows + 64, q * part : (q + 1) * part] = imag

    def store_rows(q, rows, real, imag):
        spec_u[2 * half * q + rows : 2 * half * q + rows + 64, :] = real
        spec_u[2 * half * q + half + rows : 2 * half * q + half + rows + 64, :] = imag

    spectral_blocks(lane_pair(spec_d, half), row_pair(spec_k, half), True, store)
    wide[...] = table_dot(inverse, spec_y[...])
    for c in range(4):
        back[c * half : (c + 1) * half, :part] = wide[:, c * part : (c + 1) * part].astype(BF16)
    spectral_blocks(lane_pair(spec_d, half), lane_pair(spec_v, half), True, store_rows)
    grad_kernel = table_dot(kernel_inverse, spec_u[...])
    grads = dot(normed[...], back[...], TN)
    grad_out = dot(delta[...], branch[...], TN)
    dp = slots.ref.shape[0]
    rows = width // dp
    taps = grad_kernel.shape[0] // dp
    for i in range(dp):
        r = slice(i * rows, (i + 1) * rows)
        slots.ref[i, :rows, :] = grads[r, :part].astype(slots.ref.dtype)
        slots.ref[i, rows : 2 * rows, :] = grads[r, part:].astype(slots.ref.dtype)
        slots.ref[i, 2 * rows : 3 * rows, :] = grad_out[r, :].astype(slots.ref.dtype)
        slots.ref[i, 3 * rows :, :] = grad_kernel[i * taps : (i + 1) * taps, :].astype(slots.ref.dtype)
    slots.send()
    ones = jnp.ones((8, width), BF16)
    gain_one = jnp.zeros((1, width), F32)
    sums = [[], []]
    gain = jnp.broadcast_to(gains[0:1, :], (8, width)).astype(BF16)
    for c in range(4):
        r = slice(c * step, (c + 1) * step)
        out = dot(back[r, :part], weights[0], NT) + dot(back[r, part:], weights[1], NT)
        share[r, :] = out
        first = dot(gain, out.astype(BF16), NT)
        both = out * normed[r, :].astype(F32)
        gain_one = gain_one + jnp.sum(both, 0, keepdims=True)
        second = dot(ones, both.astype(BF16), NT)
        for h in range(step // part):
            sums[0].append(first[0:1, h * part : (h + 1) * part])
            sums[1].append(second[0:1, h * part : (h + 1) * part])
    gain_one = gain_one / gains[0:1, :]
    gain = [g[:, q * part : (q + 1) * part] for g in (gain_one, gain_two[...]) for q in range(4)]
    gain_high, gain_low = split(jnp.concatenate(gain, 0))
    tail = jnp.concatenate([*sums[0], *sums[1], gain_high.astype(F32), gain_low.astype(F32)], 0)
    for k in range(4):
        block = share[:, block_at(me ^ k, part)]
        if k % 2:
            near.ref[k // 2, : share.shape[0], :] = block.astype(BF16)
            near.ref[k // 2, share.shape[0] :, :] = tail.astype(BF16)
        else:
            kept.ref[k // 2, : share.shape[0], :] = block
            kept.ref[k // 2, share.shape[0] :, :] = tail


def keeper(t):
    return 4 * (1 - t // 2) + t


def moment_kernel(info, arrived, moment, count, tail, came, moment_new, slots, came_kept):
    me = info[0]
    dp = arrived.shape[0]
    _, rows, part = moment.ref.shape
    taps = arrived.shape[1] - 3 * rows
    total = arrived[0].astype(F32)
    for i in range(1, dp):
        total = total + arrived[i].astype(F32)
    size = (came.shape[0] - 32) // 2
    below = tail[16:, :] + came[size + 16 : size + 32, :].astype(F32)
    came_kept.ref[...] = came[...]
    high, low = split(below[:8, :] + below[8:, :])
    rest = jnp.concatenate([total[3 * rows :, :], high.astype(F32), low.astype(F32)], 0).astype(slots.ref.dtype)
    moment, count = moment.ready(), count.ready()
    for which in range(3):
        value = MOMENT_DECAY * moment[which] + total[which * rows : (which + 1) * rows, :] / count[0:1, :]
        moment_new.ref[which] = value
        for z in range(dp // 2):
            slots.ref[8 * z + keeper(which), :rows, :] = value.astype(slots.ref.dtype)
    for t in range(4):
        for z in range(dp // 2):
            slots.ref[8 * z + (keeper(t) ^ 4), : taps + 16, :] = rest
            if t == 3:
                slots.ref[8 * z + keeper(t), : taps + 16, :] = rest
    slots.send()


def output_kernel(info, mine, came, out_mine, delta_own, n_own, inv, middle_own, gains, tail, input_grad, block_out):
    part = mine.shape[1]
    came = came.ready()
    gain = gains.ready()[0:1, block_at(info[0], part)]
    size = mine.shape[0]
    sums = (tail[:16, :] + came[size : size + 16, :].astype(F32)) / (4 * part)
    middle_own = middle_own.ready()
    n_own, inv, delta_own = n_own.ready(), inv.ready(), delta_own.ready()
    for h in range(mine.shape[0] // part):
        r = slice(h * part, (h + 1) * part)
        block_out.ref[r, :] = (middle_own[r, :] + (out_mine[r, :] + came[size + 32 + h * part : size + 32 + (h + 1) * part, :].astype(F32))).astype(BF16)
        column = lambda at: jnp.broadcast_to(sums[at : at + 1, :], (part, part)).T
        total = mine[r, :] + came[r, :].astype(F32)
        back = total * gain - column(h) - n_own[r, :] * column(8 + h)
        input_grad.ref[r, :] = delta_own[r, :].astype(F32) + inv[r, :] * back


def large_kernel(info, m0, m1, m2, m3, out, a, p, r):
    me, row = info[0], info[2]
    rows = r.shape[0] // 2

    @pl.when(me == 3)
    def _():
        start = pl.multiple_of((row // 2) * (2 * rows), 2 * rows)
        blocks = [lambda piece=piece: piece[...] for piece in (m0, m1, m2, m3)]
        for k, steps in enumerate(newton_schulz(blocks, a, p, r, start)):
            for y in range(2):
                out.ref[4 * y + (3 ^ k), :rows, :] = steps[y * rows : (y + 1) * rows, :].astype(out.ref.dtype)
        out.send()
        out.copy.wait()


def gather_extra(got, me, rows, packed, extra):
    total, dp = packed.shape[0], got.shape[0] // 4
    part = packed.shape[1]
    share = -(-total // dp)
    taps = -(-share // 8) * 8
    taps += (3 * rows + taps) % 16
    gain = 0.0
    for i in range(dp):
        both = got[4 * i + me, : taps + 16, :].astype(F32)
        count = min(share, total - i * share)
        if count > 0:
            packed[i * share : i * share + count, :] = both[:count, :]
        gain = gain + (both[taps : taps + 8, :] + both[taps + 8 :, :])
    high, low = split(gain)
    extra[...] = jnp.zeros_like(extra)
    for g in range(-(-total // 64)):
        count = min(64, total - 64 * g)
        extra[:count, g * part : (g + 1) * part] = packed[64 * g : 64 * g + count, :].astype(extra.dtype)
    at = (total // 64) * part
    extra[32:48, at : at + part] = jnp.concatenate([high.astype(F32), low.astype(F32)], 0).astype(extra.dtype)


def small_kernel(info, source, slots, out, got, extra, matrix, a, p, r, packed, steps, semaphore):
    me, row = info[0], info[2]
    side = row % 2
    size, width = matrix.shape
    rows = r.shape[0] // 2
    part = width // 4
    start = pl.multiple_of((row // 2) * (2 * rows), 2 * rows)
    keeps = jnp.logical_and(side == 1 - me // 2, me < 3)

    @pl.when(me < 3)
    def _():
        arrive = pltpu.make_async_copy(source, got, semaphore.at[2])
        arrive.start()
        arrive.wait()

        @pl.when(keeps)
        def _():
            for i in range(size // rows):
                for t in range(4):
                    matrix[i * rows : (i + 1) * rows, t * part : (t + 1) * part] = got[4 * i + t, :rows, :].astype(BF16)
            (result,) = newton_schulz([lambda: matrix[...]], a, p, r, start)
            for q in range(8):
                lanes = slice((q % 4) * part, (q % 4 + 1) * part)
                steps[q] = result[(q // 4) * rows : (q // 4 + 1) * rows, lanes].astype(steps.dtype)
            copy = pltpu.make_async_copy(steps, out.at[:, pl.ds(0, rows), pl.ds(0, part)], semaphore.at[0])
            copy.start()
            copy.wait()

        @pl.when(jnp.logical_not(keeps))
        def _():
            gather_extra(got, me, rows, packed, extra)
            copies = [
                pltpu.make_async_copy(extra, out.at[4 * y + me, pl.ds(0, 64), pl.ds(0, 3 * part)], semaphore.at[y])
                for y in range(2)
            ]
            for copy in copies:
                copy.start()
            for copy in copies:
                copy.wait()


def small_steps(info, got, slots, rows, width, taps):
    part = width // 4
    square = pltpu.VMEM((width, width), F32)
    return pl.pallas_call(
        small_kernel,
        out_shape=pltpu.HBM(slots.shape, slots.dtype),
        in_specs=[SMEM, HBM, HBM],
        out_specs=HBM,
        scratch_shapes=[
            pltpu.VMEM(got.shape, got.dtype), pltpu.VMEM((64, 3 * part), slots.dtype), pltpu.VMEM((width, width), BF16), square,
            square, pltpu.VMEM((2 * rows, width), F32), pltpu.VMEM((taps, part), F32), pltpu.VMEM((8, rows, part), slots.dtype),
            pltpu.SemaphoreType.DMA((3,)),
        ],
        input_output_aliases={2: 0},
        compiler_params=pltpu.CompilerParams(vmem_limit_bytes=24 * 2**20),
        cost_estimate=pl.CostEstimate(flops=18 * SCALE, bytes_accessed=0, transcendentals=0),
    )(info, pltpu.with_memory_space_constraint(got, pltpu.HBM), pltpu.with_memory_space_constraint(slots, pltpu.HBM))


def extra_kernel(rows, info, got, extra, packed):
    gather_extra(got.ready(), info[0], rows, packed, extra)


def aside_kernel(info, moment_mine, moment_back, moment_new):
    side = info[2] % 2
    moment_new.ref[side] = moment_mine.ready()[...]
    moment_new.ref[1 - side] = moment_back.ready()[...]


def final_kernel(info, got, extra_mine, mixer_weights, mlp_weights, norm_gains, gain_moment, taps, taps_moment, count,
                 mixer_new, mlp_new, gain_moment_new, gains_new, taps_moment_new, taps_new, extra):
    me, row = info[0], info[2]
    count = count.ready()
    _, rows, part = mixer_new.ref.shape
    hidden = mlp_new.ref.shape[2]
    width = 4 * part
    for t in range(3):
        old = mixer_weights[t, block_at(row, rows), :].astype(F32)
        mixer_new.ref[t] = old - MATRIX_RATE * got[keeper(t), :rows, :part].astype(F32)
    mixer_new.send()
    rate = MATRIX_RATE * math.sqrt(4 * hidden / width)
    for which in range(2):
        old = mlp_weights[which, block_at(row, rows), :].astype(F32)
        mlp_new.ref[which] = old - rate * got[4 * which + 3, :rows, :].astype(F32)
    mlp_new.send()
    @pl.when(me == 3)
    def _():
        extra[...] = extra_mine[...].astype(F32)

    @pl.when(me != 3)
    def _():
        extra[...] = got[keeper(me) ^ 4, :64, : 3 * part].astype(F32)

    total = taps.shape[0]
    grad = [extra[: min(64, total - 64 * g), g * part : (g + 1) * part] for g in range(-(-total // 64))]
    at = (total // 64) * part
    gain = extra[32:40, at : at + part] + extra[40:48, at : at + part]
    new = MOMENT_DECAY * taps_moment[...] + jnp.concatenate(grad, 0) / count[0:1, :]
    taps_moment_new[...] = new
    scale = jnp.sqrt(jnp.mean(new * new, 0, keepdims=True)) + 1e-08
    taps_new[...] = taps[...] - KERNEL_RATE * new / scale
    for which in range(2):
        for t in range(4):
            lanes = slice(t * part, (t + 1) * part)
            gain_moment_new[which : which + 1, lanes] = (
                MOMENT_DECAY * gain_moment[which : which + 1, lanes]
                + gain[4 * which + t : 4 * which + t + 1, :] / count[0:1, :]
            )
    new = gain_moment_new[...]
    scale = jnp.sqrt(jnp.mean(new * new, 1, keepdims=True)) + 1e-08
    gains_new[...] = norm_gains[...] - GAIN_RATE * new / scale


def per_device(
    tokens,
    cotangent,
    lengths,
    norm_gains,
    conv_kernel,
    mixer_weights,
    mlp_weights,
    gain_moment,
    kernel_moment,
    mixer_moment,
    mlp_moment,
):
    _, bucket, part = tokens.shape
    levels, taps, _ = conv_kernel.shape
    hidden = mlp_weights.shape[2]
    me = lax.axis_index("tensor")
    row = lax.axis_index("dp")
    dp = lax.axis_size("dp")
    width = 4 * part
    rows = width // dp
    half = bucket // 4
    piece_type = BF16 if rows % 16 == 0 else F32
    share = -(-levels * taps // dp)
    slot = -(-share // 8) * 8
    slot += (3 * rows + slot) % 16
    forward, inverse, kernel_forward, kernel_inverse = conv_tables(bucket, levels, taps, dp, slot)
    info = jnp.stack([me, lengths[0], row]).astype(jnp.int32)

    x_own, in_weights, in_gains, forward_one, inverse_one, late = fetch(
        info, 1, tokens[0], mixer_weights, norm_gains, forward, inverse, [(cotangent, 0), (mixer_weights, 2)]
    )
    (spec_k,) = call(
        spectrum_kernel,
        [((8 * half, part), F32)],
        [],
        (after(info, x_own), Late(kernel_forward), Late(conv_kernel.reshape(levels * taps, part))),
        2, 10,
    )
    x_pieces = gather_tensor(tokens[0], spec_k, x_own)

    act_like = ((bucket, part), F32)
    wide_like = ((half, width), F32)
    spec_like = ((2 * half, width), F32)
    whole_like = ((bucket, width), BF16)
    quarter_like = ((half, width), BF16)
    x, normed, n_own, inv_one, spec_v, conv, gate_act, gate_slope, branch, gains = call(
        entry_kernel,
        [whole_like, whole_like, Store(*act_like), Store((bucket, 1), F32), spec_like, act_like, act_like, act_like,
         ((bucket, part), BF16), ((2, width), F32)],
        [wide_like, spec_like],
        (info, x_own, *x_pieces[1:], in_weights, in_gains, forward_one, inverse_one, spec_k),
        0, 12,
    )
    late = gather_tensor(late, branch)
    cot, out_weights, delta_active, mlp_kept = call(
        cotangent_kernel,
        [whole_like, ((width, width), BF16), ((bucket, hidden), F32), (mlp_weights.shape, BF16)],
        [],
        (after(info, branch), *late, Late(mlp_weights)),
        3, 5,
    )
    branch_pieces = gather_tensor(branch, delta_active)
    near, kept, normed_two, active, delta_hidden, n_mine, inv_mine, middle_own = call(
        middle_kernel,
        [((width, width), BF16), ((width, width), F32), whole_like, ((bucket, hidden), BF16),
         ((bucket, hidden), BF16), wide_like, ((half, 1), F32), Store(*act_like)],
        [whole_like, ((bucket, width), F32)],
        (info, *branch_pieces, out_weights, x, gains, mlp_kept, delta_active),
        6, 12,
    )
    split_blocks = lambda v: v.reshape(2, -1, v.shape[-1])
    came = swap(split_blocks(near), "tensor", 1)
    mine, far = call(join_kernel, [wide_like, quarter_like], [], (info, split_blocks(kept), came), 1, 4)
    mlp_inputs = (normed_two, active, delta_hidden, cot)
    mlp_send, moment_send = call(
        mlp_away_kernel,
        [((width + 16, hidden), BF16), ((rows, hidden), F32)],
        [],
        (after(info, far), *mlp_inputs, Late(mlp_moment)),
        2, 5,
    )
    (mlp_keep,) = call(
        mlp_here_kernel, [((width + 16, hidden), F32)], [], (after(info, mlp_send), *mlp_inputs), 1000, 8
    )
    mlp_came = swap(mlp_send, "dp", 1)
    moment_came = swap(moment_send, "dp", 1)
    came = swap(far, "tensor", 2)
    delta_mid, grad_gain_two = call(
        norm_back_kernel,
        [quarter_like, ((1, width), F32)],
        [],
        (after(info, mlp_keep), mine, came, cot, n_mine, inv_mine, gains),
        1000, 4,
    )
    (kernel_inverse_one,) = fetch(after(info, delta_mid), 0, kernel_inverse)
    out_near, out_kept = call(
        mlp_out_kernel,
        [Store((2, bucket, part), BF16), Store((2, bucket, part), F32)],
        [((bucket, width), F32)],
        (after(info, kernel_inverse_one), active, mlp_kept),
        1, 8,
    )
    delta_pieces = gather_tensor(delta_mid, kernel_inverse_one, out_near)

    pairs = dp // 2
    parities = [[i for i in range(dp) if i % 2 == y] for y in range(2)]
    groups = [[8 * z + q for q in range(8)] for z in range(pairs)]
    block = (2 * rows + 16, hidden)
    if dp == 8:
        blocks = call(mlp_rows_kernel, [(block, BF16)] * pairs, [], (info, mlp_keep, mlp_came), 0, 6)
        blocks = [blocks[0]] + [swap(blocks[k], "dp", 2 * k) for k in range(1, pairs)]
    else:
        (blocks,) = call(mlp_rows_kernel, [((pairs, *block), BF16)], [], (info, mlp_keep, mlp_came), 0, 6)
        blocks = [lax.all_to_all(blocks, "dp", 0, 0, tiled=True, axis_index_groups=parities)]

    slots, one_near, one_kept, delta_own = call(
        mixer_back_kernel,
        [Store((dp, 3 * rows + slot, part), piece_type), Store((2, bucket + 32, part), BF16),
         Store((2, bucket + 32, part), F32), Store((bucket, part), BF16)],
        [whole_like, wide_like, spec_like, spec_like, ((8 * half, part), F32), ((bucket, 2 * part), BF16),
         ((bucket, width), F32)],
        (after(info, blocks[0]), *delta_pieces, in_weights, gate_act, gate_slope, conv, branch, normed, spec_v, spec_k, forward_one, inverse_one,
         kernel_inverse_one, gains, grad_gain_two),
        1000, 18,
    )
    arrived = lax.all_to_all(slots.astype(BF16), "dp", 0, 0, tiled=True)
    one_mine, one_tail, out_mine, far = call(
        join_late_kernel,
        [act_like, ((32, part), F32), act_like, ((2 * bucket + 32, part), BF16)],
        [],
        (info, Late(one_kept), swap(one_near, "tensor", 1), Late(out_kept), swap(out_near, "tensor", 1)),
        0, 6,
    )
    far_came = swap(far, "tensor", 2)
    pair, moment_mine, moment_other, count = call(
        mlp_moment_kernel,
        [((2 * rows, hidden), BF16), Store((rows, hidden), F32), Store((rows, hidden), F32), Store((8, part), F32)],
        [],
        (info, mlp_moment, moment_came, *blocks),
        1, 8,
    )
    if dp == 8:
        pair_pieces = [pair] + [swap(pair, "dp", 2 * k) for k in range(1, pairs)]
    else:
        pair_pieces = [lax.all_gather(pair, "dp", axis=0, tiled=True, axis_index_groups=parities)]
    height = -(-max(rows, slot + 16) // 16) * 16
    mixer_moment_new, slots, far_kept = call(
        moment_kernel,
        [Store((3, rows, part), F32), Store((4 * dp, height, part), piece_type), Store((2 * bucket + 32, part), BF16)],
        [],
        (info, arrived, Late(mixer_moment), Late(count), one_tail, far_came),
        1000, 8,
    )
    got = lax.all_to_all(slots.astype(BF16), ("dp", "tensor"), 0, 0, tiled=True)
    (mlp_columns,) = call(
        columns_kernel, [((width, hidden), BF16)], [], (after(info, slots), *pair_pieces), 1000, 4
    )
    mlp_pieces = [mlp_columns] + [lax.ppermute(mlp_columns, "tensor", [(3 ^ k, 3)]) for k in (1, 2, 3)]
    moment_back = swap(moment_other, "dp", 1)
    input_grad, block_out = call(
        output_kernel,
        [Store(*act_like), Store((bucket, part), BF16)],
        [],
        (after(info, slots), one_mine, Late(far_kept), out_mine, Late(delta_own), Late(n_own), Late(inv_one),
         Late(middle_own), Late(norm_gains), one_tail),
        0, 8,
    )
    (mlp_moment_new,) = call(
        aside_kernel, [Store((2, rows, hidden), F32)], [], (after(info, slots), Late(moment_mine), Late(moment_back)), 1, 4
    )
    square = ((width, width), F32)
    (sends,) = call(
        large_kernel,
        [Store((8, max(rows, 64), hidden), piece_type, True)],
        [square, square, ((2 * rows, width), F32)],
        (after(info, block_out, mlp_moment_new), *mlp_pieces),
        18, 24,
    )
    all_got = got
    sends = small_steps(after(info, sends), got, sends, rows, width, levels * taps)
    got = lax.all_to_all(sends.astype(BF16), ("dp", "tensor"), 0, 0, tiled=True, axis_index_groups=groups)
    (extra,) = call(
        functools.partial(extra_kernel, rows), [((64, 3 * part), BF16)], [((levels * taps, part), F32)],
        (after(info, sends), Late(all_got)), 0, 4,
    )
    flat = (levels * taps, part)
    old = fetch(
        after(info, extra), 0, mixer_weights, mlp_weights, norm_gains, gain_moment, conv_kernel.reshape(flat),
        kernel_moment.reshape(flat),
    )
    mixer_new, mlp_new, gain_moment_new, gains_new, kernel_moment_new, kernel_new = call(
        final_kernel,
        [Store((3, rows, part), F32), Store((2, rows, hidden), F32), ((2, width), F32), ((2, width), F32), (flat, F32),
         (flat, F32)],
        [((64, 3 * part), F32)],
        (info, got.astype(piece_type), extra, *old, Late(count)),
        0, 8,
    )
    kernel_moment_new, kernel_new = (v.reshape(conv_kernel.shape) for v in (kernel_moment_new, kernel_new))
    return (
        block_out[None],
        input_grad[None],
        gain_moment_new,
        gains_new,
        kernel_moment_new,
        kernel_new,
        mixer_moment_new,
        mixer_new,
        mlp_moment_new,
        mlp_new,
    )


def solution(mesh):
    tokens = P("dp", None, "tensor")
    columns = P(None, None, "tensor")
    blocks = P(None, "dp", "tensor")
    return jax.shard_map(
        per_device,
        mesh=mesh,
        in_specs=(tokens, tokens, P("dp"), P(), columns, columns, columns, P(), columns, blocks, blocks),
        out_specs=(tokens, tokens, P(), P(), columns, columns, blocks, blocks, blocks, blocks),
        check_vma=False,
    )
```

```python
import functools
import math

import jax
import jax.numpy as jnp
import ml_dtypes
import numpy as np
from jax import lax
from jax.experimental import pallas as pl
from jax.experimental.pallas import tpu as pltpu
from jax.sharding import PartitionSpec as P

NS_STEPS = 5
EPSILON = 1e-05
NS_COEF_A = 3.4445
NS_COEF_B = -4.775
NS_COEF_C = 2.0315
MOMENT_DECAY = 0.5
MATRIX_RATE = 1.0
GAIN_RATE = 0.1
KERNEL_RATE = 0.125
SCALE = 10**10
BF16 = jnp.bfloat16
F32 = jnp.float32


def conv_tables(bucket, levels, taps, dp, slot):
    half = bucket // 4
    size = 2 * half
    t = np.arange(half)
    k = np.arange(half)
    phase = 2 * np.pi * ((k[:, None] * t[None, :]) % size) / size
    forward = np.concatenate([np.cos(phase), -np.sin(phase)], 0)
    forward[half] = (-1.0) ** t
    scale = np.full((half,), 2.0 / size)
    scale[0] = 1.0 / size
    inverse = np.concatenate(
        [np.cos(phase).T * scale[None, :], -np.sin(phase).T * scale[None, :]], 1
    )
    inverse[:, half] = ((-1.0) ** t) / size
    spread = np.zeros((bucket, levels * taps))
    at = 0
    for level in range(levels):
        for tap in range(taps):
            width = 2**level
            spread[at : at + width, level * taps + tap] = 0.5**level
            at += width
    kernel_forward = np.concatenate(
        [forward @ spread[m * half : (m + 1) * half] for m in range(4)], 0
    )
    kernel_inverse = np.concatenate(
        [spread[m * half : (m + 1) * half].T @ inverse for m in range(4)], 1
    )
    share = -(-levels * taps // dp)
    kernel_inverse = np.pad(kernel_inverse, ((0, dp * share - levels * taps), (0, 0)))
    kernel_inverse = kernel_inverse.reshape(dp, share, -1)
    kernel_inverse = np.pad(kernel_inverse, ((0, 0), (0, slot - share), (0, 0))).reshape(dp * slot, -1)
    tables = []
    for table in (forward, inverse, kernel_forward, kernel_inverse):
        high = table.astype(ml_dtypes.bfloat16)
        low = (table - high.astype(np.float64)).astype(ml_dtypes.bfloat16)
        tables.append(np.stack([high, low]))
    return tables


def cross(a, b):
    return a[0] * b[0] - a[1] * b[1], a[0] * b[1] + a[1] * b[2]


def cross_conj(a, b):
    return a[0] * b[0] + a[1] * b[1], a[1] * b[2] - a[0] * b[1]


def with_edge(spec, first):
    real, imag = spec
    return real, jnp.where(first, 0.0, imag), jnp.where(first, imag, real)


def add_pairs(pairs):
    return functools.reduce(lambda p, q: (p[0] + q[0], p[1] + q[1]), pairs)


def spectral_blocks(left, right, conj, store):
    for step in range(4):
        rows = step * 64
        index = lax.broadcasted_iota(jnp.int32, (64, 128), 0)
        first = index + rows == 0
        sign = 1.0 - 2.0 * (index % 2).astype(F32)
        a = [left(r, rows) for r in range(4)]
        b = [with_edge(right(m, rows), first) for m in range(4)]
        if conj:
            sums = [add_pairs([cross_conj(a[r], b[r - q]) for r in range(q, 4)]) for q in range(4)]
        else:
            sums = [add_pairs([cross(a[r], b[q - r]) for r in range(q + 1)]) for q in range(4)]
        for q in range(4):
            other = q + 1 if conj else q - 1
            if 0 <= other < 4:
                real = sums[q][0] + sign * sums[other][0]
                imag = sums[q][1] + sign * sums[other][1]
            else:
                real, imag = sums[q]
            store(q, rows, real, imag)


def lane_pair(ref, half):
    return lambda r, rows: (
        ref[rows : rows + 64, r * 128 : (r + 1) * 128],
        ref[half + rows : half + rows + 64, r * 128 : (r + 1) * 128],
    )


def row_pair(ref, half):
    return lambda r, rows: (
        ref[2 * half * r + rows : 2 * half * r + rows + 64, :],
        ref[2 * half * r + half + rows : 2 * half * r + half + rows + 64, :],
    )


def gelu_both(x):
    c = math.sqrt(2.0 / math.pi)
    t = jnp.tanh(c * (x + 0.044715 * x * x * x))
    value = 0.5 * x * (1.0 + t)
    slope = 0.5 * (1.0 + t) + 0.5 * x * (1.0 - t * t) * (c * (1.0 + 3 * 0.044715 * x * x))
    return value, slope


def after(value, *others):
    return lax.optimization_barrier((value, *others))[0]


def swap(value, axis, k):
    size = lax.axis_size(axis)
    return lax.ppermute(value, axis, [(i, i ^ k) for i in range(size)])


def gather_tensor(value, *meanwhile):
    far = swap(value, "tensor", 2)
    near = swap(value, "tensor", 1)
    if meanwhile:
        far = after(far, *meanwhile)
    far_near = swap(far, "tensor", 1)
    return [value, near, far, far_near]


def gather_dp(value, me, low=0):
    size = lax.axis_size("dp")
    whole = value[None]
    while (1 << low) < size:
        bits = min(3, size.bit_length() - 1 - low)
        mine = (me >> low) & ((1 << bits) - 1)
        out = jnp.zeros((1 << bits,) + whole.shape, whole.dtype)
        for k in range(1 << bits):
            piece = whole if k == 0 else swap(whole, "dp", k << low)
            out = lax.dynamic_update_index_in_dim(out, piece, mine ^ k, 0)
        whole = out.reshape((-1,) + value.shape)
        low += bits
    return whole


def dot(a, b, contract):
    return lax.dot_general(a, b, ((contract[0], contract[1]), ((), ())), preferred_element_type=F32)


NN = ((1,), (0,))
NT = ((1,), (1,))
TN = ((0,), (0,))


def split(value):
    high = value.astype(BF16)
    return high, (value - high.astype(F32)).astype(BF16)


def table_dot(table, value):
    high, low = split(value)
    return dot(table[0], high, NN) + (dot(table[1], high, NN) + dot(table[0], low, NN))


def symmetric(left, right, product):
    half = left[0].shape[0] // 2
    top = product([v[:half] for v in left], right, None)
    low = product([v[half:] for v in left], right, half)
    return jnp.concatenate([top, jnp.concatenate([top[:, half:].T, low], 1)], 0)


def three_terms(left, right, cut=None):
    right = right if cut is None else [v[:, cut:] for v in right]
    left = jnp.concatenate([left[0], left[0], left[1]], 1)
    return dot(left, jnp.concatenate([right[0], right[1], right[0]], 0), NN)


def newton_schulz(blocks, a_ref, p_ref, r_ref, start):
    size = a_ref.shape[0]
    row = lax.broadcasted_iota(jnp.int32, (size, size), 0)
    col = lax.broadcasted_iota(jnp.int32, (size, size), 1)
    unit = (row == col).astype(F32)
    blocks = [block() for block in blocks]
    gram = 0.0
    for block in blocks:
        gram = gram + symmetric([block], [block], lambda a, b, cut: dot(a[0], b[0] if cut is None else b[0][cut:], NT))
    scale = 1.0 / (jnp.sqrt(jnp.sum(gram * unit)) + 1e-07)
    a_ref[...] = gram * (scale * scale)

    def advance(first):
        a = a_ref[...]
        terms = split(a)
        poly = NS_COEF_A * unit + NS_COEF_B * a + NS_COEF_C * symmetric(terms, terms, three_terms)
        poly_terms = split(poly)
        if first:
            p_ref[...] = poly
            r_ref[...] = p_ref[pl.ds(start, r_ref.shape[0]), :]
        else:
            r_ref[...] = three_terms(split(r_ref[...]), poly_terms)
        half = symmetric(terms, poly_terms, three_terms)
        a_ref[...] = symmetric(poly_terms, split(half), three_terms)

    advance(True)
    pl.loop(0, NS_STEPS - 2)(lambda _: advance(False))
    rows, terms = r_ref[...], split(a_ref[...])
    once = three_terms(split(rows), terms)
    rows = NS_COEF_A * rows + NS_COEF_B * once + NS_COEF_C * three_terms(split(once), terms)
    high, low = split(rows)
    return [scale * (dot(high, block, NN) + dot(low, block, NN)) for block in blocks]


VMEM = pl.BlockSpec(memory_space=pltpu.VMEM)
SMEM = pl.BlockSpec(memory_space=pltpu.SMEM)


HBM = pl.BlockSpec(memory_space=pltpu.HBM)


class Late:
    def __init__(self, array):
        self.shape, self.dtype = array.shape, array.dtype
        self.array = pltpu.with_memory_space_constraint(array, pltpu.HBM)


class Store:
    def __init__(self, shape, dtype, own=False):
        self.shape, self.dtype, self.own = shape, dtype, own


class Bare:
    def __init__(self, shape, dtype):
        self.shape, self.dtype = shape, dtype


class Waiting:
    def __init__(self, copy, ref):
        self.copy, self.ref, self.started = copy, ref, False

    def ready(self):
        self.copy.wait()
        return self.ref

    def send(self):
        self.copy.start()
        self.started = True


def call(kernel, outs, scratch, args, time, limit):
    outs = [o if isinstance(o, (Store, Bare)) else jax.ShapeDtypeStruct(*o) for o in outs]
    late = [a for a in (*args, *outs) if isinstance(a, (Late, Store))]
    n_in, n_out = len(args), len(outs)

    def body(*refs):
        given, rest = refs[: n_in + n_out], refs[n_in + n_out :]
        buffers, rest = rest[: len(late)], rest[len(late) :]
        semaphores = rest[-1] if late else None
        passed, stores, at = [], [], 0
        for what, ref in zip((*args, *outs), given):
            if isinstance(what, Late):
                copy = pltpu.make_async_copy(ref, buffers[at], semaphores.at[at])
                copy.start()
            elif isinstance(what, Store):
                copy = pltpu.make_async_copy(buffers[at], ref, semaphores.at[at])
            else:
                passed.append(ref)
                continue
            passed.append(Waiting(copy, buffers[at]))
            if isinstance(what, Store) and not what.own:
                stores.append(passed[-1])
            at += 1
        kernel(*passed, *(rest[:-1] if late else rest))
        for store in stores:
            if not store.started:
                store.send()
        for store in stores:
            store.copy.wait()

    return pl.pallas_call(
        body,
        out_shape=tuple(pltpu.HBM(o.shape, o.dtype) if isinstance(o, (Store, Bare)) else o for o in outs),
        in_specs=[SMEM] + [HBM if isinstance(a, Late) else VMEM for a in args[1:]],
        out_specs=tuple(HBM if isinstance(o, (Store, Bare)) else VMEM for o in outs),
        scratch_shapes=[pltpu.VMEM(a.shape, a.dtype) for a in late]
        + [pltpu.VMEM(*what) if isinstance(what, tuple) else what for what in scratch]
        + ([pltpu.SemaphoreType.DMA((len(late),))] if late else []),
        compiler_params=pltpu.CompilerParams(vmem_limit_bytes=limit * 2**20),
        cost_estimate=pl.CostEstimate(flops=max(time * SCALE, 10**6), bytes_accessed=0, transcendentals=0),
    )(*(a.array if isinstance(a, Late) else a for a in args))


def fetch(token, time, *arrays):
    arrays = [a if isinstance(a, list) else [(a, None)] for a in arrays]
    shapes = []
    for a in arrays:
        cuts = [p.shape if index is None else p.shape[1:] for p, index in a]
        shapes.append(jax.ShapeDtypeStruct((sum(c[0] for c in cuts), *cuts[0][1:]), a[0][0].dtype))
    flat = [pltpu.with_memory_space_constraint(p, pltpu.HBM) for a in arrays for p, _ in a]

    def body(token_ref, *refs):
        outs, semaphores, copies, at = refs[len(flat) : -1], refs[-1], [], 0
        for a, out in zip(arrays, outs):
            row = 0
            for _, index in a:
                source = refs[at] if index is None else refs[at].at[index]
                target = out if len(a) == 1 else out.at[row : row + source.shape[0]]
                copies.append(pltpu.make_async_copy(source, target, semaphores.at[at]))
                copies[-1].start()
                row, at = row + source.shape[0], at + 1
        for copy in copies:
            copy.wait()

    return pl.pallas_call(
        body,
        out_shape=tuple(shapes),
        in_specs=[SMEM] + [HBM] * len(flat),
        out_specs=(VMEM,) * len(shapes),
        scratch_shapes=[pltpu.SemaphoreType.DMA((len(flat),))],
        compiler_params=pltpu.CompilerParams(vmem_limit_bytes=2 * 2**20),
        cost_estimate=pl.CostEstimate(flops=max(time * SCALE, 10**6), bytes_accessed=0, transcendentals=0),
    )(token, *flat)


def block_at(index, size):
    return pl.ds(pl.multiple_of(index * size, size), size)


def row_mask(info, start, rows):
    return (start + lax.broadcasted_iota(jnp.int32, (rows, 1), 0) < info[1]).astype(F32)


def spectrum_kernel(info, table, taps, spec_k):
    taps = taps.ready()[...]
    spec_k[...] = table_dot(table.ready(), taps)


def entry_kernel(info, p0, p1, p2, p3, weights, gains, forward, inverse, spec_k,
                 x, normed, n_own, inv, spec_v, conv, act, slope, branch, gains_kept, wide, spec_y):
    me = info[0]
    part = p1.shape[1]
    for k, piece in enumerate((p0, p1, p2, p3)):
        x[:, block_at(me ^ k, part)] = piece[...]
    gains_kept[...] = gains[...]
    gain = gains[0:1, :]
    half = x.shape[0] // 4
    for c in range(4):
        r = slice(c * half, (c + 1) * half)
        v = x[r, :].astype(F32)
        mean = jnp.mean(v, 1, keepdims=True)
        centred = v - mean
        scale = lax.rsqrt(jnp.mean(centred * centred, 1, keepdims=True) + EPSILON)
        normed[r, :] = (centred * scale * gain).astype(BF16)
        inv.ref[r, :] = scale
        n_own.ref[r, :] = (p0[r, :].astype(F32) - mean) * scale
    n_own.send()
    inv.send()
    for c in range(4):
        r = slice(c * half, (c + 1) * half)
        normal = normed[r, :]
        wide[:, c * part : (c + 1) * part] = dot(normal, weights[0], NN)
        act[r, :], slope[r, :] = gelu_both(dot(normal, weights[1], NN))
    spec_v[...] = table_dot(forward, wide[...])

    def store(q, rows, real, imag):
        spec_y[rows : rows + 64, q * part : (q + 1) * part] = real
        spec_y[half + rows : half + rows + 64, q * part : (q + 1) * part] = imag

    spectral_blocks(lane_pair(spec_v, half), row_pair(spec_k, half), False, store)
    wide[...] = table_dot(inverse, spec_y[...])
    for c in range(4):
        r = slice(c * half, (c + 1) * half)
        out = wide[:, c * part : (c + 1) * part]
        conv[r, :] = out
        out = (act[r, :] * out * row_mask(info, c * half, half)).astype(BF16)
        branch[r, :] = out


def cotangent_kernel(info, p0, p1, p2, p3, weights, cot, out_w, delta, weights_kept):
    part = p0.shape[1]
    for k, piece in enumerate((p0, p1, p2, p3)):
        cot[:, block_at(info[0] ^ k, part)] = piece[: cot.shape[0], :]
        out_w[:, block_at(info[0] ^ k, part)] = piece[cot.shape[0] :, :]
    step = cot.shape[0] // 4
    weights = weights.ready()
    weights_kept[...] = weights[...]
    for c in range(4):
        r = slice(c * step, (c + 1) * step)
        delta[r, :] = dot(cot[r, :], weights[1], NN)


def middle_kernel(info, b0, b1, b2, b3, out_w, x, gains, weights, delta_active,
                  near, kept, normed, active, delta_hidden, n_mine, inv_mine, middle_own, branch, middle):
    me = info[0]
    part = b0.shape[1]
    step = x.shape[0] // 4
    for k, piece in enumerate((b0, b1, b2, b3)):
        branch[:, block_at(me ^ k, part)] = piece[...]
    gain = gains[1:2, :]
    for k in (1, 3, 0, 2):
        block = me ^ k
        r = block_at(block, step)
        mid = x[r, :].astype(F32) + dot(branch[r, :], out_w[...], NT)
        middle[r, :] = mid
        centred = mid - jnp.mean(mid, 1, keepdims=True)
        scale = lax.rsqrt(jnp.mean(centred * centred, 1, keepdims=True) + EPSILON)
        normal = centred * scale
        if k == 0:
            n_mine[...] = normal
            inv_mine[...] = scale
        normal = (normal * gain).astype(BF16)
        normed[r, :] = normal
        value, slope = gelu_both(dot(normal, weights[0], NN))
        mask = row_mask(info, block * step, step)
        active[r, :] = (value * mask).astype(BF16)
        back = (delta_active[r, :] * mask * slope).astype(BF16)
        delta_hidden[r, :] = back
        share = dot(back, weights[0], NT)
        if k % 2:
            near[(k // 2) * step : (k // 2 + 1) * step, :] = share.astype(BF16)
        else:
            kept[(k // 2) * step : (k // 2 + 1) * step, :] = share
    middle_own.ref[...] = middle[:, block_at(me, part)]


def mlp_kernel(info, normed, active, delta_hidden, cot, moment, out, moment_send, away):
    size = normed.shape[1]
    wanted = (info[2] + away) % 2

    @pl.when(wanted == 0)
    def _():
        out[:size, :] = dot(normed[...], delta_hidden[...], TN).astype(out.dtype)

    @pl.when(wanted == 1)
    def _():
        out[:size, :] = dot(cot[...], active[...], TN).astype(out.dtype)

    length = jnp.full((16, out.shape[1]), 1, jnp.int32) * info[1]
    first = lax.broadcasted_iota(jnp.int32, length.shape, 0) == 0
    out[size:, :] = jnp.where(first, length // 32, length % 32).astype(F32).astype(out.dtype)
    if away:
        moment_send[...] = moment.ready()[wanted]


def mlp_away_kernel(info, normed, active, delta_hidden, cot, moment, out, moment_send):
    mlp_kernel(info, normed, active, delta_hidden, cot, moment, out, moment_send, 1)


def mlp_here_kernel(info, normed, active, delta_hidden, cot, out):
    mlp_kernel(info, normed, active, delta_hidden, cot, None, out, None, 0)


def mlp_out_kernel(info, active, weights, near, kept, part_out):
    me = info[0]
    step = active.shape[0] // 4
    part = near.ref.shape[2]
    for c in range(4):
        r = slice(c * step, (c + 1) * step)
        part_out[r, :] = dot(active[r, :], weights[1], NT)
    for k in range(4):
        share = part_out[:, block_at(me ^ k, part)]
        if k % 2:
            near.ref[k // 2] = share.astype(BF16)
        else:
            kept.ref[k // 2] = share


def mlp_rows_kernel(info, keep, came, *outs):
    size = came.shape[0] - 16
    pairs = outs[0].shape[0] if len(outs) == 1 else len(outs)
    rows = size // pairs
    length = keep[size:, :] + came[size:, :].astype(F32)
    for k in range(pairs):
        if len(outs) == 1:
            r, out = pl.ds(k * rows, rows), outs[0].at[k]
        else:
            r, out = block_at((info[2] // 2) ^ k, rows), outs[k]
        out[:rows, :] = (keep[r, :] + came[r, :].astype(F32)).astype(out.dtype)
        out[rows:, :] = length.astype(out.dtype)


def mlp_moment_kernel(info, moment, other_moment, *refs):
    *pieces, matrix, mine, other, count = refs
    rows = moment.shape[1]
    side = info[2] % 2
    if len(pieces) == 1:
        pieces = [pieces[0].at[k] for k in range(pieces[0].shape[0])]
    total = pieces[0][...].astype(F32)
    for piece in pieces[1:]:
        total = total + piece[...].astype(F32)
    tokens = 32.0 * total[2 * rows : 2 * rows + 1, :] + total[2 * rows + 1 : 2 * rows + 2, :]
    count.ref[...] = jnp.broadcast_to(tokens[:, : count.ref.shape[1]], count.ref.shape)
    old = moment[side]
    for which in range(2):
        new = total[which * rows : (which + 1) * rows, :] / tokens

        @pl.when(side == which)
        def _(new=new, which=which):
            now = MOMENT_DECAY * old + new
            mine.ref[...] = now
            matrix[which * rows : (which + 1) * rows, :] = now.astype(matrix.dtype)

        @pl.when(side != which)
        def _(new=new, which=which):
            now = MOMENT_DECAY * other_moment[...] + new
            other.ref[...] = now
            matrix[which * rows : (which + 1) * rows, :] = now.astype(matrix.dtype)


def columns_kernel(info, *refs):
    *pieces, out = refs
    rows = pieces[0].shape[0]
    for k, piece in enumerate(pieces):
        out[block_at((info[2] // 2) ^ k, rows), :] = piece[...]


def join_kernel(info, kept, came, mine, far):
    mine[...] = kept[0] + came[0].astype(F32)
    far[...] = (kept[1] + came[1].astype(F32)).astype(BF16)


def join_late_kernel(info, one_kept, one_came, out_kept, out_came, one_mine, tail, out_mine, far):
    one_kept, out_kept = one_kept.ready(), out_kept.ready()
    size = out_mine.shape[0]
    one_mine[...] = one_kept[0, :size, :] + one_came[0, :size, :].astype(F32)
    tail[...] = one_kept[0, size:, :] + one_came[0, size:, :].astype(F32)
    far[: size + 16, :] = (one_kept[1] + one_came[1].astype(F32)).astype(BF16)
    out_mine[...] = out_kept[0] + out_came[0].astype(F32)
    far[size + 16 :, :] = (out_kept[1] + out_came[1].astype(F32)).astype(BF16)


def norm_back_kernel(info, mine, came, cot, n_mine, inv_mine, gains, delta, grad_gain):
    size = mine.shape[0]
    total = mine[...] + came[...].astype(F32)
    n = n_mine[...]
    q = total * gains[1:2, :]
    back = inv_mine[...] * (q - jnp.mean(q, 1, keepdims=True) - n * jnp.mean(q * n, 1, keepdims=True))
    delta[...] = (cot[block_at(info[0], size), :].astype(F32) + back).astype(BF16)
    grad_gain[...] = jnp.sum(total * n, 0, keepdims=True)


def mixer_back_kernel(info, d0, d1, d2, d3, weights, act, slope, conv, branch, normed, spec_v, spec_k, forward, inverse,
                      kernel_inverse, gains, gain_two,
                      keep, send, near, kept, delta_own, gain_part,
                      slots, semaphores, delta, wide, spec_d, spec_y, spec_u, back, share):
    me = info[0]
    step, width = d0.shape
    part = slots.shape[3]
    half = step
    for k, piece in enumerate((d0, d1, d2, d3)):
        block = me ^ k
        r = block_at(block, step)
        delta[r, :] = piece[...]
        down = dot(piece[...], weights[2], NN) * row_mask(info, block * step, step)
        back[r, part:] = (down * conv[r, :] * slope[r, :]).astype(BF16)
        wide[:, block_at(block, part)] = down * act[r, :]
    delta_own.ref[...] = delta[:, block_at(me, part)]
    delta_own.send()
    spec_d[...] = table_dot(forward, wide[...])

    def store(q, rows, real, imag):
        spec_y[rows : rows + 64, q * part : (q + 1) * part] = real
        spec_y[half + rows : half + rows + 64, q * part : (q + 1) * part] = imag

    def store_rows(q, rows, real, imag):
        spec_u[2 * half * q + rows : 2 * half * q + rows + 64, :] = real
        spec_u[2 * half * q + half + rows : 2 * half * q + half + rows + 64, :] = imag

    spectral_blocks(lane_pair(spec_d, half), row_pair(spec_k, half), True, store)
    wide[...] = table_dot(inverse, spec_y[...])
    for c in range(4):
        back[c * half : (c + 1) * half, :part] = wide[:, c * part : (c + 1) * part].astype(BF16)
    spectral_blocks(lane_pair(spec_d, half), lane_pair(spec_v, half), True, store_rows)
    grad_kernel = table_dot(kernel_inverse, spec_u[...])
    grads = dot(normed[...], back[...], TN)
    grad_out = dot(delta[...], branch[...], TN)
    dp = 2 * slots.shape[1]
    rows = width // dp
    taps = grad_kernel.shape[0] // dp
    for i in range(dp):
        r = slice(i * rows, (i + 1) * rows)
        slots[i % 2, i // 2, :rows, :] = grads[r, :part].astype(slots.dtype)
        slots[i % 2, i // 2, rows : 2 * rows, :] = grads[r, part:].astype(slots.dtype)
        slots[i % 2, i // 2, 2 * rows : 3 * rows, :] = grad_out[r, :].astype(slots.dtype)
        slots[i % 2, i // 2, 3 * rows :, :] = grad_kernel[i * taps : (i + 1) * taps, :].astype(slots.dtype)
    side = info[2] % 2
    copies = [
        pltpu.make_async_copy(slots.at[side], keep, semaphores.at[0]),
        pltpu.make_async_copy(slots.at[1 - side], send, semaphores.at[1]),
    ]
    for copy in copies:
        copy.start()
    ones = jnp.ones((8, width), BF16)
    gain_one = jnp.zeros((1, width), F32)
    sums = [[], []]
    gain = jnp.broadcast_to(gains[0:1, :], (8, width)).astype(BF16)
    for c in range(4):
        r = slice(c * step, (c + 1) * step)
        out = dot(back[r, :part], weights[0], NT) + dot(back[r, part:], weights[1], NT)
        share[r, :] = out
        first = dot(gain, out.astype(BF16), NT)
        both = out * normed[r, :].astype(F32)
        gain_one = gain_one + jnp.sum(both, 0, keepdims=True)
        second = dot(ones, both.astype(BF16), NT)
        for h in range(step // part):
            sums[0].append(first[0:1, h * part : (h + 1) * part])
            sums[1].append(second[0:1, h * part : (h + 1) * part])
    gain_one = gain_one / gains[0:1, :]
    gain = [g[:, q * part : (q + 1) * part] for g in (gain_one, gain_two[...]) for q in range(4)]
    gain_part.ref[...] = jnp.concatenate(gain, 0)
    tail = jnp.concatenate([*sums[0], *sums[1]], 0)
    for k in range(4):
        block = share[:, block_at(me ^ k, part)]
        if k % 2:
            near.ref[k // 2, : share.shape[0], :] = block.astype(BF16)
            near.ref[k // 2, share.shape[0] :, :] = tail.astype(BF16)
        else:
            kept.ref[k // 2, : share.shape[0], :] = block
            kept.ref[k // 2, share.shape[0] :, :] = tail
    for copy in copies:
        copy.wait()


def pair_sum_kernel(info, keep, came, out):
    keep, came = keep.ready(), came.ready()
    for z in range(keep.shape[0]):
        out.ref[z] = (keep[z].astype(F32) + came[z].astype(F32)).astype(out.ref.dtype)


def keeper(t):
    return 4 * (1 - t // 2) + t


def moment_kernel(info, arrived, moment, count, gain_part, moment_new, slots):
    me = info[0]
    pairs = arrived.shape[0]
    _, rows, part = moment.ref.shape
    taps = arrived.shape[1] - 3 * rows
    total = arrived[0].astype(F32)
    for i in range(1, pairs):
        total = total + arrived[i].astype(F32)
    high, low = split(gain_part.ready()[...])
    rest = jnp.concatenate([total[3 * rows :, :], high.astype(F32), low.astype(F32)], 0).astype(slots.ref.dtype)
    moment, count = moment.ready(), count.ready()
    for which in range(3):
        value = MOMENT_DECAY * moment[which] + total[which * rows : (which + 1) * rows, :] / count[0:1, :]
        moment_new.ref[which] = value
        for z in range(pairs):
            slots.ref[8 * z + keeper(which), :rows, :] = value.astype(slots.ref.dtype)
    for t in range(4):
        for z in range(pairs):
            slots.ref[8 * z + (keeper(t) ^ 4), : taps + 16, :] = rest
            if t == 3:
                slots.ref[8 * z + keeper(t), : taps + 16, :] = rest
    slots.send()


def output_kernel(info, mine, came, out_mine, delta_own, n_own, inv, middle_own, gains, tail, input_grad, block_out):
    part = mine.shape[1]
    came = came.ready()
    gain = gains.ready()[0:1, block_at(info[0], part)]
    size = mine.shape[0]
    sums = (tail[...] + came[size : size + 16, :].astype(F32)) / (4 * part)
    middle_own = middle_own.ready()
    n_own, inv, delta_own = n_own.ready(), inv.ready(), delta_own.ready()
    for h in range(mine.shape[0] // part):
        r = slice(h * part, (h + 1) * part)
        block_out.ref[r, :] = (middle_own[r, :] + (out_mine[r, :] + came[size + 16 + h * part : size + 16 + (h + 1) * part, :].astype(F32))).astype(BF16)
        column = lambda at: jnp.broadcast_to(sums[at : at + 1, :], (part, part)).T
        total = mine[r, :] + came[r, :].astype(F32)
        back = total * gain - column(h) - n_own[r, :] * column(8 + h)
        input_grad.ref[r, :] = delta_own[r, :].astype(F32) + inv[r, :] * back


def large_kernel(info, m0, m1, m2, m3, out, a, p, r):
    me, row = info[0], info[2]
    rows = r.shape[0] // 2

    @pl.when(me == 3)
    def _():
        start = pl.multiple_of((row // 2) * (2 * rows), 2 * rows)
        blocks = [lambda piece=piece: piece[...] for piece in (m0, m1, m2, m3)]
        for k, steps in enumerate(newton_schulz(blocks, a, p, r, start)):
            for y in range(2):
                out.ref[4 * y + (3 ^ k), :rows, :] = steps[y * rows : (y + 1) * rows, :].astype(out.ref.dtype)
        out.send()
        out.copy.wait()


def gather_extra(got, me, rows, packed, extra):
    total, dp = packed.shape[0], got.shape[0] // 4
    part = packed.shape[1]
    share = -(-total // dp)
    taps = -(-share // 8) * 8
    taps += (3 * rows + taps) % 16
    gain = 0.0
    for i in range(dp):
        both = got[4 * i + me, : taps + 16, :].astype(F32)
        count = min(share, total - i * share)
        if count > 0:
            packed[i * share : i * share + count, :] = both[:count, :]
        for t in range(4):
            both = got[4 * i + t, taps : taps + 16, :].astype(F32)
            gain = gain + (both[:8, :] + both[8:, :])
    high, low = split(gain)
    extra[...] = jnp.zeros_like(extra)
    for g in range(-(-total // 64)):
        count = min(64, total - 64 * g)
        extra[:count, g * part : (g + 1) * part] = packed[64 * g : 64 * g + count, :].astype(extra.dtype)
    at = (total // 64) * part
    extra[32:48, at : at + part] = jnp.concatenate([high.astype(F32), low.astype(F32)], 0).astype(extra.dtype)


def small_kernel(info, source, slots, out, got, extra, matrix, a, p, r, packed, steps, semaphore):
    me, row = info[0], info[2]
    side = row % 2
    size, width = matrix.shape
    rows = r.shape[0] // 2
    part = width // 4
    start = pl.multiple_of((row // 2) * (2 * rows), 2 * rows)
    keeps = jnp.logical_and(side == 1 - me // 2, me < 3)

    @pl.when(me < 3)
    def _():
        arrive = pltpu.make_async_copy(source, got, semaphore.at[2])
        arrive.start()
        arrive.wait()

        @pl.when(keeps)
        def _():
            for i in range(size // rows):
                for t in range(4):
                    matrix[i * rows : (i + 1) * rows, t * part : (t + 1) * part] = got[4 * i + t, :rows, :].astype(BF16)
            (result,) = newton_schulz([lambda: matrix[...]], a, p, r, start)
            for q in range(8):
                lanes = slice((q % 4) * part, (q % 4 + 1) * part)
                steps[q] = result[(q // 4) * rows : (q // 4 + 1) * rows, lanes].astype(steps.dtype)
            copy = pltpu.make_async_copy(steps, out.at[:, pl.ds(0, rows), pl.ds(0, part)], semaphore.at[0])
            copy.start()
            copy.wait()

        @pl.when(jnp.logical_not(keeps))
        def _():
            gather_extra(got, me, rows, packed, extra)
            copies = [
                pltpu.make_async_copy(extra, out.at[4 * y + me, pl.ds(0, 64), pl.ds(0, 3 * part)], semaphore.at[y])
                for y in range(2)
            ]
            for copy in copies:
                copy.start()
            for copy in copies:
                copy.wait()


def small_steps(info, got, slots, rows, width, taps):
    part = width // 4
    square = pltpu.VMEM((width, width), F32)
    return pl.pallas_call(
        small_kernel,
        out_shape=pltpu.HBM(slots.shape, slots.dtype),
        in_specs=[SMEM, HBM, HBM],
        out_specs=HBM,
        scratch_shapes=[
            pltpu.VMEM(got.shape, got.dtype), pltpu.VMEM((64, 3 * part), slots.dtype), pltpu.VMEM((width, width), BF16), square,
            square, pltpu.VMEM((2 * rows, width), F32), pltpu.VMEM((taps, part), F32), pltpu.VMEM((8, rows, part), slots.dtype),
            pltpu.SemaphoreType.DMA((3,)),
        ],
        input_output_aliases={2: 0},
        compiler_params=pltpu.CompilerParams(vmem_limit_bytes=24 * 2**20),
        cost_estimate=pl.CostEstimate(flops=18 * SCALE, bytes_accessed=0, transcendentals=0),
    )(info, pltpu.with_memory_space_constraint(got, pltpu.HBM), pltpu.with_memory_space_constraint(slots, pltpu.HBM))


def extra_kernel(rows, info, got, extra, packed):
    gather_extra(got.ready(), info[0], rows, packed, extra)


def aside_kernel(info, moment_mine, moment_back, moment_new):
    side = info[2] % 2
    moment_new.ref[side] = moment_mine.ready()[...]
    moment_new.ref[1 - side] = moment_back.ready()[...]


def final_kernel(info, got, extra_mine, mixer_weights, mlp_weights, norm_gains, gain_moment, taps, taps_moment, count,
                 mixer_new, mlp_new, gain_moment_new, gains_new, taps_moment_new, taps_new, extra):
    me, row = info[0], info[2]
    count = count.ready()
    _, rows, part = mixer_new.ref.shape
    hidden = mlp_new.ref.shape[2]
    width = 4 * part
    for t in range(3):
        old = mixer_weights[t, block_at(row, rows), :].astype(F32)
        mixer_new.ref[t] = old - MATRIX_RATE * got[keeper(t), :rows, :part].astype(F32)
    mixer_new.send()
    rate = MATRIX_RATE * math.sqrt(4 * hidden / width)
    for which in range(2):
        old = mlp_weights[which, block_at(row, rows), :].astype(F32)
        mlp_new.ref[which] = old - rate * got[4 * which + 3, :rows, :].astype(F32)
    mlp_new.send()
    @pl.when(me == 3)
    def _():
        extra[...] = extra_mine[...].astype(F32)

    @pl.when(me != 3)
    def _():
        extra[...] = got[keeper(me) ^ 4, :64, : 3 * part].astype(F32)

    total = taps.shape[0]
    grad = [extra[: min(64, total - 64 * g), g * part : (g + 1) * part] for g in range(-(-total // 64))]
    at = (total // 64) * part
    gain = extra[32:40, at : at + part] + extra[40:48, at : at + part]
    new = MOMENT_DECAY * taps_moment[...] + jnp.concatenate(grad, 0) / count[0:1, :]
    taps_moment_new[...] = new
    scale = jnp.sqrt(jnp.mean(new * new, 0, keepdims=True)) + 1e-08
    taps_new[...] = taps[...] - KERNEL_RATE * new / scale
    for which in range(2):
        for t in range(4):
            lanes = slice(t * part, (t + 1) * part)
            gain_moment_new[which : which + 1, lanes] = (
                MOMENT_DECAY * gain_moment[which : which + 1, lanes]
                + gain[4 * which + t : 4 * which + t + 1, :] / count[0:1, :]
            )
    new = gain_moment_new[...]
    scale = jnp.sqrt(jnp.mean(new * new, 1, keepdims=True)) + 1e-08
    gains_new[...] = norm_gains[...] - GAIN_RATE * new / scale


def per_device(
    tokens,
    cotangent,
    lengths,
    norm_gains,
    conv_kernel,
    mixer_weights,
    mlp_weights,
    gain_moment,
    kernel_moment,
    mixer_moment,
    mlp_moment,
):
    _, bucket, part = tokens.shape
    levels, taps, _ = conv_kernel.shape
    hidden = mlp_weights.shape[2]
    me = lax.axis_index("tensor")
    row = lax.axis_index("dp")
    dp = lax.axis_size("dp")
    width = 4 * part
    rows = width // dp
    half = bucket // 4
    piece_type = BF16 if rows % 16 == 0 else F32
    share = -(-levels * taps // dp)
    slot = -(-share // 8) * 8
    slot += (3 * rows + slot) % 16
    forward, inverse, kernel_forward, kernel_inverse = conv_tables(bucket, levels, taps, dp, slot)
    info = jnp.stack([me, lengths[0], row]).astype(jnp.int32)

    x_own, in_weights, in_gains, forward_one, inverse_one, late = fetch(
        info, 1, tokens[0], mixer_weights, norm_gains, forward, inverse, [(cotangent, 0), (mixer_weights, 2)]
    )
    (spec_k,) = call(
        spectrum_kernel,
        [((8 * half, part), F32)],
        [],
        (after(info, x_own), Late(kernel_forward), Late(conv_kernel.reshape(levels * taps, part))),
        2, 10,
    )
    x_pieces = gather_tensor(tokens[0], spec_k, x_own)

    act_like = ((bucket, part), F32)
    wide_like = ((half, width), F32)
    spec_like = ((2 * half, width), F32)
    whole_like = ((bucket, width), BF16)
    quarter_like = ((half, width), BF16)
    x, normed, n_own, inv_one, spec_v, conv, gate_act, gate_slope, branch, gains = call(
        entry_kernel,
        [whole_like, whole_like, Store(*act_like), Store((bucket, 1), F32), spec_like, act_like, act_like, act_like,
         ((bucket, part), BF16), ((2, width), F32)],
        [wide_like, spec_like],
        (info, x_own, *x_pieces[1:], in_weights, in_gains, forward_one, inverse_one, spec_k),
        0, 12,
    )
    late = gather_tensor(late, branch)
    cot, out_weights, delta_active, mlp_kept = call(
        cotangent_kernel,
        [whole_like, ((width, width), BF16), ((bucket, hidden), F32), (mlp_weights.shape, BF16)],
        [],
        (after(info, branch), *late, Late(mlp_weights)),
        3, 5,
    )
    branch_pieces = gather_tensor(branch, delta_active)
    near, kept, normed_two, active, delta_hidden, n_mine, inv_mine, middle_own = call(
        middle_kernel,
        [((width, width), BF16), ((width, width), F32), whole_like, ((bucket, hidden), BF16),
         ((bucket, hidden), BF16), wide_like, ((half, 1), F32), Store(*act_like)],
        [whole_like, ((bucket, width), F32)],
        (info, *branch_pieces, out_weights, x, gains, mlp_kept, delta_active),
        6, 12,
    )
    split_blocks = lambda v: v.reshape(2, -1, v.shape[-1])
    came = swap(split_blocks(near), "tensor", 1)
    mine, far = call(join_kernel, [wide_like, quarter_like], [], (info, split_blocks(kept), came), 1, 4)
    mlp_inputs = (normed_two, active, delta_hidden, cot)
    mlp_send, moment_send = call(
        mlp_away_kernel,
        [((width + 16, hidden), BF16), ((rows, hidden), F32)],
        [],
        (after(info, far), *mlp_inputs, Late(mlp_moment)),
        2, 5,
    )
    (mlp_keep,) = call(
        mlp_here_kernel, [((width + 16, hidden), F32)], [], (after(info, mlp_send), *mlp_inputs), 1000, 8
    )
    mlp_came = swap(mlp_send, "dp", 1)
    moment_came = swap(moment_send, "dp", 1)
    came = swap(far, "tensor", 2)
    delta_mid, grad_gain_two = call(
        norm_back_kernel,
        [quarter_like, ((1, width), F32)],
        [],
        (after(info, mlp_keep), mine, came, cot, n_mine, inv_mine, gains),
        1000, 4,
    )
    (kernel_inverse_one,) = fetch(after(info, delta_mid), 0, kernel_inverse)
    out_near, out_kept = call(
        mlp_out_kernel,
        [Store((2, bucket, part), BF16), Store((2, bucket, part), F32)],
        [((bucket, width), F32)],
        (after(info, kernel_inverse_one), active, mlp_kept),
        1, 8,
    )
    delta_pieces = gather_tensor(delta_mid, kernel_inverse_one, out_near)

    pairs = dp // 2
    parities = [[i for i in range(dp) if i % 2 == y] for y in range(2)]
    groups = [[8 * z + q for q in range(8)] for z in range(pairs)]
    block = (2 * rows + 16, hidden)
    if dp == 8:
        blocks = call(mlp_rows_kernel, [(block, BF16)] * pairs, [], (info, mlp_keep, mlp_came), 0, 6)
        blocks = [blocks[0]] + [swap(blocks[k], "dp", 2 * k) for k in range(1, pairs)]
    else:
        (blocks,) = call(mlp_rows_kernel, [((pairs, *block), BF16)], [], (info, mlp_keep, mlp_came), 0, 6)
        blocks = [lax.all_to_all(blocks, "dp", 0, 0, tiled=True, axis_index_groups=parities)]

    piece = (pairs, 3 * rows + slot, part)
    slots_keep, slots_send, one_near, one_kept, delta_own, gain_part = call(
        mixer_back_kernel,
        [Bare(piece, piece_type), Bare(piece, piece_type), Store((2, bucket + 16, part), BF16),
         Store((2, bucket + 16, part), F32), Store((bucket, part), BF16), Store((8, part), F32)],
        [((2, *piece), piece_type), pltpu.SemaphoreType.DMA((2,)), whole_like, wide_like, spec_like, spec_like,
         ((8 * half, part), F32), ((bucket, 2 * part), BF16), ((bucket, width), F32)],
        (after(info, blocks[0]), *delta_pieces, in_weights, gate_act, gate_slope, conv, branch, normed, spec_v, spec_k, forward_one, inverse_one,
         kernel_inverse_one, gains, grad_gain_two),
        1000, 18,
    )
    slots_came = swap(slots_send.astype(BF16), "dp", 1).astype(piece_type)
    (slots,) = call(pair_sum_kernel, [Store(piece, piece_type)], [], (info, Late(slots_keep), Late(slots_came)), 0, 6)
    arrived = lax.all_to_all(slots.astype(BF16), "dp", 0, 0, tiled=True, axis_index_groups=parities)
    one_mine, one_tail, out_mine, far = call(
        join_late_kernel,
        [act_like, ((16, part), F32), act_like, ((2 * bucket + 16, part), BF16)],
        [],
        (info, Late(one_kept), swap(one_near, "tensor", 1), Late(out_kept), swap(out_near, "tensor", 1)),
        0, 6,
    )
    far_came = swap(far, "tensor", 2)
    pair, moment_mine, moment_other, count = call(
        mlp_moment_kernel,
        [((2 * rows, hidden), BF16), Store((rows, hidden), F32), Store((rows, hidden), F32), Store((8, part), F32)],
        [],
        (after(info, far), mlp_moment, moment_came, *blocks),
        1, 8,
    )
    if dp == 8:
        pair_pieces = [pair] + [swap(pair, "dp", 2 * k) for k in range(1, pairs)]
    else:
        pair_pieces = [lax.all_gather(pair, "dp", axis=0, tiled=True, axis_index_groups=parities)]
    height = -(-max(rows, slot + 16) // 16) * 16
    mixer_moment_new, slots = call(
        moment_kernel,
        [Store((3, rows, part), F32), Store((4 * dp, height, part), piece_type)],
        [],
        (info, arrived, Late(mixer_moment), Late(count), Late(gain_part)),
        0, 8,
    )
    got = lax.all_to_all(slots.astype(BF16), ("dp", "tensor"), 0, 0, tiled=True)
    (mlp_columns,) = call(
        columns_kernel, [((width, hidden), BF16)], [], (after(info, slots), *pair_pieces), 1000, 4
    )
    mlp_pieces = [mlp_columns] + [lax.ppermute(mlp_columns, "tensor", [(3 ^ k, 3)]) for k in (1, 2, 3)]
    moment_back = swap(moment_other, "dp", 1)
    input_grad, block_out = call(
        output_kernel,
        [Store(*act_like), Store((bucket, part), BF16)],
        [],
        (after(info, slots), one_mine, Late(far_came), out_mine, Late(delta_own), Late(n_own), Late(inv_one),
         Late(middle_own), Late(norm_gains), one_tail),
        0, 8,
    )
    (mlp_moment_new,) = call(
        aside_kernel, [Store((2, rows, hidden), F32)], [], (after(info, slots), Late(moment_mine), Late(moment_back)), 1, 4
    )
    square = ((width, width), F32)
    (sends,) = call(
        large_kernel,
        [Store((8, max(rows, 64), hidden), piece_type, True)],
        [square, square, ((2 * rows, width), F32)],
        (after(info, block_out, mlp_moment_new), *mlp_pieces),
        18, 24,
    )
    all_got = got
    sends = small_steps(after(info, sends), got, sends, rows, width, levels * taps)
    got = lax.all_to_all(sends.astype(BF16), ("dp", "tensor"), 0, 0, tiled=True, axis_index_groups=groups)
    (extra,) = call(
        functools.partial(extra_kernel, rows), [((64, 3 * part), BF16)], [((levels * taps, part), F32)],
        (after(info, sends), Late(all_got)), 0, 4,
    )
    flat = (levels * taps, part)
    old = fetch(
        after(info, extra), 0, mixer_weights, mlp_weights, norm_gains, gain_moment, conv_kernel.reshape(flat),
        kernel_moment.reshape(flat),
    )
    mixer_new, mlp_new, gain_moment_new, gains_new, kernel_moment_new, kernel_new = call(
        final_kernel,
        [Store((3, rows, part), F32), Store((2, rows, hidden), F32), ((2, width), F32), ((2, width), F32), (flat, F32),
         (flat, F32)],
        [((64, 3 * part), F32)],
        (info, got.astype(piece_type), extra, *old, Late(count)),
        0, 8,
    )
    kernel_moment_new, kernel_new = (v.reshape(conv_kernel.shape) for v in (kernel_moment_new, kernel_new))
    return (
        block_out[None],
        input_grad[None],
        gain_moment_new,
        gains_new,
        kernel_moment_new,
        kernel_new,
        mixer_moment_new,
        mixer_new,
        mlp_moment_new,
        mlp_new,
    )


def solution(mesh):
    tokens = P("dp", None, "tensor")
    columns = P(None, None, "tensor")
    blocks = P(None, "dp", "tensor")
    return jax.shard_map(
        per_device,
        mesh=mesh,
        in_specs=(tokens, tokens, P("dp"), P(), columns, columns, columns, P(), columns, blocks, blocks),
        out_specs=(tokens, tokens, P(), P(), columns, columns, blocks, blocks, blocks, blocks),
        check_vma=False,
    )
```

```python
import functools
import math

import jax
import jax.numpy as jnp
import ml_dtypes
import numpy as np
from jax import lax
from jax.experimental import pallas as pl
from jax.experimental.pallas import tpu as pltpu
from jax.sharding import PartitionSpec as P

NS_STEPS = 5
EPSILON = 1e-05
NS_COEF_A = 3.4445
NS_COEF_B = -4.775
NS_COEF_C = 2.0315
MOMENT_DECAY = 0.5
MATRIX_RATE = 1.0
GAIN_RATE = 0.1
KERNEL_RATE = 0.125
SCALE = 10**10
BF16 = jnp.bfloat16
F32 = jnp.float32


def conv_tables(bucket, levels, taps, dp, slot):
    half = bucket // 4
    size = 2 * half
    t = np.arange(half)
    k = np.arange(half)
    phase = 2 * np.pi * ((k[:, None] * t[None, :]) % size) / size
    forward = np.concatenate([np.cos(phase), -np.sin(phase)], 0)
    forward[half] = (-1.0) ** t
    scale = np.full((half,), 2.0 / size)
    scale[0] = 1.0 / size
    inverse = np.concatenate(
        [np.cos(phase).T * scale[None, :], -np.sin(phase).T * scale[None, :]], 1
    )
    inverse[:, half] = ((-1.0) ** t) / size
    spread = np.zeros((bucket, levels * taps))
    at = 0
    for level in range(levels):
        for tap in range(taps):
            width = 2**level
            spread[at : at + width, level * taps + tap] = 0.5**level
            at += width
    kernel_forward = np.concatenate(
        [forward @ spread[m * half : (m + 1) * half] for m in range(4)], 0
    )
    kernel_inverse = np.concatenate(
        [spread[m * half : (m + 1) * half].T @ inverse for m in range(4)], 1
    )
    share = -(-levels * taps // dp)
    kernel_inverse = np.pad(kernel_inverse, ((0, dp * share - levels * taps), (0, 0)))
    kernel_inverse = kernel_inverse.reshape(dp, share, -1)
    kernel_inverse = np.pad(kernel_inverse, ((0, 0), (0, slot - share), (0, 0))).reshape(dp * slot, -1)
    tables = []
    for table in (forward, inverse, kernel_forward, kernel_inverse):
        high = table.astype(ml_dtypes.bfloat16)
        low = (table - high.astype(np.float64)).astype(ml_dtypes.bfloat16)
        tables.append(np.stack([high, low]))
    return tables


def cross(a, b):
    return a[0] * b[0] - a[1] * b[1], a[0] * b[1] + a[1] * b[2]


def cross_conj(a, b):
    return a[0] * b[0] + a[1] * b[1], a[1] * b[2] - a[0] * b[1]


def with_edge(spec, first):
    real, imag = spec
    return real, jnp.where(first, 0.0, imag), jnp.where(first, imag, real)


def add_pairs(pairs):
    return functools.reduce(lambda p, q: (p[0] + q[0], p[1] + q[1]), pairs)


def spectral_blocks(left, right, conj, store):
    for step in range(4):
        rows = step * 64
        index = lax.broadcasted_iota(jnp.int32, (64, 128), 0)
        first = index + rows == 0
        sign = 1.0 - 2.0 * (index % 2).astype(F32)
        a = [left(r, rows) for r in range(4)]
        b = [with_edge(right(m, rows), first) for m in range(4)]
        if conj:
            sums = [add_pairs([cross_conj(a[r], b[r - q]) for r in range(q, 4)]) for q in range(4)]
        else:
            sums = [add_pairs([cross(a[r], b[q - r]) for r in range(q + 1)]) for q in range(4)]
        for q in range(4):
            other = q + 1 if conj else q - 1
            if 0 <= other < 4:
                real = sums[q][0] + sign * sums[other][0]
                imag = sums[q][1] + sign * sums[other][1]
            else:
                real, imag = sums[q]
            store(q, rows, real, imag)


def lane_pair(ref, half):
    return lambda r, rows: (
        ref[rows : rows + 64, r * 128 : (r + 1) * 128],
        ref[half + rows : half + rows + 64, r * 128 : (r + 1) * 128],
    )


def row_pair(ref, half):
    return lambda r, rows: (
        ref[2 * half * r + rows : 2 * half * r + rows + 64, :],
        ref[2 * half * r + half + rows : 2 * half * r + half + rows + 64, :],
    )


def gelu_both(x):
    c = math.sqrt(2.0 / math.pi)
    t = jnp.tanh(c * (x + 0.044715 * x * x * x))
    value = 0.5 * x * (1.0 + t)
    slope = 0.5 * (1.0 + t) + 0.5 * x * (1.0 - t * t) * (c * (1.0 + 3 * 0.044715 * x * x))
    return value, slope


def after(value, *others):
    return lax.optimization_barrier((value, *others))[0]


def swap(value, axis, k):
    size = lax.axis_size(axis)
    return lax.ppermute(value, axis, [(i, i ^ k) for i in range(size)])


def gather_tensor(value, *meanwhile):
    far = swap(value, "tensor", 2)
    near = swap(value, "tensor", 1)
    if meanwhile:
        far = after(far, *meanwhile)
    far_near = swap(far, "tensor", 1)
    return [value, near, far, far_near]


def gather_dp(value, me, low=0):
    size = lax.axis_size("dp")
    whole = value[None]
    while (1 << low) < size:
        bits = min(3, size.bit_length() - 1 - low)
        mine = (me >> low) & ((1 << bits) - 1)
        out = jnp.zeros((1 << bits,) + whole.shape, whole.dtype)
        for k in range(1 << bits):
            piece = whole if k == 0 else swap(whole, "dp", k << low)
            out = lax.dynamic_update_index_in_dim(out, piece, mine ^ k, 0)
        whole = out.reshape((-1,) + value.shape)
        low += bits
    return whole


def dot(a, b, contract):
    return lax.dot_general(a, b, ((contract[0], contract[1]), ((), ())), preferred_element_type=F32)


NN = ((1,), (0,))
NT = ((1,), (1,))
TN = ((0,), (0,))


def split(value):
    high = value.astype(BF16)
    return high, (value - high.astype(F32)).astype(BF16)


def table_dot(table, value):
    high, low = split(value)
    return dot(table[0], high, NN) + (dot(table[1], high, NN) + dot(table[0], low, NN))


def symmetric(left, right, product):
    half = left[0].shape[0] // 2
    top = product([v[:half] for v in left], right, None)
    low = product([v[half:] for v in left], right, half)
    return jnp.concatenate([top, jnp.concatenate([top[:, half:].T, low], 1)], 0)


def three_terms(left, right, cut=None):
    right = right if cut is None else [v[:, cut:] for v in right]
    left = jnp.concatenate([left[0], left[0], left[1]], 1)
    return dot(left, jnp.concatenate([right[0], right[1], right[0]], 0), NN)


def newton_schulz(blocks, a_ref, p_ref, r_ref, start):
    size = a_ref.shape[0]
    row = lax.broadcasted_iota(jnp.int32, (size, size), 0)
    col = lax.broadcasted_iota(jnp.int32, (size, size), 1)
    unit = (row == col).astype(F32)
    blocks = [block() for block in blocks]
    gram = 0.0
    for block in blocks:
        gram = gram + symmetric([block], [block], lambda a, b, cut: dot(a[0], b[0] if cut is None else b[0][cut:], NT))
    scale = 1.0 / (jnp.sqrt(jnp.sum(gram * unit)) + 1e-07)
    a_ref[...] = gram * (scale * scale)

    def advance(first):
        a = a_ref[...]
        terms = split(a)
        poly = NS_COEF_A * unit + NS_COEF_B * a + NS_COEF_C * symmetric(terms, terms, three_terms)
        poly_terms = split(poly)
        if first:
            p_ref[...] = poly
            r_ref[...] = p_ref[pl.ds(start, r_ref.shape[0]), :]
        else:
            r_ref[...] = three_terms(split(r_ref[...]), poly_terms)
        half = symmetric(terms, poly_terms, three_terms)
        a_ref[...] = symmetric(poly_terms, split(half), three_terms)

    advance(True)
    pl.loop(0, NS_STEPS - 2)(lambda _: advance(False))
    rows, terms = r_ref[...], split(a_ref[...])
    once = three_terms(split(rows), terms)
    rows = NS_COEF_A * rows + NS_COEF_B * once + NS_COEF_C * three_terms(split(once), terms)
    high, low = split(rows)
    return [scale * (dot(high, block, NN) + dot(low, block, NN)) for block in blocks]


VMEM = pl.BlockSpec(memory_space=pltpu.VMEM)
SMEM = pl.BlockSpec(memory_space=pltpu.SMEM)


HBM = pl.BlockSpec(memory_space=pltpu.HBM)


class Late:
    def __init__(self, array):
        self.shape, self.dtype = array.shape, array.dtype
        self.array = pltpu.with_memory_space_constraint(array, pltpu.HBM)


class Store:
    def __init__(self, shape, dtype, own=False):
        self.shape, self.dtype, self.own = shape, dtype, own


class Waiting:
    def __init__(self, copy, ref):
        self.copy, self.ref, self.started = copy, ref, False

    def ready(self):
        self.copy.wait()
        return self.ref

    def send(self):
        self.copy.start()
        self.started = True


def call(kernel, outs, scratch, args, time, limit):
    outs = [o if isinstance(o, Store) else jax.ShapeDtypeStruct(*o) for o in outs]
    late = [a for a in (*args, *outs) if isinstance(a, (Late, Store))]
    n_in, n_out = len(args), len(outs)

    def body(*refs):
        given, rest = refs[: n_in + n_out], refs[n_in + n_out :]
        buffers, rest = rest[: len(late)], rest[len(late) :]
        semaphores = rest[-1] if late else None
        passed, stores, at = [], [], 0
        for what, ref in zip((*args, *outs), given):
            if isinstance(what, Late):
                copy = pltpu.make_async_copy(ref, buffers[at], semaphores.at[at])
                copy.start()
            elif isinstance(what, Store):
                copy = pltpu.make_async_copy(buffers[at], ref, semaphores.at[at])
            else:
                passed.append(ref)
                continue
            passed.append(Waiting(copy, buffers[at]))
            if isinstance(what, Store) and not what.own:
                stores.append(passed[-1])
            at += 1
        kernel(*passed, *(rest[:-1] if late else rest))
        for store in stores:
            if not store.started:
                store.send()
        for store in stores:
            store.copy.wait()

    return pl.pallas_call(
        body,
        out_shape=tuple(pltpu.HBM(o.shape, o.dtype) if isinstance(o, Store) else o for o in outs),
        in_specs=[SMEM] + [HBM if isinstance(a, Late) else VMEM for a in args[1:]],
        out_specs=tuple(HBM if isinstance(o, Store) else VMEM for o in outs),
        scratch_shapes=[pltpu.VMEM(a.shape, a.dtype) for a in late]
        + [pltpu.VMEM(*what) if isinstance(what, tuple) else what for what in scratch]
        + ([pltpu.SemaphoreType.DMA((len(late),))] if late else []),
        compiler_params=pltpu.CompilerParams(vmem_limit_bytes=limit * 2**20),
        cost_estimate=pl.CostEstimate(flops=max(time * SCALE, 10**6), bytes_accessed=0, transcendentals=0),
    )(*(a.array if isinstance(a, Late) else a for a in args))


def fetch(token, time, *arrays):
    arrays = [a if isinstance(a, list) else [(a, None)] for a in arrays]
    shapes = []
    for a in arrays:
        cuts = [p.shape if index is None else p.shape[1:] for p, index in a]
        shapes.append(jax.ShapeDtypeStruct((sum(c[0] for c in cuts), *cuts[0][1:]), a[0][0].dtype))
    flat = [pltpu.with_memory_space_constraint(p, pltpu.HBM) for a in arrays for p, _ in a]

    def body(token_ref, *refs):
        outs, semaphores, copies, at = refs[len(flat) : -1], refs[-1], [], 0
        for a, out in zip(arrays, outs):
            row = 0
            for _, index in a:
                source = refs[at] if index is None else refs[at].at[index]
                target = out if len(a) == 1 else out.at[row : row + source.shape[0]]
                copies.append(pltpu.make_async_copy(source, target, semaphores.at[at]))
                copies[-1].start()
                row, at = row + source.shape[0], at + 1
        for copy in copies:
            copy.wait()

    return pl.pallas_call(
        body,
        out_shape=tuple(shapes),
        in_specs=[SMEM] + [HBM] * len(flat),
        out_specs=(VMEM,) * len(shapes),
        scratch_shapes=[pltpu.SemaphoreType.DMA((len(flat),))],
        compiler_params=pltpu.CompilerParams(vmem_limit_bytes=2 * 2**20),
        cost_estimate=pl.CostEstimate(flops=max(time * SCALE, 10**6), bytes_accessed=0, transcendentals=0),
    )(token, *flat)


def block_at(index, size):
    return pl.ds(pl.multiple_of(index * size, size), size)


def row_mask(info, start, rows):
    return (start + lax.broadcasted_iota(jnp.int32, (rows, 1), 0) < info[1]).astype(F32)


def spectrum_kernel(info, table, taps, spec_k):
    taps = taps.ready()[...]
    spec_k[...] = table_dot(table.ready(), taps)


def entry_kernel(info, p0, p1, p2, p3, weights, gains, forward, inverse, spec_k,
                 x, normed, n_own, inv, spec_v, conv, act, slope, branch, gains_kept, wide, spec_y):
    me = info[0]
    part = p1.shape[1]
    for k, piece in enumerate((p0, p1, p2, p3)):
        x[:, block_at(me ^ k, part)] = piece[...]
    gains_kept[...] = gains[...]
    gain = gains[0:1, :]
    half = x.shape[0] // 4
    for c in range(4):
        r = slice(c * half, (c + 1) * half)
        v = x[r, :].astype(F32)
        mean = jnp.mean(v, 1, keepdims=True)
        centred = v - mean
        scale = lax.rsqrt(jnp.mean(centred * centred, 1, keepdims=True) + EPSILON)
        normed[r, :] = (centred * scale * gain).astype(BF16)
        inv.ref[r, :] = scale
        n_own.ref[r, :] = (p0[r, :].astype(F32) - mean) * scale
    n_own.send()
    inv.send()
    for c in range(4):
        r = slice(c * half, (c + 1) * half)
        normal = normed[r, :]
        wide[:, c * part : (c + 1) * part] = dot(normal, weights[0], NN)
        act[r, :], slope[r, :] = gelu_both(dot(normal, weights[1], NN))
    spec_v[...] = table_dot(forward, wide[...])

    def store(q, rows, real, imag):
        spec_y[rows : rows + 64, q * part : (q + 1) * part] = real
        spec_y[half + rows : half + rows + 64, q * part : (q + 1) * part] = imag

    spectral_blocks(lane_pair(spec_v, half), row_pair(spec_k, half), False, store)
    wide[...] = table_dot(inverse, spec_y[...])
    for c in range(4):
        r = slice(c * half, (c + 1) * half)
        out = wide[:, c * part : (c + 1) * part]
        conv[r, :] = out
        out = (act[r, :] * out * row_mask(info, c * half, half)).astype(BF16)
        branch[r, :] = out


def cotangent_kernel(info, p0, p1, p2, p3, weights, cot, out_w, delta, weights_kept):
    part = p0.shape[1]
    for k, piece in enumerate((p0, p1, p2, p3)):
        cot[:, block_at(info[0] ^ k, part)] = piece[: cot.shape[0], :]
        out_w[:, block_at(info[0] ^ k, part)] = piece[cot.shape[0] :, :]
    step = cot.shape[0] // 4
    weights = weights.ready()
    weights_kept[...] = weights[...]
    for c in range(4):
        r = slice(c * step, (c + 1) * step)
        delta[r, :] = dot(cot[r, :], weights[1], NN)


def middle_kernel(info, b0, b1, b2, b3, out_w, x, gains, weights, delta_active,
                  near, kept, normed, active, delta_hidden, n_mine, inv_mine, middle_own, branch, middle):
    me = info[0]
    part = b0.shape[1]
    step = x.shape[0] // 4
    for k, piece in enumerate((b0, b1, b2, b3)):
        branch[:, block_at(me ^ k, part)] = piece[...]
    gain = gains[1:2, :]
    for k in (1, 3, 0, 2):
        block = me ^ k
        r = block_at(block, step)
        mid = x[r, :].astype(F32) + dot(branch[r, :], out_w[...], NT)
        middle[r, :] = mid
        centred = mid - jnp.mean(mid, 1, keepdims=True)
        scale = lax.rsqrt(jnp.mean(centred * centred, 1, keepdims=True) + EPSILON)
        normal = centred * scale
        if k == 0:
            n_mine[...] = normal
            inv_mine[...] = scale
        normal = (normal * gain).astype(BF16)
        normed[r, :] = normal
        value, slope = gelu_both(dot(normal, weights[0], NN))
        mask = row_mask(info, block * step, step)
        active[r, :] = (value * mask).astype(BF16)
        back = (delta_active[r, :] * mask * slope).astype(BF16)
        delta_hidden[r, :] = back
        share = dot(back, weights[0], NT)
        if k % 2:
            near[(k // 2) * step : (k // 2 + 1) * step, :] = share.astype(BF16)
        else:
            kept[(k // 2) * step : (k // 2 + 1) * step, :] = share
    middle_own.ref[...] = middle[:, block_at(me, part)]


def mlp_kernel(info, normed, active, delta_hidden, cot, moment, out, moment_send, away):
    size = normed.shape[1]
    wanted = (info[2] + away) % 2

    @pl.when(wanted == 0)
    def _():
        out[:size, :] = dot(normed[...], delta_hidden[...], TN).astype(out.dtype)

    @pl.when(wanted == 1)
    def _():
        out[:size, :] = dot(cot[...], active[...], TN).astype(out.dtype)

    length = jnp.full((16, out.shape[1]), 1, jnp.int32) * info[1]
    first = lax.broadcasted_iota(jnp.int32, length.shape, 0) == 0
    out[size:, :] = jnp.where(first, length // 32, length % 32).astype(F32).astype(out.dtype)
    if away:
        moment_send[...] = moment.ready()[wanted]


def mlp_away_kernel(info, normed, active, delta_hidden, cot, moment, out, moment_send):
    mlp_kernel(info, normed, active, delta_hidden, cot, moment, out, moment_send, 1)


def mlp_here_kernel(info, normed, active, delta_hidden, cot, out):
    mlp_kernel(info, normed, active, delta_hidden, cot, None, out, None, 0)


def mlp_out_kernel(info, active, weights, near, kept, part_out):
    me = info[0]
    step = active.shape[0] // 4
    part = near.ref.shape[2]
    for c in range(4):
        r = slice(c * step, (c + 1) * step)
        part_out[r, :] = dot(active[r, :], weights[1], NT)
    for k in range(4):
        share = part_out[:, block_at(me ^ k, part)]
        if k % 2:
            near.ref[k // 2] = share.astype(BF16)
        else:
            kept.ref[k // 2] = share


def mlp_rows_kernel(info, keep, came, *outs):
    size = came.shape[0] - 16
    pairs = outs[0].shape[0] if len(outs) == 1 else len(outs)
    rows = size // pairs
    length = keep[size:, :] + came[size:, :].astype(F32)
    for k in range(pairs):
        if len(outs) == 1:
            r, out = pl.ds(k * rows, rows), outs[0].at[k]
        else:
            r, out = block_at((info[2] // 2) ^ k, rows), outs[k]
        out[:rows, :] = (keep[r, :] + came[r, :].astype(F32)).astype(out.dtype)
        out[rows:, :] = length.astype(out.dtype)


def mlp_moment_kernel(info, moment, other_moment, *refs):
    *pieces, matrix, mine, other, count = refs
    rows = moment.shape[1]
    side = info[2] % 2
    if len(pieces) == 1:
        pieces = [pieces[0].at[k] for k in range(pieces[0].shape[0])]
    total = pieces[0][...].astype(F32)
    for piece in pieces[1:]:
        total = total + piece[...].astype(F32)
    tokens = 32.0 * total[2 * rows : 2 * rows + 1, :] + total[2 * rows + 1 : 2 * rows + 2, :]
    count.ref[...] = jnp.broadcast_to(tokens[:, : count.ref.shape[1]], count.ref.shape)
    old = moment[side]
    for which in range(2):
        new = total[which * rows : (which + 1) * rows, :] / tokens

        @pl.when(side == which)
        def _(new=new, which=which):
            now = MOMENT_DECAY * old + new
            mine.ref[...] = now
            matrix[which * rows : (which + 1) * rows, :] = now.astype(matrix.dtype)

        @pl.when(side != which)
        def _(new=new, which=which):
            now = MOMENT_DECAY * other_moment[...] + new
            other.ref[...] = now
            matrix[which * rows : (which + 1) * rows, :] = now.astype(matrix.dtype)


def columns_kernel(info, *refs):
    *pieces, out = refs
    rows = pieces[0].shape[0]
    for k, piece in enumerate(pieces):
        out[block_at((info[2] // 2) ^ k, rows), :] = piece[...]


def join_kernel(info, kept, came, mine, far):
    mine[...] = kept[0] + came[0].astype(F32)
    far[...] = (kept[1] + came[1].astype(F32)).astype(BF16)


def join_late_kernel(info, one_kept, one_came, out_kept, out_came, one_mine, tail, out_mine, far):
    one_kept, out_kept = one_kept.ready(), out_kept.ready()
    size = out_mine.shape[0]
    one_mine[...] = one_kept[0, :size, :] + one_came[0, :size, :].astype(F32)
    tail[...] = one_kept[0, size:, :] + one_came[0, size:, :].astype(F32)
    far[: size + 16, :] = (one_kept[1] + one_came[1].astype(F32)).astype(BF16)
    out_mine[...] = out_kept[0] + out_came[0].astype(F32)
    far[size + 16 :, :] = (out_kept[1] + out_came[1].astype(F32)).astype(BF16)


def norm_back_kernel(info, mine, came, cot, n_mine, inv_mine, gains, delta, grad_gain):
    size = mine.shape[0]
    total = mine[...] + came[...].astype(F32)
    n = n_mine[...]
    q = total * gains[1:2, :]
    back = inv_mine[...] * (q - jnp.mean(q, 1, keepdims=True) - n * jnp.mean(q * n, 1, keepdims=True))
    delta[...] = (cot[block_at(info[0], size), :].astype(F32) + back).astype(BF16)
    grad_gain[...] = jnp.sum(total * n, 0, keepdims=True)


def mixer_back_kernel(info, d0, d1, d2, d3, weights, act, slope, conv, branch, normed, spec_v, spec_k, forward, inverse,
                      kernel_inverse, gains, gain_two,
                      keep, send, near, kept, delta_own, gain_part,
                      slots, semaphores, delta, wide, spec_d, spec_y, spec_u, back, share):
    me = info[0]
    step, width = d0.shape
    part = slots.shape[3]
    half = step
    for k, piece in enumerate((d0, d1, d2, d3)):
        block = me ^ k
        r = block_at(block, step)
        delta[r, :] = piece[...]
        down = dot(piece[...], weights[2], NN) * row_mask(info, block * step, step)
        back[r, part:] = (down * conv[r, :] * slope[r, :]).astype(BF16)
        wide[:, block_at(block, part)] = down * act[r, :]
    delta_own.ref[...] = delta[:, block_at(me, part)]
    delta_own.send()
    spec_d[...] = table_dot(forward, wide[...])

    def store(q, rows, real, imag):
        spec_y[rows : rows + 64, q * part : (q + 1) * part] = real
        spec_y[half + rows : half + rows + 64, q * part : (q + 1) * part] = imag

    def store_rows(q, rows, real, imag):
        spec_u[2 * half * q + rows : 2 * half * q + rows + 64, :] = real
        spec_u[2 * half * q + half + rows : 2 * half * q + half + rows + 64, :] = imag

    spectral_blocks(lane_pair(spec_d, half), row_pair(spec_k, half), True, store)
    wide[...] = table_dot(inverse, spec_y[...])
    for c in range(4):
        back[c * half : (c + 1) * half, :part] = wide[:, c * part : (c + 1) * part].astype(BF16)
    spectral_blocks(lane_pair(spec_d, half), lane_pair(spec_v, half), True, store_rows)
    grad_kernel = table_dot(kernel_inverse, spec_u[...])
    grads = dot(normed[...], back[...], TN)
    grad_out = dot(delta[...], branch[...], TN)
    dp = 2 * slots.shape[1]
    rows = width // dp
    taps = grad_kernel.shape[0] // dp
    for i in range(dp):
        r = slice(i * rows, (i + 1) * rows)
        slots[i % 2, i // 2, :rows, :] = grads[r, :part].astype(slots.dtype)
        slots[i % 2, i // 2, rows : 2 * rows, :] = grads[r, part:].astype(slots.dtype)
        slots[i % 2, i // 2, 2 * rows : 3 * rows, :] = grad_out[r, :].astype(slots.dtype)
        slots[i % 2, i // 2, 3 * rows :, :] = grad_kernel[i * taps : (i + 1) * taps, :].astype(slots.dtype)
    side = info[2] % 2
    copies = [
        pltpu.make_async_copy(slots.at[side], keep, semaphores.at[0]),
        pltpu.make_async_copy(slots.at[1 - side], send, semaphores.at[1]),
    ]
    for copy in copies:
        copy.start()
    ones = jnp.ones((8, width), BF16)
    gain_one = jnp.zeros((1, width), F32)
    sums = [[], []]
    gain = jnp.broadcast_to(gains[0:1, :], (8, width)).astype(BF16)
    for c in range(4):
        r = slice(c * step, (c + 1) * step)
        out = dot(back[r, :part], weights[0], NT) + dot(back[r, part:], weights[1], NT)
        share[r, :] = out
        first = dot(gain, out.astype(BF16), NT)
        both = out * normed[r, :].astype(F32)
        gain_one = gain_one + jnp.sum(both, 0, keepdims=True)
        second = dot(ones, both.astype(BF16), NT)
        for h in range(step // part):
            sums[0].append(first[0:1, h * part : (h + 1) * part])
            sums[1].append(second[0:1, h * part : (h + 1) * part])
    gain_one = gain_one / gains[0:1, :]
    gain = [g[:, q * part : (q + 1) * part] for g in (gain_one, gain_two[...]) for q in range(4)]
    gain_part.ref[...] = jnp.concatenate(gain, 0)
    tail = jnp.concatenate([*sums[0], *sums[1]], 0)
    for k in range(4):
        block = share[:, block_at(me ^ k, part)]
        if k % 2:
            near.ref[k // 2, : share.shape[0], :] = block.astype(BF16)
            near.ref[k // 2, share.shape[0] :, :] = tail.astype(BF16)
        else:
            kept.ref[k // 2, : share.shape[0], :] = block
            kept.ref[k // 2, share.shape[0] :, :] = tail
    for copy in copies:
        copy.wait()


def pair_sum_kernel(info, keep, came, out):
    for z in range(keep.shape[0]):
        out.ref[z] = (keep[z].astype(F32) + came[z].astype(F32)).astype(out.ref.dtype)


def keeper(t):
    return 4 * (1 - t // 2) + t


def moment_kernel(info, arrived, moment, count, gain_part, moment_new, slots):
    me = info[0]
    pairs = arrived.shape[0]
    _, rows, part = moment.ref.shape
    taps = arrived.shape[1] - 3 * rows
    total = arrived[0].astype(F32)
    for i in range(1, pairs):
        total = total + arrived[i].astype(F32)
    high, low = split(gain_part.ready()[...])
    rest = jnp.concatenate([total[3 * rows :, :], high.astype(F32), low.astype(F32)], 0).astype(slots.ref.dtype)
    moment, count = moment.ready(), count.ready()
    for which in range(3):
        value = MOMENT_DECAY * moment[which] + total[which * rows : (which + 1) * rows, :] / count[0:1, :]
        moment_new.ref[which] = value
        for z in range(pairs):
            slots.ref[8 * z + keeper(which), :rows, :] = value.astype(slots.ref.dtype)
    for t in range(4):
        for z in range(pairs):
            slots.ref[8 * z + (keeper(t) ^ 4), : taps + 16, :] = rest
            if t == 3:
                slots.ref[8 * z + keeper(t), : taps + 16, :] = rest
    slots.send()


def output_kernel(info, mine, came, out_mine, delta_own, n_own, inv, middle_own, gains, tail, input_grad, block_out):
    part = mine.shape[1]
    came = came.ready()
    gain = gains.ready()[0:1, block_at(info[0], part)]
    size = mine.shape[0]
    sums = (tail[...] + came[size : size + 16, :].astype(F32)) / (4 * part)
    middle_own = middle_own.ready()
    n_own, inv, delta_own = n_own.ready(), inv.ready(), delta_own.ready()
    for h in range(mine.shape[0] // part):
        r = slice(h * part, (h + 1) * part)
        block_out.ref[r, :] = (middle_own[r, :] + (out_mine[r, :] + came[size + 16 + h * part : size + 16 + (h + 1) * part, :].astype(F32))).astype(BF16)
        column = lambda at: jnp.broadcast_to(sums[at : at + 1, :], (part, part)).T
        total = mine[r, :] + came[r, :].astype(F32)
        back = total * gain - column(h) - n_own[r, :] * column(8 + h)
        input_grad.ref[r, :] = delta_own[r, :].astype(F32) + inv[r, :] * back


def large_kernel(info, m0, m1, m2, m3, out, a, p, r):
    me, row = info[0], info[2]
    rows = r.shape[0] // 2

    @pl.when(me == 3)
    def _():
        start = pl.multiple_of((row // 2) * (2 * rows), 2 * rows)
        blocks = [lambda piece=piece: piece[...] for piece in (m0, m1, m2, m3)]
        for k, steps in enumerate(newton_schulz(blocks, a, p, r, start)):
            for y in range(2):
                out.ref[4 * y + (3 ^ k), :rows, :] = steps[y * rows : (y + 1) * rows, :].astype(out.ref.dtype)
        out.send()
        out.copy.wait()


def gather_extra(got, me, rows, packed, extra):
    total, dp = packed.shape[0], got.shape[0] // 4
    part = packed.shape[1]
    share = -(-total // dp)
    taps = -(-share // 8) * 8
    taps += (3 * rows + taps) % 16
    gain = 0.0
    for i in range(dp):
        both = got[4 * i + me, : taps + 16, :].astype(F32)
        count = min(share, total - i * share)
        if count > 0:
            packed[i * share : i * share + count, :] = both[:count, :]
        for t in range(4):
            both = got[4 * i + t, taps : taps + 16, :].astype(F32)
            gain = gain + (both[:8, :] + both[8:, :])
    high, low = split(gain)
    extra[...] = jnp.zeros_like(extra)
    for g in range(-(-total // 64)):
        count = min(64, total - 64 * g)
        extra[:count, g * part : (g + 1) * part] = packed[64 * g : 64 * g + count, :].astype(extra.dtype)
    at = (total // 64) * part
    extra[32:48, at : at + part] = jnp.concatenate([high.astype(F32), low.astype(F32)], 0).astype(extra.dtype)


def small_kernel(info, source, slots, out, got, extra, matrix, a, p, r, packed, steps, semaphore):
    me, row = info[0], info[2]
    side = row % 2
    size, width = matrix.shape
    rows = r.shape[0] // 2
    part = width // 4
    start = pl.multiple_of((row // 2) * (2 * rows), 2 * rows)
    keeps = jnp.logical_and(side == 1 - me // 2, me < 3)

    @pl.when(me < 3)
    def _():
        arrive = pltpu.make_async_copy(source, got, semaphore.at[2])
        arrive.start()
        arrive.wait()

        @pl.when(keeps)
        def _():
            for i in range(size // rows):
                for t in range(4):
                    matrix[i * rows : (i + 1) * rows, t * part : (t + 1) * part] = got[4 * i + t, :rows, :].astype(BF16)
            (result,) = newton_schulz([lambda: matrix[...]], a, p, r, start)
            for q in range(8):
                lanes = slice((q % 4) * part, (q % 4 + 1) * part)
                steps[q] = result[(q // 4) * rows : (q // 4 + 1) * rows, lanes].astype(steps.dtype)
            copy = pltpu.make_async_copy(steps, out.at[:, pl.ds(0, rows), pl.ds(0, part)], semaphore.at[0])
            copy.start()
            copy.wait()

        @pl.when(jnp.logical_not(keeps))
        def _():
            gather_extra(got, me, rows, packed, extra)
            copies = [
                pltpu.make_async_copy(extra, out.at[4 * y + me, pl.ds(0, 64), pl.ds(0, 3 * part)], semaphore.at[y])
                for y in range(2)
            ]
            for copy in copies:
                copy.start()
            for copy in copies:
                copy.wait()


def small_steps(info, got, slots, rows, width, taps):
    part = width // 4
    square = pltpu.VMEM((width, width), F32)
    return pl.pallas_call(
        small_kernel,
        out_shape=pltpu.HBM(slots.shape, slots.dtype),
        in_specs=[SMEM, HBM, HBM],
        out_specs=HBM,
        scratch_shapes=[
            pltpu.VMEM(got.shape, got.dtype), pltpu.VMEM((64, 3 * part), slots.dtype), pltpu.VMEM((width, width), BF16), square,
            square, pltpu.VMEM((2 * rows, width), F32), pltpu.VMEM((taps, part), F32), pltpu.VMEM((8, rows, part), slots.dtype),
            pltpu.SemaphoreType.DMA((3,)),
        ],
        input_output_aliases={2: 0},
        compiler_params=pltpu.CompilerParams(vmem_limit_bytes=24 * 2**20),
        cost_estimate=pl.CostEstimate(flops=18 * SCALE, bytes_accessed=0, transcendentals=0),
    )(info, pltpu.with_memory_space_constraint(got, pltpu.HBM), pltpu.with_memory_space_constraint(slots, pltpu.HBM))


def extra_kernel(rows, info, got, extra, packed):
    gather_extra(got.ready(), info[0], rows, packed, extra)


def aside_kernel(info, moment_mine, moment_back, moment_new):
    side = info[2] % 2
    moment_new.ref[side] = moment_mine.ready()[...]
    moment_new.ref[1 - side] = moment_back.ready()[...]


def final_kernel(info, got, extra_mine, mixer_weights, mlp_weights, norm_gains, gain_moment, taps, taps_moment, count,
                 mixer_new, mlp_new, gain_moment_new, gains_new, taps_moment_new, taps_new, extra):
    me, row = info[0], info[2]
    count = count.ready()
    _, rows, part = mixer_new.ref.shape
    hidden = mlp_new.ref.shape[2]
    width = 4 * part
    for t in range(3):
        old = mixer_weights[t, block_at(row, rows), :].astype(F32)
        mixer_new.ref[t] = old - MATRIX_RATE * got[keeper(t), :rows, :part].astype(F32)
    mixer_new.send()
    rate = MATRIX_RATE * math.sqrt(4 * hidden / width)
    for which in range(2):
        old = mlp_weights[which, block_at(row, rows), :].astype(F32)
        mlp_new.ref[which] = old - rate * got[4 * which + 3, :rows, :].astype(F32)
    mlp_new.send()
    @pl.when(me == 3)
    def _():
        extra[...] = extra_mine[...].astype(F32)

    @pl.when(me != 3)
    def _():
        extra[...] = got[keeper(me) ^ 4, :64, : 3 * part].astype(F32)

    total = taps.shape[0]
    grad = [extra[: min(64, total - 64 * g), g * part : (g + 1) * part] for g in range(-(-total // 64))]
    at = (total // 64) * part
    gain = extra[32:40, at : at + part] + extra[40:48, at : at + part]
    new = MOMENT_DECAY * taps_moment[...] + jnp.concatenate(grad, 0) / count[0:1, :]
    taps_moment_new[...] = new
    scale = jnp.sqrt(jnp.mean(new * new, 0, keepdims=True)) + 1e-08
    taps_new[...] = taps[...] - KERNEL_RATE * new / scale
    for which in range(2):
        for t in range(4):
            lanes = slice(t * part, (t + 1) * part)
            gain_moment_new[which : which + 1, lanes] = (
                MOMENT_DECAY * gain_moment[which : which + 1, lanes]
                + gain[4 * which + t : 4 * which + t + 1, :] / count[0:1, :]
            )
    new = gain_moment_new[...]
    scale = jnp.sqrt(jnp.mean(new * new, 1, keepdims=True)) + 1e-08
    gains_new[...] = norm_gains[...] - GAIN_RATE * new / scale


def per_device(
    tokens,
    cotangent,
    lengths,
    norm_gains,
    conv_kernel,
    mixer_weights,
    mlp_weights,
    gain_moment,
    kernel_moment,
    mixer_moment,
    mlp_moment,
):
    _, bucket, part = tokens.shape
    levels, taps, _ = conv_kernel.shape
    hidden = mlp_weights.shape[2]
    me = lax.axis_index("tensor")
    row = lax.axis_index("dp")
    dp = lax.axis_size("dp")
    width = 4 * part
    rows = width // dp
    half = bucket // 4
    piece_type = BF16 if rows % 16 == 0 else F32
    share = -(-levels * taps // dp)
    slot = -(-share // 8) * 8
    slot += (3 * rows + slot) % 16
    forward, inverse, kernel_forward, kernel_inverse = conv_tables(bucket, levels, taps, dp, slot)
    info = jnp.stack([me, lengths[0], row]).astype(jnp.int32)

    x_own, in_weights, in_gains, forward_one, inverse_one, late = fetch(
        info, 1, tokens[0], mixer_weights, norm_gains, forward, inverse, [(cotangent, 0), (mixer_weights, 2)]
    )
    (spec_k,) = call(
        spectrum_kernel,
        [((8 * half, part), F32)],
        [],
        (after(info, x_own), Late(kernel_forward), Late(conv_kernel.reshape(levels * taps, part))),
        2, 10,
    )
    x_pieces = gather_tensor(tokens[0], spec_k, x_own)

    act_like = ((bucket, part), F32)
    wide_like = ((half, width), F32)
    spec_like = ((2 * half, width), F32)
    whole_like = ((bucket, width), BF16)
    quarter_like = ((half, width), BF16)
    x, normed, n_own, inv_one, spec_v, conv, gate_act, gate_slope, branch, gains = call(
        entry_kernel,
        [whole_like, whole_like, Store(*act_like), Store((bucket, 1), F32), spec_like, act_like, act_like, act_like,
         ((bucket, part), BF16), ((2, width), F32)],
        [wide_like, spec_like],
        (info, x_own, *x_pieces[1:], in_weights, in_gains, forward_one, inverse_one, spec_k),
        0, 12,
    )
    late = gather_tensor(late, branch)
    cot, out_weights, delta_active, mlp_kept = call(
        cotangent_kernel,
        [whole_like, ((width, width), BF16), ((bucket, hidden), F32), (mlp_weights.shape, BF16)],
        [],
        (after(info, branch), *late, Late(mlp_weights)),
        3, 5,
    )
    branch_pieces = gather_tensor(branch, delta_active)
    near, kept, normed_two, active, delta_hidden, n_mine, inv_mine, middle_own = call(
        middle_kernel,
        [((width, width), BF16), ((width, width), F32), whole_like, ((bucket, hidden), BF16),
         ((bucket, hidden), BF16), wide_like, ((half, 1), F32), Store(*act_like)],
        [whole_like, ((bucket, width), F32)],
        (info, *branch_pieces, out_weights, x, gains, mlp_kept, delta_active),
        6, 12,
    )
    split_blocks = lambda v: v.reshape(2, -1, v.shape[-1])
    came = swap(split_blocks(near), "tensor", 1)
    mine, far = call(join_kernel, [wide_like, quarter_like], [], (info, split_blocks(kept), came), 1, 4)
    mlp_inputs = (normed_two, active, delta_hidden, cot)
    mlp_send, moment_send = call(
        mlp_away_kernel,
        [((width + 16, hidden), BF16), ((rows, hidden), F32)],
        [],
        (after(info, far), *mlp_inputs, Late(mlp_moment)),
        2, 5,
    )
    (mlp_keep,) = call(
        mlp_here_kernel, [((width + 16, hidden), F32)], [], (after(info, mlp_send), *mlp_inputs), 1000, 8
    )
    mlp_came = swap(mlp_send, "dp", 1)
    moment_came = swap(moment_send, "dp", 1)
    came = swap(far, "tensor", 2)
    delta_mid, grad_gain_two = call(
        norm_back_kernel,
        [quarter_like, ((1, width), F32)],
        [],
        (after(info, mlp_keep), mine, came, cot, n_mine, inv_mine, gains),
        1000, 4,
    )
    (kernel_inverse_one,) = fetch(after(info, delta_mid), 0, kernel_inverse)
    out_near, out_kept = call(
        mlp_out_kernel,
        [Store((2, bucket, part), BF16), Store((2, bucket, part), F32)],
        [((bucket, width), F32)],
        (after(info, kernel_inverse_one), active, mlp_kept),
        1, 8,
    )
    delta_pieces = gather_tensor(delta_mid, kernel_inverse_one, out_near)

    pairs = dp // 2
    parities = [[i for i in range(dp) if i % 2 == y] for y in range(2)]
    groups = [[8 * z + q for q in range(8)] for z in range(pairs)]
    block = (2 * rows + 16, hidden)
    if dp == 8:
        blocks = call(mlp_rows_kernel, [(block, BF16)] * pairs, [], (info, mlp_keep, mlp_came), 0, 6)
        blocks = [blocks[0]] + [swap(blocks[k], "dp", 2 * k) for k in range(1, pairs)]
    else:
        (blocks,) = call(mlp_rows_kernel, [((pairs, *block), BF16)], [], (info, mlp_keep, mlp_came), 0, 6)
        blocks = [lax.all_to_all(blocks, "dp", 0, 0, tiled=True, axis_index_groups=parities)]

    piece = (pairs, 3 * rows + slot, part)
    slots_keep, slots_send, one_near, one_kept, delta_own, gain_part = call(
        mixer_back_kernel,
        [(piece, piece_type), (piece, piece_type), Store((2, bucket + 16, part), BF16),
         Store((2, bucket + 16, part), F32), Store((bucket, part), BF16), Store((8, part), F32)],
        [((2, *piece), piece_type), pltpu.SemaphoreType.DMA((2,)), whole_like, wide_like, spec_like, spec_like,
         ((8 * half, part), F32), ((bucket, 2 * part), BF16), ((bucket, width), F32)],
        (after(info, blocks[0]), *delta_pieces, in_weights, gate_act, gate_slope, conv, branch, normed, spec_v, spec_k, forward_one, inverse_one,
         kernel_inverse_one, gains, grad_gain_two),
        1000, 18,
    )
    slots_came = swap(slots_send.astype(BF16), "dp", 1).astype(piece_type)
    (slots,) = call(pair_sum_kernel, [Store(piece, piece_type)], [], (info, slots_keep, slots_came), 0, 6)
    arrived = lax.all_to_all(slots.astype(BF16), "dp", 0, 0, tiled=True, axis_index_groups=parities)
    one_mine, one_tail, out_mine, far = call(
        join_late_kernel,
        [act_like, ((16, part), F32), act_like, ((2 * bucket + 16, part), BF16)],
        [],
        (info, Late(one_kept), swap(one_near, "tensor", 1), Late(out_kept), swap(out_near, "tensor", 1)),
        0, 6,
    )
    far_came = swap(far, "tensor", 2)
    pair, moment_mine, moment_other, count = call(
        mlp_moment_kernel,
        [((2 * rows, hidden), BF16), Store((rows, hidden), F32), Store((rows, hidden), F32), Store((8, part), F32)],
        [],
        (after(info, far), mlp_moment, moment_came, *blocks),
        1, 8,
    )
    if dp == 8:
        pair_pieces = [pair] + [swap(pair, "dp", 2 * k) for k in range(1, pairs)]
    else:
        pair_pieces = [lax.all_gather(pair, "dp", axis=0, tiled=True, axis_index_groups=parities)]
    height = -(-max(rows, slot + 16) // 16) * 16
    mixer_moment_new, slots = call(
        moment_kernel,
        [Store((3, rows, part), F32), Store((4 * dp, height, part), piece_type)],
        [],
        (info, arrived, Late(mixer_moment), Late(count), Late(gain_part)),
        0, 8,
    )
    got = lax.all_to_all(slots.astype(BF16), ("dp", "tensor"), 0, 0, tiled=True)
    (mlp_columns,) = call(
        columns_kernel, [((width, hidden), BF16)], [], (after(info, slots), *pair_pieces), 1000, 4
    )
    mlp_pieces = [mlp_columns] + [lax.ppermute(mlp_columns, "tensor", [(3 ^ k, 3)]) for k in (1, 2, 3)]
    moment_back = swap(moment_other, "dp", 1)
    input_grad, block_out = call(
        output_kernel,
        [Store(*act_like), Store((bucket, part), BF16)],
        [],
        (after(info, slots), one_mine, Late(far_came), out_mine, Late(delta_own), Late(n_own), Late(inv_one),
         Late(middle_own), Late(norm_gains), one_tail),
        0, 8,
    )
    (mlp_moment_new,) = call(
        aside_kernel, [Store((2, rows, hidden), F32)], [], (after(info, slots), Late(moment_mine), Late(moment_back)), 1, 4
    )
    square = ((width, width), F32)
    (sends,) = call(
        large_kernel,
        [Store((8, max(rows, 64), hidden), piece_type, True)],
        [square, square, ((2 * rows, width), F32)],
        (after(info, block_out, mlp_moment_new), *mlp_pieces),
        18, 24,
    )
    all_got = got
    sends = small_steps(after(info, sends), got, sends, rows, width, levels * taps)
    got = lax.all_to_all(sends.astype(BF16), ("dp", "tensor"), 0, 0, tiled=True, axis_index_groups=groups)
    (extra,) = call(
        functools.partial(extra_kernel, rows), [((64, 3 * part), BF16)], [((levels * taps, part), F32)],
        (after(info, sends), Late(all_got)), 0, 4,
    )
    flat = (levels * taps, part)
    old = fetch(
        after(info, extra), 0, mixer_weights, mlp_weights, norm_gains, gain_moment, conv_kernel.reshape(flat),
        kernel_moment.reshape(flat),
    )
    mixer_new, mlp_new, gain_moment_new, gains_new, kernel_moment_new, kernel_new = call(
        final_kernel,
        [Store((3, rows, part), F32), Store((2, rows, hidden), F32), ((2, width), F32), ((2, width), F32), (flat, F32),
         (flat, F32)],
        [((64, 3 * part), F32)],
        (info, got.astype(piece_type), extra, *old, Late(count)),
        0, 8,
    )
    kernel_moment_new, kernel_new = (v.reshape(conv_kernel.shape) for v in (kernel_moment_new, kernel_new))
    return (
        block_out[None],
        input_grad[None],
        gain_moment_new,
        gains_new,
        kernel_moment_new,
        kernel_new,
        mixer_moment_new,
        mixer_new,
        mlp_moment_new,
        mlp_new,
    )


def solution(mesh):
    tokens = P("dp", None, "tensor")
    columns = P(None, None, "tensor")
    blocks = P(None, "dp", "tensor")
    return jax.shard_map(
        per_device,
        mesh=mesh,
        in_specs=(tokens, tokens, P("dp"), P(), columns, columns, columns, P(), columns, blocks, blocks),
        out_specs=(tokens, tokens, P(), P(), columns, columns, blocks, blocks, blocks, blocks),
        check_vma=False,
    )
```

```python
import functools
import math

import jax
import jax.numpy as jnp
import ml_dtypes
import numpy as np
from jax import lax
from jax.experimental import pallas as pl
from jax.experimental.pallas import tpu as pltpu
from jax.sharding import PartitionSpec as P

NS_STEPS = 5
EPSILON = 1e-05
NS_COEF_A = 3.4445
NS_COEF_B = -4.775
NS_COEF_C = 2.0315
MOMENT_DECAY = 0.5
MATRIX_RATE = 1.0
GAIN_RATE = 0.1
KERNEL_RATE = 0.125
SCALE = 10**10
BF16 = jnp.bfloat16
F32 = jnp.float32


def conv_tables(bucket, levels, taps, dp, slot):
    half = bucket // 4
    size = 2 * half
    t = np.arange(half)
    k = np.arange(half)
    phase = 2 * np.pi * ((k[:, None] * t[None, :]) % size) / size
    forward = np.concatenate([np.cos(phase), -np.sin(phase)], 0)
    forward[half] = (-1.0) ** t
    scale = np.full((half,), 2.0 / size)
    scale[0] = 1.0 / size
    inverse = np.concatenate(
        [np.cos(phase).T * scale[None, :], -np.sin(phase).T * scale[None, :]], 1
    )
    inverse[:, half] = ((-1.0) ** t) / size
    spread = np.zeros((bucket, levels * taps))
    at = 0
    for level in range(levels):
        for tap in range(taps):
            width = 2**level
            spread[at : at + width, level * taps + tap] = 0.5**level
            at += width
    kernel_forward = np.concatenate(
        [forward @ spread[m * half : (m + 1) * half] for m in range(4)], 0
    )
    kernel_inverse = np.concatenate(
        [spread[m * half : (m + 1) * half].T @ inverse for m in range(4)], 1
    )
    share = -(-levels * taps // dp)
    kernel_inverse = np.pad(kernel_inverse, ((0, dp * share - levels * taps), (0, 0)))
    kernel_inverse = kernel_inverse.reshape(dp, share, -1)
    kernel_inverse = np.pad(kernel_inverse, ((0, 0), (0, slot - share), (0, 0))).reshape(dp * slot, -1)
    tables = []
    for table in (forward, inverse, kernel_forward, kernel_inverse):
        high = table.astype(ml_dtypes.bfloat16)
        low = (table - high.astype(np.float64)).astype(ml_dtypes.bfloat16)
        tables.append(np.stack([high, low]))
    return tables


def cross(a, b):
    return a[0] * b[0] - a[1] * b[1], a[0] * b[1] + a[1] * b[2]


def cross_conj(a, b):
    return a[0] * b[0] + a[1] * b[1], a[1] * b[2] - a[0] * b[1]


def with_edge(spec, first):
    real, imag = spec
    return real, jnp.where(first, 0.0, imag), jnp.where(first, imag, real)


def add_pairs(pairs):
    return functools.reduce(lambda p, q: (p[0] + q[0], p[1] + q[1]), pairs)


def spectral_blocks(left, right, conj, store):
    for step in range(4):
        rows = step * 64
        index = lax.broadcasted_iota(jnp.int32, (64, 128), 0)
        first = index + rows == 0
        sign = 1.0 - 2.0 * (index % 2).astype(F32)
        a = [left(r, rows) for r in range(4)]
        b = [with_edge(right(m, rows), first) for m in range(4)]
        if conj:
            sums = [add_pairs([cross_conj(a[r], b[r - q]) for r in range(q, 4)]) for q in range(4)]
        else:
            sums = [add_pairs([cross(a[r], b[q - r]) for r in range(q + 1)]) for q in range(4)]
        for q in range(4):
            other = q + 1 if conj else q - 1
            if 0 <= other < 4:
                real = sums[q][0] + sign * sums[other][0]
                imag = sums[q][1] + sign * sums[other][1]
            else:
                real, imag = sums[q]
            store(q, rows, real, imag)


def lane_pair(ref, half):
    return lambda r, rows: (
        ref[rows : rows + 64, r * 128 : (r + 1) * 128],
        ref[half + rows : half + rows + 64, r * 128 : (r + 1) * 128],
    )


def row_pair(ref, half):
    return lambda r, rows: (
        ref[2 * half * r + rows : 2 * half * r + rows + 64, :],
        ref[2 * half * r + half + rows : 2 * half * r + half + rows + 64, :],
    )


def gelu_both(x):
    c = math.sqrt(2.0 / math.pi)
    t = jnp.tanh(c * (x + 0.044715 * x * x * x))
    value = 0.5 * x * (1.0 + t)
    slope = 0.5 * (1.0 + t) + 0.5 * x * (1.0 - t * t) * (c * (1.0 + 3 * 0.044715 * x * x))
    return value, slope


def after(value, *others):
    return lax.optimization_barrier((value, *others))[0]


def swap(value, axis, k):
    size = lax.axis_size(axis)
    return lax.ppermute(value, axis, [(i, i ^ k) for i in range(size)])


def gather_tensor(value, *meanwhile):
    far = swap(value, "tensor", 2)
    near = swap(value, "tensor", 1)
    if meanwhile:
        far = after(far, *meanwhile)
    far_near = swap(far, "tensor", 1)
    return [value, near, far, far_near]


def gather_dp(value, me, low=0):
    size = lax.axis_size("dp")
    whole = value[None]
    while (1 << low) < size:
        bits = min(3, size.bit_length() - 1 - low)
        mine = (me >> low) & ((1 << bits) - 1)
        out = jnp.zeros((1 << bits,) + whole.shape, whole.dtype)
        for k in range(1 << bits):
            piece = whole if k == 0 else swap(whole, "dp", k << low)
            out = lax.dynamic_update_index_in_dim(out, piece, mine ^ k, 0)
        whole = out.reshape((-1,) + value.shape)
        low += bits
    return whole


def dot(a, b, contract):
    return lax.dot_general(a, b, ((contract[0], contract[1]), ((), ())), preferred_element_type=F32)


NN = ((1,), (0,))
NT = ((1,), (1,))
TN = ((0,), (0,))


def split(value):
    high = value.astype(BF16)
    return high, (value - high.astype(F32)).astype(BF16)


def table_dot(table, value):
    high, low = split(value)
    return dot(table[0], high, NN) + (dot(table[1], high, NN) + dot(table[0], low, NN))


def symmetric(left, right, product):
    half = left[0].shape[0] // 2
    top = product([v[:half] for v in left], right, None)
    low = product([v[half:] for v in left], right, half)
    return jnp.concatenate([top, jnp.concatenate([top[:, half:].T, low], 1)], 0)


def three_terms(left, right, cut=None):
    right = right if cut is None else [v[:, cut:] for v in right]
    left = jnp.concatenate([left[0], left[0], left[1]], 1)
    return dot(left, jnp.concatenate([right[0], right[1], right[0]], 0), NN)


def newton_schulz(blocks, a_ref, p_ref, r_ref, start):
    size = a_ref.shape[0]
    row = lax.broadcasted_iota(jnp.int32, (size, size), 0)
    col = lax.broadcasted_iota(jnp.int32, (size, size), 1)
    unit = (row == col).astype(F32)
    blocks = [block() for block in blocks]
    whole = jnp.concatenate(blocks, 1) if len(blocks) > 1 else blocks[0]
    gram = symmetric([whole], [whole], lambda a, b, cut: dot(a[0], b[0] if cut is None else b[0][cut:], NT))
    scale = 1.0 / (jnp.sqrt(jnp.sum(gram * unit)) + 1e-07)
    a_ref[...] = gram * (scale * scale)

    def advance(first):
        a = a_ref[...]
        terms = split(a)
        poly = NS_COEF_A * unit + NS_COEF_B * a + NS_COEF_C * symmetric(terms, terms, three_terms)
        poly_terms = split(poly)
        if first:
            p_ref[...] = poly
            r_ref[...] = p_ref[pl.ds(start, r_ref.shape[0]), :]
        else:
            r_ref[...] = three_terms(split(r_ref[...]), poly_terms)
        half = symmetric(terms, poly_terms, three_terms)
        a_ref[...] = symmetric(poly_terms, split(half), three_terms)

    advance(True)
    pl.loop(0, NS_STEPS - 2)(lambda _: advance(False))
    rows, terms = r_ref[...], split(a_ref[...])
    once = three_terms(split(rows), terms)
    rows = NS_COEF_A * rows + NS_COEF_B * once + NS_COEF_C * three_terms(split(once), terms)
    count = rows.shape[0]
    terms = jnp.concatenate(split(rows), 0)
    both = [dot(terms, block, NN) for block in blocks]
    return [scale * (v[:count] + v[count:]) for v in both]


VMEM = pl.BlockSpec(memory_space=pltpu.VMEM)
SMEM = pl.BlockSpec(memory_space=pltpu.SMEM)


HBM = pl.BlockSpec(memory_space=pltpu.HBM)


class Late:
    def __init__(self, array):
        self.shape, self.dtype = array.shape, array.dtype
        self.array = pltpu.with_memory_space_constraint(array, pltpu.HBM)


class Store:
    def __init__(self, shape, dtype, own=False):
        self.shape, self.dtype, self.own = shape, dtype, own


class Waiting:
    def __init__(self, copy, ref):
        self.copy, self.ref, self.started = copy, ref, False

    def ready(self):
        self.copy.wait()
        return self.ref

    def send(self):
        self.copy.start()
        self.started = True


def call(kernel, outs, scratch, args, time, limit):
    outs = [o if isinstance(o, Store) else jax.ShapeDtypeStruct(*o) for o in outs]
    late = [a for a in (*args, *outs) if isinstance(a, (Late, Store))]
    n_in, n_out = len(args), len(outs)

    def body(*refs):
        given, rest = refs[: n_in + n_out], refs[n_in + n_out :]
        buffers, rest = rest[: len(late)], rest[len(late) :]
        semaphores = rest[-1] if late else None
        passed, stores, at = [], [], 0
        for what, ref in zip((*args, *outs), given):
            if isinstance(what, Late):
                copy = pltpu.make_async_copy(ref, buffers[at], semaphores.at[at])
                copy.start()
            elif isinstance(what, Store):
                copy = pltpu.make_async_copy(buffers[at], ref, semaphores.at[at])
            else:
                passed.append(ref)
                continue
            passed.append(Waiting(copy, buffers[at]))
            if isinstance(what, Store) and not what.own:
                stores.append(passed[-1])
            at += 1
        kernel(*passed, *(rest[:-1] if late else rest))
        for store in stores:
            if not store.started:
                store.send()
        for store in stores:
            store.copy.wait()

    return pl.pallas_call(
        body,
        out_shape=tuple(pltpu.HBM(o.shape, o.dtype) if isinstance(o, Store) else o for o in outs),
        in_specs=[SMEM] + [HBM if isinstance(a, Late) else VMEM for a in args[1:]],
        out_specs=tuple(HBM if isinstance(o, Store) else VMEM for o in outs),
        scratch_shapes=[pltpu.VMEM(a.shape, a.dtype) for a in late]
        + [pltpu.VMEM(*what) if isinstance(what, tuple) else what for what in scratch]
        + ([pltpu.SemaphoreType.DMA((len(late),))] if late else []),
        compiler_params=pltpu.CompilerParams(vmem_limit_bytes=limit * 2**20),
        cost_estimate=pl.CostEstimate(flops=max(time * SCALE, 10**6), bytes_accessed=0, transcendentals=0),
    )(*(a.array if isinstance(a, Late) else a for a in args))


def fetch(token, time, *arrays):
    arrays = [a if isinstance(a, list) else [(a, None)] for a in arrays]
    shapes = []
    for a in arrays:
        cuts = [p.shape if index is None else p.shape[1:] for p, index in a]
        shapes.append(jax.ShapeDtypeStruct((sum(c[0] for c in cuts), *cuts[0][1:]), a[0][0].dtype))
    flat = [pltpu.with_memory_space_constraint(p, pltpu.HBM) for a in arrays for p, _ in a]

    def body(token_ref, *refs):
        outs, semaphores, copies, at = refs[len(flat) : -1], refs[-1], [], 0
        for a, out in zip(arrays, outs):
            row = 0
            for _, index in a:
                source = refs[at] if index is None else refs[at].at[index]
                target = out if len(a) == 1 else out.at[row : row + source.shape[0]]
                copies.append(pltpu.make_async_copy(source, target, semaphores.at[at]))
                copies[-1].start()
                row, at = row + source.shape[0], at + 1
        for copy in copies:
            copy.wait()

    return pl.pallas_call(
        body,
        out_shape=tuple(shapes),
        in_specs=[SMEM] + [HBM] * len(flat),
        out_specs=(VMEM,) * len(shapes),
        scratch_shapes=[pltpu.SemaphoreType.DMA((len(flat),))],
        compiler_params=pltpu.CompilerParams(vmem_limit_bytes=2 * 2**20),
        cost_estimate=pl.CostEstimate(flops=max(time * SCALE, 10**6), bytes_accessed=0, transcendentals=0),
    )(token, *flat)


def block_at(index, size):
    return pl.ds(pl.multiple_of(index * size, size), size)


def row_mask(info, start, rows):
    return (start + lax.broadcasted_iota(jnp.int32, (rows, 1), 0) < info[1]).astype(F32)


def spectrum_kernel(info, table, taps, spec_k):
    taps = taps.ready()[...]
    spec_k[...] = table_dot(table.ready(), taps)


def entry_kernel(info, p0, p1, p2, p3, weights, gains, forward, inverse, spec_k,
                 x, normed, n_own, inv, spec_v, conv, act, slope, branch, gains_kept, wide, spec_y):
    me = info[0]
    part = p1.shape[1]
    for k, piece in enumerate((p0, p1, p2, p3)):
        x[:, block_at(me ^ k, part)] = piece[...]
    gains_kept[...] = gains[...]
    gain = gains[0:1, :]
    half = x.shape[0] // 4
    for c in range(4):
        r = slice(c * half, (c + 1) * half)
        v = x[r, :].astype(F32)
        mean = jnp.mean(v, 1, keepdims=True)
        centred = v - mean
        scale = lax.rsqrt(jnp.mean(centred * centred, 1, keepdims=True) + EPSILON)
        normed[r, :] = (centred * scale * gain).astype(BF16)
        inv.ref[r, :] = scale
        n_own.ref[r, :] = (p0[r, :].astype(F32) - mean) * scale
    n_own.send()
    inv.send()
    for c in range(4):
        r = slice(c * half, (c + 1) * half)
        normal = normed[r, :]
        wide[:, c * part : (c + 1) * part] = dot(normal, weights[0], NN)
        act[r, :], slope[r, :] = gelu_both(dot(normal, weights[1], NN))
    spec_v[...] = table_dot(forward, wide[...])

    def store(q, rows, real, imag):
        spec_y[rows : rows + 64, q * part : (q + 1) * part] = real
        spec_y[half + rows : half + rows + 64, q * part : (q + 1) * part] = imag

    spectral_blocks(lane_pair(spec_v, half), row_pair(spec_k, half), False, store)
    wide[...] = table_dot(inverse, spec_y[...])
    for c in range(4):
        r = slice(c * half, (c + 1) * half)
        out = wide[:, c * part : (c + 1) * part]
        conv[r, :] = out
        out = (act[r, :] * out * row_mask(info, c * half, half)).astype(BF16)
        branch[r, :] = out


def cotangent_kernel(info, p0, p1, p2, p3, weights, cot, out_w, delta, weights_kept):
    part = p0.shape[1]
    for k, piece in enumerate((p0, p1, p2, p3)):
        cot[:, block_at(info[0] ^ k, part)] = piece[: cot.shape[0], :]
        out_w[:, block_at(info[0] ^ k, part)] = piece[cot.shape[0] :, :]
    step = cot.shape[0] // 4
    weights = weights.ready()
    weights_kept[...] = weights[...]
    for c in range(4):
        r = slice(c * step, (c + 1) * step)
        delta[r, :] = dot(cot[r, :], weights[1], NN)


def middle_kernel(info, b0, b1, b2, b3, out_w, x, gains, weights, delta_active,
                  near, kept, normed, active, delta_hidden, n_mine, inv_mine, middle_own, branch, middle):
    me = info[0]
    part = b0.shape[1]
    step = x.shape[0] // 4
    for k, piece in enumerate((b0, b1, b2, b3)):
        branch[:, block_at(me ^ k, part)] = piece[...]
    gain = gains[1:2, :]
    for k in (1, 3, 0, 2):
        block = me ^ k
        r = block_at(block, step)
        mid = x[r, :].astype(F32) + dot(branch[r, :], out_w[...], NT)
        middle[r, :] = mid
        centred = mid - jnp.mean(mid, 1, keepdims=True)
        scale = lax.rsqrt(jnp.mean(centred * centred, 1, keepdims=True) + EPSILON)
        normal = centred * scale
        if k == 0:
            n_mine[...] = normal
            inv_mine[...] = scale
        normal = (normal * gain).astype(BF16)
        normed[r, :] = normal
        value, slope = gelu_both(dot(normal, weights[0], NN))
        mask = row_mask(info, block * step, step)
        active[r, :] = (value * mask).astype(BF16)
        back = (delta_active[r, :] * mask * slope).astype(BF16)
        delta_hidden[r, :] = back
        share = dot(back, weights[0], NT)
        if k % 2:
            near[(k // 2) * step : (k // 2 + 1) * step, :] = share.astype(BF16)
        else:
            kept[(k // 2) * step : (k // 2 + 1) * step, :] = share
    middle_own.ref[...] = middle[:, block_at(me, part)]


def mlp_kernel(info, normed, active, delta_hidden, cot, moment, out, moment_send, away):
    size = normed.shape[1]
    wanted = (info[2] + away) % 2

    @pl.when(wanted == 0)
    def _():
        out[:size, :] = dot(normed[...], delta_hidden[...], TN).astype(out.dtype)

    @pl.when(wanted == 1)
    def _():
        out[:size, :] = dot(cot[...], active[...], TN).astype(out.dtype)

    length = jnp.full((16, out.shape[1]), 1, jnp.int32) * info[1]
    first = lax.broadcasted_iota(jnp.int32, length.shape, 0) == 0
    out[size:, :] = jnp.where(first, length // 32, length % 32).astype(F32).astype(out.dtype)
    if away:
        moment_send[...] = moment.ready()[wanted]


def mlp_away_kernel(info, normed, active, delta_hidden, cot, moment, out, moment_send):
    mlp_kernel(info, normed, active, delta_hidden, cot, moment, out, moment_send, 1)


def mlp_here_kernel(info, normed, active, delta_hidden, cot, out):
    mlp_kernel(info, normed, active, delta_hidden, cot, None, out, None, 0)


def mlp_out_kernel(info, active, weights, near, kept, part_out):
    me = info[0]
    step = active.shape[0] // 4
    part = near.ref.shape[2]
    for c in range(4):
        r = slice(c * step, (c + 1) * step)
        part_out[r, :] = dot(active[r, :], weights[1], NT)
    for k in range(4):
        share = part_out[:, block_at(me ^ k, part)]
        if k % 2:
            near.ref[k // 2] = share.astype(BF16)
        else:
            kept.ref[k // 2] = share.astype(BF16)


def mlp_rows_kernel(info, keep, came, *outs):
    size = came.shape[0] - 16
    pairs = outs[0].shape[0] if len(outs) == 1 else len(outs)
    rows = size // pairs
    length = keep[size:, :] + came[size:, :].astype(F32)
    for k in range(pairs):
        if len(outs) == 1:
            r, out = pl.ds(k * rows, rows), outs[0].at[k]
        else:
            r, out = block_at((info[2] // 2) ^ k, rows), outs[k]
        out[:rows, :] = (keep[r, :] + came[r, :].astype(F32)).astype(out.dtype)
        out[rows:, :] = length.astype(out.dtype)


def mlp_moment_kernel(info, moment, other_moment, *refs):
    *pieces, matrix, mine, other, count = refs
    rows = moment.shape[1]
    side = info[2] % 2
    if len(pieces) == 1:
        pieces = [pieces[0].at[k] for k in range(pieces[0].shape[0])]
    total = pieces[0][...].astype(F32)
    for piece in pieces[1:]:
        total = total + piece[...].astype(F32)
    tokens = 32.0 * total[2 * rows : 2 * rows + 1, :] + total[2 * rows + 1 : 2 * rows + 2, :]
    count.ref[...] = jnp.broadcast_to(tokens[:, : count.ref.shape[1]], count.ref.shape)
    old = moment[side]
    for which in range(2):
        new = total[which * rows : (which + 1) * rows, :] / tokens

        @pl.when(side == which)
        def _(new=new, which=which):
            now = MOMENT_DECAY * old + new
            mine.ref[...] = now
            matrix[which * rows : (which + 1) * rows, :] = now.astype(matrix.dtype)

        @pl.when(side != which)
        def _(new=new, which=which):
            now = MOMENT_DECAY * other_moment[...] + new
            other.ref[...] = now
            matrix[which * rows : (which + 1) * rows, :] = now.astype(matrix.dtype)


def columns_kernel(info, *refs):
    *pieces, out = refs
    rows = pieces[0].shape[0]
    for k, piece in enumerate(pieces):
        out[block_at((info[2] // 2) ^ k, rows), :] = piece[...]


def join_kernel(info, kept, came, mine, far):
    mine[...] = kept[0] + came[0].astype(F32)
    far[...] = (kept[1] + came[1].astype(F32)).astype(BF16)


def join_late_kernel(info, one_kept, one_came, out_kept, out_came, one_mine, tail, out_mine, far):
    one_kept, out_kept = one_kept.ready(), out_kept.ready()
    size = out_mine.shape[0]
    one_mine[...] = one_kept[0, :size, :] + one_came[0, :size, :].astype(F32)
    tail[...] = one_kept[0, size:, :] + one_came[0, size:, :].astype(F32)
    far[: size + 16, :] = (one_kept[1] + one_came[1].astype(F32)).astype(BF16)
    out_mine[...] = out_kept[0].astype(F32) + out_came[0].astype(F32)
    far[size + 16 :, :] = (out_kept[1].astype(F32) + out_came[1].astype(F32)).astype(BF16)


def norm_back_kernel(info, mine, came, cot, n_mine, inv_mine, gains, delta, grad_gain):
    size = mine.shape[0]
    total = mine[...] + came[...].astype(F32)
    n = n_mine[...]
    q = total * gains[1:2, :]
    back = inv_mine[...] * (q - jnp.mean(q, 1, keepdims=True) - n * jnp.mean(q * n, 1, keepdims=True))
    delta[...] = (cot[block_at(info[0], size), :].astype(F32) + back).astype(BF16)
    grad_gain[...] = jnp.sum(total * n, 0, keepdims=True)


def mixer_back_kernel(info, d0, d1, d2, d3, weights, act, slope, conv, branch, normed, spec_v, spec_k, forward, inverse,
                      kernel_inverse, gains, gain_two,
                      keep, send, near, kept, delta_own, gain_part,
                      slots, semaphores, delta, wide, spec_d, spec_y, spec_u, back, share):
    me = info[0]
    step, width = d0.shape
    part = slots.shape[3]
    half = step
    for k, piece in enumerate((d0, d1, d2, d3)):
        block = me ^ k
        r = block_at(block, step)
        delta[r, :] = piece[...]
        down = dot(piece[...], weights[2], NN) * row_mask(info, block * step, step)
        back[r, part:] = (down * conv[r, :] * slope[r, :]).astype(BF16)
        wide[:, block_at(block, part)] = down * act[r, :]
    delta_own.ref[...] = delta[:, block_at(me, part)]
    delta_own.send()
    spec_d[...] = table_dot(forward, wide[...])

    def store(q, rows, real, imag):
        spec_y[rows : rows + 64, q * part : (q + 1) * part] = real
        spec_y[half + rows : half + rows + 64, q * part : (q + 1) * part] = imag

    def store_rows(q, rows, real, imag):
        spec_u[2 * half * q + rows : 2 * half * q + rows + 64, :] = real
        spec_u[2 * half * q + half + rows : 2 * half * q + half + rows + 64, :] = imag

    spectral_blocks(lane_pair(spec_d, half), row_pair(spec_k, half), True, store)
    wide[...] = table_dot(inverse, spec_y[...])
    for c in range(4):
        back[c * half : (c + 1) * half, :part] = wide[:, c * part : (c + 1) * part].astype(BF16)
    spectral_blocks(lane_pair(spec_d, half), lane_pair(spec_v, half), True, store_rows)
    grad_kernel = table_dot(kernel_inverse, spec_u[...])
    grads = dot(normed[...], back[...], TN)
    grad_out = dot(delta[...], branch[...], TN)
    dp = 2 * slots.shape[1]
    rows = width // dp
    taps = grad_kernel.shape[0] // dp
    for i in range(dp):
        r = slice(i * rows, (i + 1) * rows)
        slots[i % 2, i // 2, :rows, :] = grads[r, :part].astype(slots.dtype)
        slots[i % 2, i // 2, rows : 2 * rows, :] = grads[r, part:].astype(slots.dtype)
        slots[i % 2, i // 2, 2 * rows : 3 * rows, :] = grad_out[r, :].astype(slots.dtype)
        slots[i % 2, i // 2, 3 * rows :, :] = grad_kernel[i * taps : (i + 1) * taps, :].astype(slots.dtype)
    side = info[2] % 2
    copies = [
        pltpu.make_async_copy(slots.at[side], keep, semaphores.at[0]),
        pltpu.make_async_copy(slots.at[1 - side], send, semaphores.at[1]),
    ]
    for copy in copies:
        copy.start()
    ones = jnp.ones((8, width), BF16)
    gain_one = jnp.zeros((1, width), F32)
    sums = [[], []]
    gain = jnp.broadcast_to(gains[0:1, :], (8, width)).astype(BF16)
    for c in range(4):
        r = slice(c * step, (c + 1) * step)
        out = dot(back[r, :part], weights[0], NT) + dot(back[r, part:], weights[1], NT)
        share[r, :] = out
        first = dot(gain, out.astype(BF16), NT)
        both = out * normed[r, :].astype(F32)
        gain_one = gain_one + jnp.sum(both, 0, keepdims=True)
        second = dot(ones, both.astype(BF16), NT)
        for h in range(step // part):
            sums[0].append(first[0:1, h * part : (h + 1) * part])
            sums[1].append(second[0:1, h * part : (h + 1) * part])
    gain_one = gain_one / gains[0:1, :]
    gain = [g[:, q * part : (q + 1) * part] for g in (gain_one, gain_two[...]) for q in range(4)]
    gain_part.ref[...] = jnp.concatenate(gain, 0)
    tail = jnp.concatenate([*sums[0], *sums[1]], 0)
    for k in range(4):
        block = share[:, block_at(me ^ k, part)]
        if k % 2:
            near.ref[k // 2, : share.shape[0], :] = block.astype(BF16)
            near.ref[k // 2, share.shape[0] :, :] = tail.astype(BF16)
        else:
            kept.ref[k // 2, : share.shape[0], :] = block
            kept.ref[k // 2, share.shape[0] :, :] = tail
    for copy in copies:
        copy.wait()


def pair_sum_kernel(info, keep, came, out):
    for z in range(keep.shape[0]):
        out.ref[z] = (keep[z].astype(F32) + came[z].astype(F32)).astype(out.ref.dtype)


def keeper(t):
    return 4 * (1 - t // 2) + t


def moment_kernel(info, arrived, moment, count, gain_part, moment_new, slots):
    me = info[0]
    pairs = arrived.shape[0]
    _, rows, part = moment.ref.shape
    taps = arrived.shape[1] - 3 * rows
    total = arrived[0].astype(F32)
    for i in range(1, pairs):
        total = total + arrived[i].astype(F32)
    high, low = split(gain_part.ready()[...])
    rest = jnp.concatenate([total[3 * rows :, :], high.astype(F32), low.astype(F32)], 0).astype(slots.ref.dtype)
    moment, count = moment.ready(), count.ready()
    for which in range(3):
        value = MOMENT_DECAY * moment[which] + total[which * rows : (which + 1) * rows, :] / count[0:1, :]
        moment_new.ref[which] = value
        for z in range(pairs):
            slots.ref[8 * z + keeper(which), :rows, :] = value.astype(slots.ref.dtype)
    for t in range(4):
        for z in range(pairs):
            slots.ref[8 * z + (keeper(t) ^ 4), : taps + 16, :] = rest
            if t == 3:
                slots.ref[8 * z + keeper(t), : taps + 16, :] = rest
    slots.send()


def output_kernel(info, mine, came, out_mine, delta_own, n_own, inv, middle_own, gains, tail, input_grad, block_out):
    part = mine.shape[1]
    came = came.ready()
    gain = gains.ready()[0:1, block_at(info[0], part)]
    size = mine.shape[0]
    sums = (tail[...] + came[size : size + 16, :].astype(F32)) / (4 * part)
    middle_own = middle_own.ready()
    n_own, inv, delta_own = n_own.ready(), inv.ready(), delta_own.ready()
    for h in range(mine.shape[0] // part):
        r = slice(h * part, (h + 1) * part)
        block_out.ref[r, :] = (middle_own[r, :] + (out_mine[r, :] + came[size + 16 + h * part : size + 16 + (h + 1) * part, :].astype(F32))).astype(BF16)
        column = lambda at: jnp.broadcast_to(sums[at : at + 1, :], (part, part)).T
        total = mine[r, :] + came[r, :].astype(F32)
        back = total * gain - column(h) - n_own[r, :] * column(8 + h)
        input_grad.ref[r, :] = delta_own[r, :].astype(F32) + inv[r, :] * back


def large_kernel(info, m0, m1, m2, m3, out, a, p, r):
    me, row = info[0], info[2]
    rows = r.shape[0] // 2

    @pl.when(me == 3)
    def _():
        start = pl.multiple_of((row // 2) * (2 * rows), 2 * rows)
        blocks = [lambda piece=piece: piece[...] for piece in (m0, m1, m2, m3)]
        for k, steps in enumerate(newton_schulz(blocks, a, p, r, start)):
            for y in range(2):
                out.ref[4 * y + (3 ^ k), :rows, :] = steps[y * rows : (y + 1) * rows, :].astype(out.ref.dtype)
        out.send()
        out.copy.wait()


def gather_extra(got, me, rows, packed, extra):
    total, dp = packed.shape[0], got.shape[0] // 4
    part = packed.shape[1]
    share = -(-total // dp)
    taps = -(-share // 8) * 8
    taps += (3 * rows + taps) % 16
    gain = 0.0
    for i in range(dp):
        both = got[4 * i + me, : taps + 16, :].astype(F32)
        count = min(share, total - i * share)
        if count > 0:
            packed[i * share : i * share + count, :] = both[:count, :]
        for t in range(4):
            both = got[4 * i + t, taps : taps + 16, :].astype(F32)
            gain = gain + (both[:8, :] + both[8:, :])
    high, low = split(gain)
    extra[...] = jnp.zeros_like(extra)
    for g in range(-(-total // 64)):
        count = min(64, total - 64 * g)
        extra[:count, g * part : (g + 1) * part] = packed[64 * g : 64 * g + count, :].astype(extra.dtype)
    at = (total // 64) * part
    extra[32:48, at : at + part] = jnp.concatenate([high.astype(F32), low.astype(F32)], 0).astype(extra.dtype)


def small_kernel(info, source, slots, out, got, extra, matrix, a, p, r, packed, steps, semaphore):
    me, row = info[0], info[2]
    side = row % 2
    size, width = matrix.shape
    rows = r.shape[0] // 2
    part = width // 4
    start = pl.multiple_of((row // 2) * (2 * rows), 2 * rows)
    keeps = jnp.logical_and(side == 1 - me // 2, me < 3)

    @pl.when(me < 3)
    def _():
        arrive = pltpu.make_async_copy(source, got, semaphore.at[2])
        arrive.start()
        arrive.wait()

        @pl.when(keeps)
        def _():
            for i in range(size // rows):
                for t in range(4):
                    matrix[i * rows : (i + 1) * rows, t * part : (t + 1) * part] = got[4 * i + t, :rows, :].astype(BF16)
            (result,) = newton_schulz([lambda: matrix[...]], a, p, r, start)
            for q in range(8):
                lanes = slice((q % 4) * part, (q % 4 + 1) * part)
                steps[q] = result[(q // 4) * rows : (q // 4 + 1) * rows, lanes].astype(steps.dtype)
            copy = pltpu.make_async_copy(steps, out.at[:, pl.ds(0, rows), pl.ds(0, part)], semaphore.at[0])
            copy.start()
            copy.wait()

        @pl.when(jnp.logical_not(keeps))
        def _():
            gather_extra(got, me, rows, packed, extra)
            copies = [
                pltpu.make_async_copy(extra, out.at[4 * y + me, pl.ds(0, 64), pl.ds(0, 3 * part)], semaphore.at[y])
                for y in range(2)
            ]
            for copy in copies:
                copy.start()
            for copy in copies:
                copy.wait()


def small_steps(info, got, slots, rows, width, taps):
    part = width // 4
    square = pltpu.VMEM((width, width), F32)
    return pl.pallas_call(
        small_kernel,
        out_shape=pltpu.HBM(slots.shape, slots.dtype),
        in_specs=[SMEM, HBM, HBM],
        out_specs=HBM,
        scratch_shapes=[
            pltpu.VMEM(got.shape, got.dtype), pltpu.VMEM((64, 3 * part), slots.dtype), pltpu.VMEM((width, width), BF16), square,
            square, pltpu.VMEM((2 * rows, width), F32), pltpu.VMEM((taps, part), F32), pltpu.VMEM((8, rows, part), slots.dtype),
            pltpu.SemaphoreType.DMA((3,)),
        ],
        input_output_aliases={2: 0},
        compiler_params=pltpu.CompilerParams(vmem_limit_bytes=24 * 2**20),
        cost_estimate=pl.CostEstimate(flops=18 * SCALE, bytes_accessed=0, transcendentals=0),
    )(info, pltpu.with_memory_space_constraint(got, pltpu.HBM), pltpu.with_memory_space_constraint(slots, pltpu.HBM))


def extra_kernel(rows, info, got, extra, packed):
    gather_extra(got.ready(), info[0], rows, packed, extra)


def aside_kernel(info, moment_mine, moment_back, moment_new):
    side = info[2] % 2
    moment_new.ref[side] = moment_mine.ready()[...]
    moment_new.ref[1 - side] = moment_back.ready()[...]


def final_kernel(info, got, extra_mine, mixer_weights, mlp_weights, norm_gains, gain_moment, taps, taps_moment, count,
                 mixer_new, mlp_new, gain_moment_new, gains_new, taps_moment_new, taps_new, extra):
    me, row = info[0], info[2]
    count = count.ready()
    _, rows, part = mixer_new.ref.shape
    hidden = mlp_new.ref.shape[2]
    width = 4 * part
    for t in range(3):
        old = mixer_weights[t, block_at(row, rows), :].astype(F32)
        mixer_new.ref[t] = old - MATRIX_RATE * got[keeper(t), :rows, :part].astype(F32)
    mixer_new.send()
    rate = MATRIX_RATE * math.sqrt(4 * hidden / width)
    for which in range(2):
        old = mlp_weights[which, block_at(row, rows), :].astype(F32)
        mlp_new.ref[which] = old - rate * got[4 * which + 3, :rows, :].astype(F32)
    mlp_new.send()
    @pl.when(me == 3)
    def _():
        extra[...] = extra_mine[...].astype(F32)

    @pl.when(me != 3)
    def _():
        extra[...] = got[keeper(me) ^ 4, :64, : 3 * part].astype(F32)

    total = taps.shape[0]
    grad = [extra[: min(64, total - 64 * g), g * part : (g + 1) * part] for g in range(-(-total // 64))]
    at = (total // 64) * part
    gain = extra[32:40, at : at + part] + extra[40:48, at : at + part]
    new = MOMENT_DECAY * taps_moment[...] + jnp.concatenate(grad, 0) / count[0:1, :]
    taps_moment_new[...] = new
    scale = jnp.sqrt(jnp.mean(new * new, 0, keepdims=True)) + 1e-08
    taps_new[...] = taps[...] - KERNEL_RATE * new / scale
    for which in range(2):
        for t in range(4):
            lanes = slice(t * part, (t + 1) * part)
            gain_moment_new[which : which + 1, lanes] = (
                MOMENT_DECAY * gain_moment[which : which + 1, lanes]
                + gain[4 * which + t : 4 * which + t + 1, :] / count[0:1, :]
            )
    new = gain_moment_new[...]
    scale = jnp.sqrt(jnp.mean(new * new, 1, keepdims=True)) + 1e-08
    gains_new[...] = norm_gains[...] - GAIN_RATE * new / scale


def per_device(
    tokens,
    cotangent,
    lengths,
    norm_gains,
    conv_kernel,
    mixer_weights,
    mlp_weights,
    gain_moment,
    kernel_moment,
    mixer_moment,
    mlp_moment,
):
    _, bucket, part = tokens.shape
    levels, taps, _ = conv_kernel.shape
    hidden = mlp_weights.shape[2]
    me = lax.axis_index("tensor")
    row = lax.axis_index("dp")
    dp = lax.axis_size("dp")
    width = 4 * part
    rows = width // dp
    half = bucket // 4
    piece_type = BF16 if rows % 16 == 0 else F32
    share = -(-levels * taps // dp)
    slot = -(-share // 8) * 8
    slot += (3 * rows + slot) % 16
    forward, inverse, kernel_forward, kernel_inverse = conv_tables(bucket, levels, taps, dp, slot)
    info = jnp.stack([me, lengths[0], row]).astype(jnp.int32)

    x_own, in_weights, in_gains, forward_one, inverse_one, late = fetch(
        info, 1, tokens[0], mixer_weights, norm_gains, forward, inverse, [(cotangent, 0), (mixer_weights, 2)]
    )
    (spec_k,) = call(
        spectrum_kernel,
        [((8 * half, part), F32)],
        [],
        (after(info, x_own), Late(kernel_forward), Late(conv_kernel.reshape(levels * taps, part))),
        2, 10,
    )
    x_pieces = gather_tensor(tokens[0], spec_k, x_own)

    act_like = ((bucket, part), F32)
    wide_like = ((half, width), F32)
    spec_like = ((2 * half, width), F32)
    whole_like = ((bucket, width), BF16)
    quarter_like = ((half, width), BF16)
    x, normed, n_own, inv_one, spec_v, conv, gate_act, gate_slope, branch, gains = call(
        entry_kernel,
        [whole_like, whole_like, Store(*act_like), Store((bucket, 1), F32), spec_like, act_like, act_like, act_like,
         ((bucket, part), BF16), ((2, width), F32)],
        [wide_like, spec_like],
        (info, x_own, *x_pieces[1:], in_weights, in_gains, forward_one, inverse_one, spec_k),
        0, 12,
    )
    late = gather_tensor(late, branch)
    cot, out_weights, delta_active, mlp_kept = call(
        cotangent_kernel,
        [whole_like, ((width, width), BF16), ((bucket, hidden), F32), (mlp_weights.shape, BF16)],
        [],
        (after(info, branch), *late, Late(mlp_weights)),
        3, 5,
    )
    branch_pieces = gather_tensor(branch, delta_active)
    near, kept, normed_two, active, delta_hidden, n_mine, inv_mine, middle_own = call(
        middle_kernel,
        [((width, width), BF16), ((width, width), F32), whole_like, ((bucket, hidden), BF16),
         ((bucket, hidden), BF16), wide_like, ((half, 1), F32), Store(*act_like)],
        [whole_like, ((bucket, width), F32)],
        (info, *branch_pieces, out_weights, x, gains, mlp_kept, delta_active),
        6, 12,
    )
    split_blocks = lambda v: v.reshape(2, -1, v.shape[-1])
    came = swap(split_blocks(near), "tensor", 1)
    mine, far = call(join_kernel, [wide_like, quarter_like], [], (info, split_blocks(kept), came), 1, 4)
    mlp_inputs = (normed_two, active, delta_hidden, cot)
    mlp_send, moment_send = call(
        mlp_away_kernel,
        [((width + 16, hidden), BF16), ((rows, hidden), F32)],
        [],
        (after(info, far), *mlp_inputs, Late(mlp_moment)),
        2, 5,
    )
    (mlp_keep,) = call(
        mlp_here_kernel, [((width + 16, hidden), F32)], [], (after(info, mlp_send), *mlp_inputs), 1000, 8
    )
    mlp_came = swap(mlp_send, "dp", 1)
    moment_came = swap(moment_send, "dp", 1)
    came = swap(far, "tensor", 2)
    delta_mid, grad_gain_two = call(
        norm_back_kernel,
        [quarter_like, ((1, width), F32)],
        [],
        (after(info, mlp_keep), mine, came, cot, n_mine, inv_mine, gains),
        1000, 4,
    )
    (kernel_inverse_one,) = fetch(after(info, delta_mid), 0, kernel_inverse)
    out_near, out_kept = call(
        mlp_out_kernel,
        [Store((2, bucket, part), BF16), Store((2, bucket, part), BF16)],
        [((bucket, width), F32)],
        (after(info, kernel_inverse_one), active, mlp_kept),
        1, 8,
    )
    delta_pieces = gather_tensor(delta_mid, kernel_inverse_one, out_near)

    pairs = dp // 2
    parities = [[i for i in range(dp) if i % 2 == y] for y in range(2)]
    groups = [[8 * z + q for q in range(8)] for z in range(pairs)]
    block = (2 * rows + 16, hidden)
    if dp == 8:
        blocks = call(mlp_rows_kernel, [(block, BF16)] * pairs, [], (info, mlp_keep, mlp_came), 0, 6)
        blocks = [blocks[0]] + [swap(blocks[k], "dp", 2 * k) for k in range(1, pairs)]
    else:
        (blocks,) = call(mlp_rows_kernel, [((pairs, *block), BF16)], [], (info, mlp_keep, mlp_came), 0, 6)
        blocks = [lax.all_to_all(blocks, "dp", 0, 0, tiled=True, axis_index_groups=parities)]

    piece = (pairs, 3 * rows + slot, part)
    slots_keep, slots_send, one_near, one_kept, delta_own, gain_part = call(
        mixer_back_kernel,
        [(piece, piece_type), (piece, piece_type), Store((2, bucket + 16, part), BF16),
         Store((2, bucket + 16, part), F32), Store((bucket, part), BF16), Store((8, part), F32)],
        [((2, *piece), piece_type), pltpu.SemaphoreType.DMA((2,)), whole_like, wide_like, spec_like, spec_like,
         ((8 * half, part), F32), ((bucket, 2 * part), BF16), ((bucket, width), F32)],
        (after(info, blocks[0]), *delta_pieces, in_weights, gate_act, gate_slope, conv, branch, normed, spec_v, spec_k, forward_one, inverse_one,
         kernel_inverse_one, gains, grad_gain_two),
        1000, 18,
    )
    slots_came = swap(slots_send.astype(BF16), "dp", 1).astype(piece_type)
    (slots,) = call(pair_sum_kernel, [Store(piece, piece_type)], [], (info, slots_keep, slots_came), 0, 6)
    arrived = lax.all_to_all(slots.astype(BF16), "dp", 0, 0, tiled=True, axis_index_groups=parities)
    one_mine, one_tail, out_mine, far = call(
        join_late_kernel,
        [act_like, ((16, part), F32), act_like, ((2 * bucket + 16, part), BF16)],
        [],
        (info, Late(one_kept), swap(one_near, "tensor", 1), Late(out_kept), swap(out_near, "tensor", 1)),
        0, 6,
    )
    far_came = swap(far, "tensor", 2)
    pair, moment_mine, moment_other, count = call(
        mlp_moment_kernel,
        [((2 * rows, hidden), BF16), Store((rows, hidden), F32), Store((rows, hidden), F32), Store((8, part), F32)],
        [],
        (after(info, far), mlp_moment, moment_came, *blocks),
        1, 8,
    )
    if dp == 8:
        pair_pieces = [pair] + [swap(pair, "dp", 2 * k) for k in range(1, pairs)]
    else:
        pair_pieces = [lax.all_gather(pair, "dp", axis=0, tiled=True, axis_index_groups=parities)]
    height = -(-max(rows, slot + 16) // 16) * 16
    mixer_moment_new, slots = call(
        moment_kernel,
        [Store((3, rows, part), F32), Store((4 * dp, height, part), piece_type)],
        [],
        (info, arrived, Late(mixer_moment), Late(count), Late(gain_part)),
        0, 8,
    )
    got = lax.all_to_all(slots.astype(BF16), ("dp", "tensor"), 0, 0, tiled=True)
    (mlp_columns,) = call(
        columns_kernel, [((width, hidden), BF16)], [], (after(info, slots), *pair_pieces), 1000, 4
    )
    mlp_pieces = [mlp_columns] + [lax.ppermute(mlp_columns, "tensor", [(3 ^ k, 3)]) for k in (1, 2, 3)]
    moment_back = swap(moment_other, "dp", 1)
    input_grad, block_out = call(
        output_kernel,
        [Store(*act_like), Store((bucket, part), BF16)],
        [],
        (after(info, slots), one_mine, Late(far_came), out_mine, Late(delta_own), Late(n_own), Late(inv_one),
         Late(middle_own), Late(norm_gains), one_tail),
        0, 8,
    )
    (mlp_moment_new,) = call(
        aside_kernel, [Store((2, rows, hidden), F32)], [], (after(info, slots), Late(moment_mine), Late(moment_back)), 1, 4
    )
    square = ((width, width), F32)
    (sends,) = call(
        large_kernel,
        [Store((8, max(rows, 64), hidden), piece_type, True)],
        [square, square, ((2 * rows, width), F32)],
        (after(info, block_out, mlp_moment_new), *mlp_pieces),
        18, 24,
    )
    all_got = got
    sends = small_steps(after(info, sends), got, sends, rows, width, levels * taps)
    got = lax.all_to_all(sends.astype(BF16), ("dp", "tensor"), 0, 0, tiled=True, axis_index_groups=groups)
    (extra,) = call(
        functools.partial(extra_kernel, rows), [((64, 3 * part), BF16)], [((levels * taps, part), F32)],
        (after(info, sends), Late(all_got)), 0, 4,
    )
    flat = (levels * taps, part)
    old = fetch(
        after(info, extra), 0, mixer_weights, mlp_weights, norm_gains, gain_moment, conv_kernel.reshape(flat),
        kernel_moment.reshape(flat),
    )
    mixer_new, mlp_new, gain_moment_new, gains_new, kernel_moment_new, kernel_new = call(
        final_kernel,
        [Store((3, rows, part), F32), Store((2, rows, hidden), F32), ((2, width), F32), ((2, width), F32), (flat, F32),
         (flat, F32)],
        [((64, 3 * part), F32)],
        (info, got.astype(piece_type), extra, *old, Late(count)),
        0, 8,
    )
    kernel_moment_new, kernel_new = (v.reshape(conv_kernel.shape) for v in (kernel_moment_new, kernel_new))
    return (
        block_out[None],
        input_grad[None],
        gain_moment_new,
        gains_new,
        kernel_moment_new,
        kernel_new,
        mixer_moment_new,
        mixer_new,
        mlp_moment_new,
        mlp_new,
    )


def solution(mesh):
    tokens = P("dp", None, "tensor")
    columns = P(None, None, "tensor")
    blocks = P(None, "dp", "tensor")
    return jax.shard_map(
        per_device,
        mesh=mesh,
        in_specs=(tokens, tokens, P("dp"), P(), columns, columns, columns, P(), columns, blocks, blocks),
        out_specs=(tokens, tokens, P(), P(), columns, columns, blocks, blocks, blocks, blocks),
        check_vma=False,
    )
```
